256 devices in a mesh: inst: 32 (over y, z), tp: 8 (over x, core).
Axes of the slice: x: 4, y: 4, z: 8, core: 2. Of those that a mesh axis runs over, the one named last changes fastest.
Arguments:
- queries: bfloat16 [256, 3, 8192], P('inst', None, 'tp')
- new_kv: bfloat16 [256, 2, 3, 1024], P('inst', None, None, 'tp')
- key_value_pool: bfloat16 [3840, 2, 64, 1024], P('inst', None, None, 'tp'), may hold values from -5 to 5
- ctx_len: int32 [256], P('inst'), may hold values from 257 to 960, as said below
- entry_lender: int32 [256, 5], P('inst'), may hold values from 0 to 31, as said below
- entry_blocks: int32 [256, 5], P('inst'), may hold values from 1 to 3
- entry_slot: int32 [256, 5], P('inst'), may hold values from 0 to 117, as said below
- out_weight: bfloat16 [8192, 4096], P('tp'), may hold values from -0.0625 to 0.0625
Outputs:
- attention: bfloat16 [256, 3, 8192], P('inst', None, 'tp')
- projected: bfloat16 [256, 3, 4096], P('inst', None, 'tp')
The draws below stay inside these ranges and needn't reach their ends.
Inputs may be any that keep to these rules, and one draw needn't show every extreme that they name: `ctx_len`: A request holds ((blocks of all its entries) - 1) * 64 + 1 to (blocks of all its entries) * 64 cached tokens. `entry_lender`: entry 0 is the request's home instance, the index of inst that holds its row; the other entries name other instances. The requests of one home name one other instance in at most 2 entries, and each instance is named by exactly 8 * (4) entries of other homes' requests. entry_slot + 3 <= 120; the blocks entry_slot to entry_slot + 2 of different entries on one instance never meet.
All inputs are finite; a program needn't handle non-finite values.
Results may differ from the reference program's by a relative error of at most 0.02.
Values may be sent and summed in bfloat16 or wider, within the bound.
No kernel may reach another device: no remote copies, remote signals or barrier semaphores. Data moves between devices by JAX's collectives and lax.ppermute only.
A program may use at most 128 MiB of HBM per device.

```python
import math
import jax
import jax.numpy as jnp
from jax import lax

QUERY_HEADS = 64
KEY_VALUE_HEADS = 8
HEAD_SIZE = 128
DWIN = 4096
DECODE_STEPS = 3
BLOCK_TOKENS = 64
MOST_BLOCKS = 3
LEND = 5
REQ_DEV = 8
REQUEST_TOTAL = 256
POOL = 120
POOL_BLOCKS = 3840
N_INST = 32


def block_plan(key):
    instances = N_INST
    lent_items = REQ_DEV * (LEND - 1)
    random_keys = jax.random.split(key, 6)
    placing = jax.random.permutation(random_keys[0], instances).astype(jnp.int32)
    inverse = jnp.argsort(placing).astype(jnp.int32)
    turning = jax.random.randint(random_keys[1], (), 0, instances - 1)
    homes = jnp.arange(instances, dtype=jnp.int32)[:, None]
    item_index = jnp.arange(lent_items, dtype=jnp.int32)[None, :]
    offsets = 1 + (item_index // 2 + turning) % (instances - 1)
    lender_item = inverse[(placing[homes] + offsets) % instances]
    groups = jax.vmap(lambda sub: jax.random.permutation(sub, REQ_DEV * LEND))(jax.random.split(random_keys[2], instances)).astype(jnp.int32)
    slot_item = groups[lender_item, REQ_DEV + item_index] * MOST_BLOCKS
    shuffled = jax.vmap(lambda sub: jax.random.permutation(sub, lent_items))(jax.random.split(random_keys[3], instances)).astype(jnp.int32)
    lender_far = jnp.take_along_axis(lender_item, shuffled, axis=1).reshape(instances, REQ_DEV, LEND - 1)
    slot_far = jnp.take_along_axis(slot_item, shuffled, axis=1).reshape(instances, REQ_DEV, LEND - 1)
    lenders = jnp.concatenate([jnp.broadcast_to(homes[:, :, None], (instances, REQ_DEV, 1)), lender_far], axis=2)
    slots = jnp.concatenate([(groups[:, :REQ_DEV] * MOST_BLOCKS)[:, :, None], slot_far], axis=2)
    blocks = jax.random.randint(random_keys[4], (instances, REQ_DEV, LEND), 1, MOST_BLOCKS + 1)
    blocks = blocks.at[:, 0, :].set(MOST_BLOCKS)
    blocks = blocks.at[1, 0, :].set(1)
    overall = jnp.sum(blocks, axis=2)
    length = BLOCK_TOKENS * (overall - 1) + jax.random.randint(random_keys[5], (instances, REQ_DEV), 1, BLOCK_TOKENS + 1)
    length = length.at[:, 0].set(BLOCK_TOKENS * overall[:, 0])
    length = length.at[1, 0].set(BLOCK_TOKENS * (LEND - 1) + 1)
    return (lenders.reshape(-1, LEND).astype(jnp.int32), blocks.reshape(-1, LEND).astype(jnp.int32), slots.reshape(-1, LEND).astype(jnp.int32), length.reshape(-1).astype(jnp.int32))


def fresh_keys(key):
    random_keys = jax.random.split(key, 3)
    base_random = jax.random.truncated_normal(random_keys[0], -4.0, 4.0, (REQUEST_TOTAL, DECODE_STEPS, KEY_VALUE_HEADS * HEAD_SIZE), jnp.float32)
    picked = jax.random.uniform(random_keys[2], (REQUEST_TOTAL,)) < 0.15
    moved = base_random[:, 1]
    second = jnp.where(picked[:, None], moved, base_random[:, 1])
    return base_random.at[:, 1].set(second)


def draw_ctx_len(key, part):
    return block_plan(key)[3]


def draw_entry_lender(key, part):
    return block_plan(key)[0]


def draw_entry_blocks(key, part):
    return block_plan(key)[1]


def draw_entry_slot(key, part):
    return block_plan(key)[2]


def draw_new_kv(key, part):
    local_keys = fresh_keys(key)
    key = jax.random.fold_in(key, 11)
    cached_values = jax.random.truncated_normal(key, -4.0, 4.0, (REQUEST_TOTAL, DECODE_STEPS, KEY_VALUE_HEADS * HEAD_SIZE), jnp.float32)
    return jnp.stack([local_keys, cached_values], axis=1).astype(jnp.bfloat16)


def draw_queries(key, part):
    local_keys = fresh_keys(key)
    key = jax.random.fold_in(key, 12)
    random_keys = jax.random.split(key, 3)
    expanded_heads = jnp.repeat(local_keys.reshape(REQUEST_TOTAL, DECODE_STEPS, KEY_VALUE_HEADS, 1, HEAD_SIZE), QUERY_HEADS // KEY_VALUE_HEADS, axis=3).reshape(REQUEST_TOTAL, DECODE_STEPS, QUERY_HEADS * HEAD_SIZE)
    result = 0.5 * expanded_heads + 0.9 * jax.random.truncated_normal(random_keys[2], -4.0, 4.0, expanded_heads.shape, jnp.float32)
    return result.astype(jnp.bfloat16)


def shard_levels(stream_key, extent, shards, least, largest):
    def one(position, parts):
        steps = jax.random.uniform(jax.random.fold_in(jax.random.fold_in(stream_key, 6), position), (parts,), jnp.float32, least / len(shards), largest / len(shards))
        return jnp.repeat(jnp.exp(steps), extent[position] // parts).reshape((-1,) + (1,) * (len(extent) - position - 1))

    gain = one(*shards[0])
    for cut in shards[1:]:
        gain = gain * one(*cut)
    return gain


def centred(stream_key, dims, scale, bound, pieces=(), held_as=jnp.bfloat16):
    values = scale * jax.random.normal(stream_key, dims, jnp.float32)
    if pieces:
        values = values * shard_levels(stream_key, dims, pieces, -0.22, 0.18)
    return jnp.clip(values, -bound, bound).astype(held_as)


def setup_inputs(seed: int = 0) -> dict:
    keys = jax.random.split(jax.random.key(seed), 9)
    return {
        "queries": draw_queries(jax.random.fold_in(keys[8], 71), 0),
        "new_kv": draw_new_kv(jax.random.fold_in(keys[8], 71), 0),
        "key_value_pool": centred(keys[2], (POOL_BLOCKS, 2, BLOCK_TOKENS, KEY_VALUE_HEADS * HEAD_SIZE), 1.0, 5.0, ((0, 32), (3, 8))),
        "ctx_len": draw_ctx_len(jax.random.fold_in(keys[8], 71), 0),
        "entry_lender": draw_entry_lender(jax.random.fold_in(keys[8], 71), 0),
        "entry_blocks": draw_entry_blocks(jax.random.fold_in(keys[8], 71), 0),
        "entry_slot": draw_entry_slot(jax.random.fold_in(keys[8], 71), 0),
        "out_weight": centred(keys[7], (QUERY_HEADS * HEAD_SIZE, DWIN), (QUERY_HEADS * HEAD_SIZE) ** -0.5, 0.0625, ((0, 8),)),
    }


def segment_attend(rows_of_queries, rows_of_keys, rows_of_values, visible):
    count_of_tokens = rows_of_keys.shape[0]
    head_groups = QUERY_HEADS // KEY_VALUE_HEADS
    heads_of_queries = rows_of_queries.astype(jnp.float32).reshape(DECODE_STEPS, KEY_VALUE_HEADS, head_groups, HEAD_SIZE)
    heads_of_keys = rows_of_keys.astype(jnp.float32).reshape(count_of_tokens, KEY_VALUE_HEADS, HEAD_SIZE)
    heads_of_values = rows_of_values.astype(jnp.float32).reshape(count_of_tokens, KEY_VALUE_HEADS, HEAD_SIZE)
    scores = jnp.einsum('sagd,tad->sagt', heads_of_queries, heads_of_keys, precision=lax.Precision.HIGHEST) * (1.0 / math.sqrt(HEAD_SIZE))
    scores = jnp.where(visible[:, None, None, :], scores, -1e+30)
    highest = lax.optimization_barrier(jnp.max(scores, axis=-1, keepdims=True))
    expits = jnp.exp(scores - highest)
    totals = lax.optimization_barrier(jnp.sum(expits, axis=-1, keepdims=True))
    logsum = (highest + jnp.log(totals))[..., 0].reshape(DECODE_STEPS, QUERY_HEADS)
    rounded = lax.optimization_barrier(expits.astype(jnp.bfloat16)).astype(jnp.float32)
    partial_out = jnp.einsum('sagt,tad->sagd', rounded, heads_of_values, precision=lax.Precision.HIGHEST) / totals
    return (partial_out.reshape(DECODE_STEPS, QUERY_HEADS * HEAD_SIZE).astype(jnp.bfloat16), logsum)

def request_attention(packed, key_value_pool):
    rows_of_queries, fresh, length, lenders, blocks, slots = packed
    positions = jnp.arange(MOST_BLOCKS * BLOCK_TOKENS, dtype=jnp.int32)
    earlier = jnp.cumsum(blocks) - blocks
    causal = jnp.arange(DECODE_STEPS)[None, :] <= jnp.arange(DECODE_STEPS)[:, None]
    partials = []
    logsums = []
    for entry_index in range(LEND):
        block_ids = (lenders[entry_index] * POOL + slots[entry_index] + jnp.arange(MOST_BLOCKS, dtype=jnp.int32)).astype(jnp.int32)
        selected_entries = key_value_pool[block_ids]
        rows_of_keys = selected_entries[:, 0].reshape(MOST_BLOCKS * BLOCK_TOKENS, KEY_VALUE_HEADS * HEAD_SIZE)
        rows_of_values = selected_entries[:, 1].reshape(MOST_BLOCKS * BLOCK_TOKENS, KEY_VALUE_HEADS * HEAD_SIZE)
        live_count = jnp.clip(length - BLOCK_TOKENS * earlier[entry_index], 0, BLOCK_TOKENS * blocks[entry_index])
        visible = jnp.broadcast_to(positions[None, :] < live_count, (DECODE_STEPS, MOST_BLOCKS * BLOCK_TOKENS))
        if entry_index == 0:
            rows_of_keys = jnp.concatenate([rows_of_keys, fresh[0]], axis=0)
            rows_of_values = jnp.concatenate([rows_of_values, fresh[1]], axis=0)
            visible = jnp.concatenate([visible, causal], axis=1)
        partial_out, logsum = segment_attend(rows_of_queries, rows_of_keys, rows_of_values, visible)
        partials.append(partial_out)
        logsums.append(logsum)
    logsums = jnp.stack(logsums)
    partials = jnp.stack(partials).astype(jnp.float32).reshape(LEND, DECODE_STEPS, QUERY_HEADS, HEAD_SIZE)
    highest = lax.optimization_barrier(jnp.max(logsums, axis=0, keepdims=True))
    weights = jnp.exp(logsums - highest)
    merged = lax.optimization_barrier(jnp.sum(weights[..., None] * partials, axis=0)) / lax.optimization_barrier(jnp.sum(weights, axis=0))[..., None]
    return merged.reshape(DECODE_STEPS, QUERY_HEADS * HEAD_SIZE).astype(jnp.bfloat16)

def reference(queries, new_kv, key_value_pool, ctx_len, entry_lender, entry_blocks, entry_slot, out_weight):
    attention = lax.map(lambda packed: request_attention(packed, key_value_pool), (queries, new_kv, ctx_len, entry_lender, entry_blocks, entry_slot))
    flat = attention.reshape(REQUEST_TOTAL * DECODE_STEPS, QUERY_HEADS * HEAD_SIZE)
    projected = jnp.dot(flat, out_weight, preferred_element_type=jnp.float32).astype(jnp.bfloat16)
    return (attention, projected.reshape(REQUEST_TOTAL, DECODE_STEPS, DWIN))
```

```python
import functools
import math

import jax
import jax.numpy as jnp
from jax import lax
from jax.experimental import pallas as pl
from jax.experimental.pallas import tpu as pltpu
from jax.sharding import PartitionSpec as P

HEAD_SIZE = 128
MOST_BLOCKS = 3
STEPS = 3
HEADS = 8
REQUESTS = 8
ENTRIES = 5
INSTANCES = 32
SLOTS = 2
BLOCK_TOKENS = 64
SPAN = MOST_BLOCKS * BLOCK_TOKENS
ROWS = STEPS * HEADS
LENT = REQUESTS * (ENTRIES - 1)
TP = 8
GROUP = 8
META = SLOTS * STEPS
SCALE = 1.0 / math.sqrt(HEAD_SIZE)
F32 = jnp.float32
BF16 = jnp.bfloat16
VMEM_SPEC = pl.BlockSpec(memory_space=pltpu.VMEM)
SMEM_SPEC = pl.BlockSpec(memory_space=pltpu.SMEM)


def lanes_of(shape):
    return lax.broadcasted_iota(jnp.int32, shape, len(shape) - 1)


def clear_counts(count_ref):
    for index in range(INSTANCES):
        count_ref[index] = 0


def next_rank(count_ref, lender):
    rank = count_ref[lender]
    count_ref[lender] = rank + 1
    return rank


def live_of(ctx_ref, blocks_ref, request, entry, earlier):
    blocks = blocks_ref[request, entry]
    live = jnp.clip(ctx_ref[request] - BLOCK_TOKENS * earlier, 0, BLOCK_TOKENS * blocks)
    return live, earlier + blocks


def pack_kernel(ctx_ref, lender_ref, blocks_ref, slot_ref, q_ref, send_ref, rows_ref, regroup, count_ref):
    for step in range(STEPS):
        for head in range(HEADS):
            tile = q_ref[step, :, head * HEAD_SIZE : (head + 1) * HEAD_SIZE].astype(F32)
            regroup[pl.ds(step * HEADS + head, REQUESTS, stride=ROWS), :] = tile
    send_ref[:, META, :, :] = jnp.zeros((INSTANCES, 8, HEAD_SIZE), BF16)
    clear_counts(count_ref)
    lane = lanes_of((8, HEAD_SIZE))
    first_row = lax.broadcasted_iota(jnp.int32, (8, HEAD_SIZE), 0) == 0
    for request in range(REQUESTS):
        rows = regroup[request * ROWS : (request + 1) * ROWS, :].astype(BF16)
        rows_ref[request] = rows
        tiles = regroup[request * ROWS : (request + 1) * ROWS, :].reshape(STEPS, HEADS, HEAD_SIZE).astype(BF16)
        earlier = blocks_ref[request, 0]
        for entry in range(1, ENTRIES):
            lender = lender_ref[request, entry]
            rank = next_rank(count_ref, lender)
            live, earlier = live_of(ctx_ref, blocks_ref, request, entry, earlier)
            send_ref[lender, pl.ds(rank * STEPS, STEPS), :, :] = tiles
            meta = send_ref[lender, META].astype(F32)
            meta = jnp.where(first_row & (lane == 2 * rank), slot_ref[request, entry].astype(F32), meta)
            meta = jnp.where(first_row & (lane == 2 * rank + 1), live.astype(F32), meta)
            send_ref[lender, META] = meta.astype(BF16)


def scores_of(query, keys):
    return lax.dot_general(query, keys, (((1,), (1,)), ((), ())), preferred_element_type=F32) * SCALE


def home_kernel(
    ctx_ref, blocks_ref, slot_ref, rows_ref, fresh_ref, pool_ref, part_ref, logsum_ref
):
    token = lanes_of((ROWS, SPAN))
    fresh_token = lanes_of((ROWS, STEPS))
    step_of_row = lax.broadcasted_iota(jnp.int32, (ROWS, STEPS), 0) // HEADS
    fresh_seen = fresh_token <= step_of_row
    cached, fresh, values, fresh_values = [], [], [], []
    for request in range(REQUESTS):
        live, _ = live_of(ctx_ref, blocks_ref, request, 0, 0)
        slot = slot_ref[request, 0]
        query = rows_ref[request]
        keys = pool_ref[pl.ds(slot, MOST_BLOCKS), 0].reshape(SPAN, HEAD_SIZE)
        values.append(pool_ref[pl.ds(slot, MOST_BLOCKS), 1].reshape(SPAN, HEAD_SIZE))
        fresh_values.append(fresh_ref[request, 1].astype(F32))
        cached.append(jnp.where(token < live, scores_of(query, keys), -1e30))
        fresh.append(jnp.where(fresh_seen, scores_of(query, fresh_ref[request, 0]), -1e30))
    for request in range(REQUESTS):
        top = jnp.maximum(
            jnp.max(cached[request], axis=1, keepdims=True), jnp.max(fresh[request], axis=1, keepdims=True)
        )
        cached_expits = jnp.exp(cached[request] - top)
        fresh_expits = jnp.exp(fresh[request] - top)
        totals = jnp.sum(cached_expits, axis=1, keepdims=True) + jnp.sum(fresh_expits, axis=1, keepdims=True)
        out = jnp.dot(cached_expits.astype(BF16), values[request], preferred_element_type=F32)
        rounded = fresh_expits.astype(BF16).astype(F32)
        for index in range(STEPS):
            out = out + rounded[:, index : index + 1] * fresh_values[request][index : index + 1, :]
        part_ref[request] = (out / totals).astype(BF16)
        logsum_ref[request] = jnp.broadcast_to(top + jnp.log(totals), (ROWS, HEAD_SIZE))


def lent_kernel(got_ref, pool_ref, back_ref, meta_vector, meta_ref, item_ref, sem):
    meta_vector[...] = jnp.sum(got_ref[:, META].astype(F32), axis=1).astype(jnp.int32)
    copy = pltpu.make_async_copy(meta_vector, meta_ref, sem)
    copy.start()
    back_ref[:, META, :, :] = jnp.zeros((INSTANCES, 8, HEAD_SIZE), BF16)
    copy.wait()

    def compact(index, found):
        live = meta_ref[index // SLOTS, 2 * (index % SLOTS) + 1]
        item_ref[found] = index
        return found + (live > 0).astype(jnp.int32)

    lax.fori_loop(0, INSTANCES * SLOTS, compact, 0, unroll=8)
    token = lanes_of((ROWS, SPAN))
    lane = lanes_of((8, HEAD_SIZE))

    @pl.loop(0, LENT // GROUP)
    def _(group):
        items = [item_ref[group * GROUP + member] for member in range(GROUP)]
        source = [item // SLOTS for item in items]
        rank = [item % SLOTS for item in items]
        scores, values = [], []
        for member in range(GROUP):
            slot = meta_ref[source[member], 2 * rank[member]]
            live = meta_ref[source[member], 2 * rank[member] + 1]
            query = got_ref[source[member], pl.ds(rank[member] * STEPS, STEPS)]
            query = query.astype(F32).reshape(ROWS, HEAD_SIZE).astype(BF16)
            keys = pool_ref[pl.ds(slot, MOST_BLOCKS), 0].reshape(SPAN, HEAD_SIZE)
            values.append(pool_ref[pl.ds(slot, MOST_BLOCKS), 1].reshape(SPAN, HEAD_SIZE))
            scores.append(jnp.where(token < live, scores_of(query, keys), -1e30))
        parts, logsums = [], []
        for member in range(GROUP):
            top = jnp.max(scores[member], axis=1, keepdims=True)
            expits = jnp.exp(scores[member] - top)
            totals = jnp.sum(expits, axis=1, keepdims=True)
            out = jnp.dot(expits.astype(BF16), values[member], preferred_element_type=F32)
            parts.append(out / totals)
            logsums.append(jnp.broadcast_to(top + jnp.log(totals), (ROWS, HEAD_SIZE)))
        for member in range(GROUP):
            back_ref[source[member], pl.ds(rank[member] * STEPS, STEPS)] = (
                parts[member].reshape(STEPS, HEADS, HEAD_SIZE).astype(BF16)
            )
            high = logsums[member].astype(BF16).astype(F32)
            middle = (logsums[member] - high).astype(BF16).astype(F32)
            low = logsums[member] - high - middle
            at = lane - 9 * rank[member]
            block = back_ref[source[member], META].astype(F32)
            for step in range(STEPS):
                for place, piece in enumerate((high, middle, low)):
                    block = jnp.where(at == 3 * step + place, piece[step * HEADS : (step + 1) * HEADS], block)
            back_ref[source[member], META] = block.astype(BF16)


def merge_kernel(
    lender_ref, back_ref, part_ref, logsum_ref, weight_ref, attention_ref, terms_ref, merged, count_ref
):
    clear_counts(count_ref)
    lane = lanes_of((8, HEAD_SIZE))
    for request in range(REQUESTS):
        logsums = [logsum_ref[request]]
        parts = [part_ref[request].astype(F32)]
        for entry in range(1, ENTRIES):
            lender = lender_ref[request, entry]
            rank = next_rank(count_ref, lender)
            parts.append(
                back_ref[lender, pl.ds(rank * STEPS, STEPS)].astype(F32).reshape(ROWS, HEAD_SIZE)
            )
            block = back_ref[lender, META].astype(F32)
            at = lane - 9 * rank
            columns = []
            for step in range(STEPS):
                mine = (at >= 3 * step) & (at < 3 * step + 3)
                columns.append(
                    jnp.broadcast_to(
                        jnp.sum(jnp.where(mine, block, 0.0), axis=1, keepdims=True), (HEADS, HEAD_SIZE)
                    )
                )
            logsums.append(jnp.concatenate(columns, axis=0))
        highest = functools.reduce(jnp.maximum, logsums)
        weights = [jnp.exp(logsum - highest) for logsum in logsums]
        total = functools.reduce(jnp.add, weights)
        blended = functools.reduce(jnp.add, [weight * part for weight, part in zip(weights, parts)])
        merged[request * ROWS : (request + 1) * ROWS, :] = blended / total
    for step in range(STEPS):
        for head in range(HEADS):
            tile = merged[pl.ds(step * HEADS + head, REQUESTS, stride=ROWS), :]
            attention_ref[step, :, head * HEAD_SIZE : (head + 1) * HEAD_SIZE] = tile.astype(BF16)
    attention = attention_ref[...].astype(F32).reshape(ROWS, HEADS * HEAD_SIZE).astype(BF16)

    @pl.loop(0, TP)
    def _(part):
        columns = pl.ds(pl.multiple_of(part * 512, 512), 512)
        terms = jnp.dot(attention, weight_ref[:, columns], preferred_element_type=F32)
        terms_ref[part] = terms.astype(BF16)


def local(
    queries, new_kv, key_value_pool, ctx_len, entry_lender, entry_blocks, entry_slot, out_weight
):
    message = jax.ShapeDtypeStruct((INSTANCES, META + 1, 8, HEAD_SIZE), BF16)
    rows = jax.ShapeDtypeStruct((REQUESTS, ROWS, HEAD_SIZE), BF16)
    send, query_rows = pl.pallas_call(
        pack_kernel,
        out_shape=(message, rows),
        in_specs=[SMEM_SPEC] * 4 + [VMEM_SPEC],
        out_specs=(VMEM_SPEC, VMEM_SPEC),
        scratch_shapes=[pltpu.VMEM((REQUESTS * ROWS, HEAD_SIZE), F32), pltpu.SMEM((INSTANCES,), jnp.int32)],
        name="pack",
    )(ctx_len, entry_lender, entry_blocks, entry_slot, queries.transpose(1, 0, 2))
    got = lax.all_to_all(send, "inst", split_axis=0, concat_axis=0, tiled=True)
    home_part, home_logsum = pl.pallas_call(
        home_kernel,
        out_shape=(rows, jax.ShapeDtypeStruct((REQUESTS, ROWS, HEAD_SIZE), F32)),
        in_specs=[SMEM_SPEC] * 3 + [VMEM_SPEC] * 3,
        out_specs=(VMEM_SPEC, VMEM_SPEC),
        cost_estimate=pl.CostEstimate(flops=10**8, bytes_accessed=4 * 10**6, transcendentals=0),
        name="home",
    )(ctx_len, entry_blocks, entry_slot, query_rows, new_kv, key_value_pool)
    back = pl.pallas_call(
        lent_kernel,
        out_shape=message,
        in_specs=[VMEM_SPEC] * 2,
        out_specs=VMEM_SPEC,
        scratch_shapes=[
            pltpu.VMEM((INSTANCES, HEAD_SIZE), jnp.int32),
            pltpu.SMEM((INSTANCES, HEAD_SIZE), jnp.int32),
            pltpu.SMEM((INSTANCES * SLOTS + 1,), jnp.int32),
            pltpu.SemaphoreType.DMA(()),
        ],
        name="lent",
    )(got, key_value_pool)
    back = lax.all_to_all(back, "inst", split_axis=0, concat_axis=0, tiled=True)
    attention, terms = pl.pallas_call(
        merge_kernel,
        out_shape=(
            jax.ShapeDtypeStruct((STEPS, REQUESTS, HEADS * HEAD_SIZE), BF16),
            jax.ShapeDtypeStruct((TP, ROWS, 512), BF16),
        ),
        in_specs=[SMEM_SPEC] + [VMEM_SPEC] * 4,
        out_specs=(VMEM_SPEC, VMEM_SPEC),
        scratch_shapes=[pltpu.VMEM((REQUESTS * ROWS, HEAD_SIZE), F32), pltpu.SMEM((INSTANCES,), jnp.int32)],
        compiler_params=pltpu.CompilerParams(vmem_limit_bytes=24 * 2**20),
        name="merge",
    )(entry_lender, back, home_part, home_logsum, out_weight)
    terms = lax.all_to_all(terms, "tp", split_axis=0, concat_axis=0, tiled=True)
    projected = jnp.sum(terms.astype(F32), axis=0).astype(BF16)
    return (attention.transpose(1, 0, 2), projected.reshape(STEPS, REQUESTS, -1).transpose(1, 0, 2))


def solution(mesh):
    return jax.shard_map(
        local,
        mesh=mesh,
        in_specs=(
            P("inst", None, "tp"),
            P("inst", None, None, "tp"),
            P("inst", None, None, "tp"),
            P("inst"),
            P("inst", None),
            P("inst", None),
            P("inst", None),
            P("tp", None),
        ),
        out_specs=(P("inst", None, "tp"), P("inst", None, "tp")),
        check_vma=False,
    )
```

```python
import functools
import math

import jax
import jax.numpy as jnp
from jax import lax
from jax.experimental import pallas as pl
from jax.experimental.pallas import tpu as pltpu
from jax.sharding import PartitionSpec as P

HEAD_SIZE = 128
MOST_BLOCKS = 3
STEPS = 3
HEADS = 8
REQUESTS = 8
ENTRIES = 5
INSTANCES = 32
SLOTS = 2
BLOCK_TOKENS = 64
SPAN = MOST_BLOCKS * BLOCK_TOKENS
ROWS = STEPS * HEADS
LENT = REQUESTS * (ENTRIES - 1)
TP = 8
CORES = 2
CHIPS = TP // CORES
WIDTH = 512
GROUP = 8
META = SLOTS * STEPS
SCALE = 1.0 / math.sqrt(HEAD_SIZE)
F32 = jnp.float32
BF16 = jnp.bfloat16
VMEM_SPEC = pl.BlockSpec(memory_space=pltpu.VMEM)
SMEM_SPEC = pl.BlockSpec(memory_space=pltpu.SMEM)


def lanes_of(shape):
    return lax.broadcasted_iota(jnp.int32, shape, len(shape) - 1)


def clear_counts(count_ref):
    for index in range(INSTANCES):
        count_ref[index] = 0


def next_rank(count_ref, lender):
    rank = count_ref[lender]
    count_ref[lender] = rank + 1
    return rank


def live_of(ctx_ref, blocks_ref, request, entry, earlier):
    blocks = blocks_ref[request, entry]
    live = jnp.clip(ctx_ref[request] - BLOCK_TOKENS * earlier, 0, BLOCK_TOKENS * blocks)
    return live, earlier + blocks


def pack_kernel(ctx_ref, lender_ref, blocks_ref, slot_ref, q_ref, send_ref, rows_ref, regroup, count_ref):
    for step in range(STEPS):
        for head in range(HEADS):
            tile = q_ref[step, :, head * HEAD_SIZE : (head + 1) * HEAD_SIZE].astype(F32)
            regroup[pl.ds(step * HEADS + head, REQUESTS, stride=ROWS), :] = tile
    send_ref[:, META, :, :] = jnp.zeros((INSTANCES, 8, HEAD_SIZE), BF16)
    clear_counts(count_ref)
    lane = lanes_of((8, HEAD_SIZE))
    first_row = lax.broadcasted_iota(jnp.int32, (8, HEAD_SIZE), 0) == 0
    for request in range(REQUESTS):
        rows = regroup[request * ROWS : (request + 1) * ROWS, :].astype(BF16)
        rows_ref[request] = rows
        tiles = regroup[request * ROWS : (request + 1) * ROWS, :].reshape(STEPS, HEADS, HEAD_SIZE).astype(BF16)
        earlier = blocks_ref[request, 0]
        for entry in range(1, ENTRIES):
            lender = lender_ref[request, entry]
            rank = next_rank(count_ref, lender)
            live, earlier = live_of(ctx_ref, blocks_ref, request, entry, earlier)
            send_ref[lender, pl.ds(rank * STEPS, STEPS), :, :] = tiles
            meta = send_ref[lender, META].astype(F32)
            meta = jnp.where(first_row & (lane == 2 * rank), slot_ref[request, entry].astype(F32), meta)
            meta = jnp.where(first_row & (lane == 2 * rank + 1), live.astype(F32), meta)
            send_ref[lender, META] = meta.astype(BF16)


def scores_of(query, keys):
    return lax.dot_general(query, keys, (((1,), (1,)), ((), ())), preferred_element_type=F32) * SCALE


def home_kernel(
    ctx_ref, blocks_ref, slot_ref, rows_ref, fresh_ref, pool_ref, part_ref, logsum_ref
):
    token = lanes_of((ROWS, SPAN))
    fresh_token = lanes_of((ROWS, STEPS))
    step_of_row = lax.broadcasted_iota(jnp.int32, (ROWS, STEPS), 0) // HEADS
    fresh_seen = fresh_token <= step_of_row
    cached, fresh, values, fresh_values = [], [], [], []
    for request in range(REQUESTS):
        live, _ = live_of(ctx_ref, blocks_ref, request, 0, 0)
        slot = slot_ref[request, 0]
        query = rows_ref[request]
        keys = pool_ref[pl.ds(slot, MOST_BLOCKS), 0].reshape(SPAN, HEAD_SIZE)
        values.append(pool_ref[pl.ds(slot, MOST_BLOCKS), 1].reshape(SPAN, HEAD_SIZE))
        fresh_values.append(fresh_ref[request, 1].astype(F32))
        cached.append(jnp.where(token < live, scores_of(query, keys), -1e30))
        fresh.append(jnp.where(fresh_seen, scores_of(query, fresh_ref[request, 0]), -1e30))
    for request in range(REQUESTS):
        top = jnp.maximum(
            jnp.max(cached[request], axis=1, keepdims=True), jnp.max(fresh[request], axis=1, keepdims=True)
        )
        cached_expits = jnp.exp(cached[request] - top)
        fresh_expits = jnp.exp(fresh[request] - top)
        totals = jnp.sum(cached_expits, axis=1, keepdims=True) + jnp.sum(fresh_expits, axis=1, keepdims=True)
        out = jnp.dot(cached_expits.astype(BF16), values[request], preferred_element_type=F32)
        rounded = fresh_expits.astype(BF16).astype(F32)
        for index in range(STEPS):
            out = out + rounded[:, index : index + 1] * fresh_values[request][index : index + 1, :]
        part_ref[request] = (out / totals).astype(BF16)
        logsum_ref[request] = jnp.broadcast_to(top + jnp.log(totals), (ROWS, HEAD_SIZE))


def lent_kernel(got_ref, pool_ref, back_ref, meta_vector, meta_ref, item_ref, sem):
    meta_vector[...] = jnp.sum(got_ref[:, META].astype(F32), axis=1).astype(jnp.int32)
    copy = pltpu.make_async_copy(meta_vector, meta_ref, sem)
    copy.start()
    back_ref[:, META, :, :] = jnp.zeros((INSTANCES, 8, HEAD_SIZE), BF16)
    copy.wait()

    def compact(index, found):
        live = meta_ref[index // SLOTS, 2 * (index % SLOTS) + 1]
        item_ref[found] = index
        return found + (live > 0).astype(jnp.int32)

    lax.fori_loop(0, INSTANCES * SLOTS, compact, 0, unroll=8)
    token = lanes_of((ROWS, SPAN))
    lane = lanes_of((8, HEAD_SIZE))

    @pl.loop(0, LENT // GROUP)
    def _(group):
        items = [item_ref[group * GROUP + member] for member in range(GROUP)]
        source = [item // SLOTS for item in items]
        rank = [item % SLOTS for item in items]
        scores, values = [], []
        for member in range(GROUP):
            slot = meta_ref[source[member], 2 * rank[member]]
            live = meta_ref[source[member], 2 * rank[member] + 1]
            query = got_ref[source[member], pl.ds(rank[member] * STEPS, STEPS)]
            query = query.astype(F32).reshape(ROWS, HEAD_SIZE).astype(BF16)
            keys = pool_ref[pl.ds(slot, MOST_BLOCKS), 0].reshape(SPAN, HEAD_SIZE)
            values.append(pool_ref[pl.ds(slot, MOST_BLOCKS), 1].reshape(SPAN, HEAD_SIZE))
            scores.append(jnp.where(token < live, scores_of(query, keys), -1e30))
        parts, logsums = [], []
        for member in range(GROUP):
            top = jnp.max(scores[member], axis=1, keepdims=True)
            expits = jnp.exp(scores[member] - top)
            totals = jnp.sum(expits, axis=1, keepdims=True)
            out = jnp.dot(expits.astype(BF16), values[member], preferred_element_type=F32)
            parts.append(out / totals)
            logsums.append(jnp.broadcast_to(top + jnp.log(totals), (ROWS, HEAD_SIZE)))
        for member in range(GROUP):
            back_ref[source[member], pl.ds(rank[member] * STEPS, STEPS)] = (
                parts[member].reshape(STEPS, HEADS, HEAD_SIZE).astype(BF16)
            )
            high = logsums[member].astype(BF16).astype(F32)
            middle = (logsums[member] - high).astype(BF16).astype(F32)
            low = logsums[member] - high - middle
            at = lane - 9 * rank[member]
            block = back_ref[source[member], META].astype(F32)
            for step in range(STEPS):
                for place, piece in enumerate((high, middle, low)):
                    block = jnp.where(at == 3 * step + place, piece[step * HEADS : (step + 1) * HEADS], block)
            back_ref[source[member], META] = block.astype(BF16)


def merge_kernel(
    lender_ref, back_ref, part_ref, logsum_ref, weight_ref, attention_ref, terms_ref, merged, count_ref
):
    clear_counts(count_ref)
    lane = lanes_of((8, HEAD_SIZE))
    for request in range(REQUESTS):
        logsums = [logsum_ref[request]]
        parts = [part_ref[request].astype(F32)]
        for entry in range(1, ENTRIES):
            lender = lender_ref[request, entry]
            rank = next_rank(count_ref, lender)
            parts.append(
                back_ref[lender, pl.ds(rank * STEPS, STEPS)].astype(F32).reshape(ROWS, HEAD_SIZE)
            )
            block = back_ref[lender, META].astype(F32)
            at = lane - 9 * rank
            columns = []
            for step in range(STEPS):
                mine = (at >= 3 * step) & (at < 3 * step + 3)
                columns.append(
                    jnp.broadcast_to(
                        jnp.sum(jnp.where(mine, block, 0.0), axis=1, keepdims=True), (HEADS, HEAD_SIZE)
                    )
                )
            logsums.append(jnp.concatenate(columns, axis=0))
        highest = functools.reduce(jnp.maximum, logsums)
        weights = [jnp.exp(logsum - highest) for logsum in logsums]
        total = functools.reduce(jnp.add, weights)
        blended = functools.reduce(jnp.add, [weight * part for weight, part in zip(weights, parts)])
        merged[request * ROWS : (request + 1) * ROWS, :] = blended / total
    for step in range(STEPS):
        for head in range(HEADS):
            tile = merged[pl.ds(step * HEADS + head, REQUESTS, stride=ROWS), :]
            attention_ref[step * REQUESTS : (step + 1) * REQUESTS, head * HEAD_SIZE : (head + 1) * HEAD_SIZE] = tile
    project(attention_ref, weight_ref, terms_ref, 1)


def project(attention_ref, weight_ref, terms_ref, other_core):
    attention = attention_ref[...].astype(BF16)
    place = lax.axis_index("tp")
    core = lax.rem(place + other_core, CORES)

    @pl.loop(0, CHIPS)
    def _(ahead):
        part = lax.rem(place // CORES + ahead, CHIPS) * CORES + core
        columns = pl.ds(pl.multiple_of(part * WIDTH, WIDTH), WIDTH)
        terms = jnp.dot(attention, weight_ref[:, columns], preferred_element_type=F32)
        terms_ref[ahead] = terms.astype(terms_ref.dtype)


def own_kernel(attention_ref, weight_ref, terms_ref, out_ref):
    out_ref[...] = attention_ref[...].reshape(STEPS, REQUESTS, HEADS * HEAD_SIZE).astype(BF16)
    project(attention_ref, weight_ref, terms_ref, 0)


def pair_kernel(mine_ref, other_ref, *sum_refs):
    for ahead, sum_ref in enumerate(sum_refs):
        sum_ref[...] = (mine_ref[ahead] + other_ref[ahead].astype(F32)).astype(sum_ref.dtype)


def total_kernel(own_ref, *refs):
    total = own_ref[...]
    for ref in refs[:-1]:
        total = total + ref[...].astype(F32)
    refs[-1][...] = total.astype(BF16)


def local(
    queries, new_kv, key_value_pool, ctx_len, entry_lender, entry_blocks, entry_slot, out_weight
):
    message = jax.ShapeDtypeStruct((INSTANCES, META + 1, 8, HEAD_SIZE), BF16)
    rows = jax.ShapeDtypeStruct((REQUESTS, ROWS, HEAD_SIZE), BF16)
    send, query_rows = pl.pallas_call(
        pack_kernel,
        out_shape=(message, rows),
        in_specs=[SMEM_SPEC] * 4 + [VMEM_SPEC],
        out_specs=(VMEM_SPEC, VMEM_SPEC),
        scratch_shapes=[pltpu.VMEM((REQUESTS * ROWS, HEAD_SIZE), F32), pltpu.SMEM((INSTANCES,), jnp.int32)],
        compiler_params=pltpu.CompilerParams(vmem_limit_bytes=4 * 2**20),
        name="pack",
    )(ctx_len, entry_lender, entry_blocks, entry_slot, queries.transpose(1, 0, 2))
    got = lax.all_to_all(send, "inst", split_axis=0, concat_axis=0, tiled=True)
    home_part, home_logsum = pl.pallas_call(
        home_kernel,
        out_shape=(rows, jax.ShapeDtypeStruct((REQUESTS, ROWS, HEAD_SIZE), F32)),
        in_specs=[SMEM_SPEC] * 3 + [VMEM_SPEC] * 3,
        out_specs=(VMEM_SPEC, VMEM_SPEC),
        cost_estimate=pl.CostEstimate(flops=10**8, bytes_accessed=4 * 10**6, transcendentals=0),
        compiler_params=pltpu.CompilerParams(vmem_limit_bytes=12 * 2**20),
        name="home",
    )(ctx_len, entry_blocks, entry_slot, query_rows, new_kv, key_value_pool)
    back = pl.pallas_call(
        lent_kernel,
        out_shape=message,
        in_specs=[VMEM_SPEC] * 2,
        out_specs=VMEM_SPEC,
        scratch_shapes=[
            pltpu.VMEM((INSTANCES, HEAD_SIZE), jnp.int32),
            pltpu.SMEM((INSTANCES, HEAD_SIZE), jnp.int32),
            pltpu.SMEM((INSTANCES * SLOTS + 1,), jnp.int32),
            pltpu.SemaphoreType.DMA(()),
        ],
        compiler_params=pltpu.CompilerParams(vmem_limit_bytes=12 * 2**20),
        name="lent",
    )(got, key_value_pool)
    back = lax.all_to_all(back, "inst", split_axis=0, concat_axis=0, tiled=True)
    merged, terms = pl.pallas_call(
        merge_kernel,
        out_shape=(
            jax.ShapeDtypeStruct((ROWS, HEADS * HEAD_SIZE), F32),
            jax.ShapeDtypeStruct((CHIPS, ROWS, WIDTH), BF16),
        ),
        in_specs=[SMEM_SPEC] + [VMEM_SPEC] * 4,
        out_specs=(VMEM_SPEC, VMEM_SPEC),
        scratch_shapes=[pltpu.VMEM((REQUESTS * ROWS, HEAD_SIZE), F32), pltpu.SMEM((INSTANCES,), jnp.int32)],
        compiler_params=pltpu.CompilerParams(vmem_limit_bytes=16 * 2**20),
        name="merge",
    )(entry_lender, back, home_part, home_logsum, out_weight)
    swap = [(place, place ^ 1) for place in range(TP)]
    other = lax.ppermute(terms, "tp", swap)
    mine, attention = pl.pallas_call(
        own_kernel,
        out_shape=(
            jax.ShapeDtypeStruct((CHIPS, ROWS, WIDTH), F32),
            jax.ShapeDtypeStruct((STEPS, REQUESTS, HEADS * HEAD_SIZE), BF16),
        ),
        in_specs=[VMEM_SPEC] * 2,
        out_specs=(VMEM_SPEC, VMEM_SPEC),
        compiler_params=pltpu.CompilerParams(vmem_limit_bytes=16 * 2**20),
        cost_estimate=pl.CostEstimate(flops=10**8, bytes_accessed=4 * 10**6, transcendentals=0),
        name="own",
    )(merged, out_weight)
    sums = pl.pallas_call(
        pair_kernel,
        out_shape=[jax.ShapeDtypeStruct((ROWS, WIDTH), F32)] + [jax.ShapeDtypeStruct((ROWS, WIDTH), BF16)] * 3,
        in_specs=[VMEM_SPEC] * 2,
        out_specs=[VMEM_SPEC] * CHIPS,
        compiler_params=pltpu.CompilerParams(vmem_limit_bytes=4 * 2**20),
        name="pair",
    )(mine, other)
    arrived = []
    for ahead in (2, 1, 3):
        shift = [(place, (place + CORES * ahead) % TP) for place in range(TP)]
        arrived.append(lax.ppermute(sums[ahead], "tp", shift))
    projected = pl.pallas_call(
        total_kernel,
        out_shape=jax.ShapeDtypeStruct((ROWS, WIDTH), BF16),
        in_specs=[VMEM_SPEC] * CHIPS,
        out_specs=VMEM_SPEC,
        compiler_params=pltpu.CompilerParams(vmem_limit_bytes=4 * 2**20),
        name="total",
    )(sums[0], *arrived)
    return (attention.transpose(1, 0, 2), projected.reshape(STEPS, REQUESTS, -1).transpose(1, 0, 2))


def solution(mesh):
    return jax.shard_map(
        local,
        mesh=mesh,
        in_specs=(
            P("inst", None, "tp"),
            P("inst", None, None, "tp"),
            P("inst", None, None, "tp"),
            P("inst"),
            P("inst", None),
            P("inst", None),
            P("inst", None),
            P("tp", None),
        ),
        out_specs=(P("inst", None, "tp"), P("inst", None, "tp")),
        check_vma=False,
    )
```

```python
import functools
import math

import jax
import jax.numpy as jnp
from jax import lax
from jax.experimental import pallas as pl
from jax.experimental.pallas import tpu as pltpu
from jax.sharding import PartitionSpec as P

HEAD_SIZE = 128
MOST_BLOCKS = 3
STEPS = 3
HEADS = 8
REQUESTS = 8
ENTRIES = 5
INSTANCES = 32
SLOTS = 2
BLOCK_TOKENS = 64
SPAN = MOST_BLOCKS * BLOCK_TOKENS
ROWS = STEPS * HEADS
LENT = REQUESTS * (ENTRIES - 1)
TP = 8
CORES = 2
CHIPS = TP // CORES
WIDTH = 512
GROUP = 8
META = SLOTS * STEPS
SCALE = 1.0 / math.sqrt(HEAD_SIZE)
F32 = jnp.float32
BF16 = jnp.bfloat16
VMEM_SPEC = pl.BlockSpec(memory_space=pltpu.VMEM)
HBM_SPEC = pl.BlockSpec(memory_space=pltpu.HBM)


def in_hbm(array):
    return pltpu.with_memory_space_constraint(array, pltpu.HBM)


def lanes_of(shape):
    return lax.broadcasted_iota(jnp.int32, shape, len(shape) - 1)


def clear_counts(count_ref):
    for index in range(INSTANCES):
        count_ref[index] = 0


def next_rank(count_ref, lender):
    rank = count_ref[lender]
    count_ref[lender] = rank + 1
    return rank


def live_of(ctx_ref, blocks_ref, request, entry, earlier):
    blocks = blocks_ref[request, entry]
    live = jnp.clip(ctx_ref[request] - BLOCK_TOKENS * earlier, 0, BLOCK_TOKENS * blocks)
    return live, earlier + blocks


def start_copies(sources, targets, sems):
    copies = [pltpu.make_async_copy(*pair, sems.at[index]) for index, pair in enumerate(zip(sources, targets))]
    for copy in copies:
        copy.start()
    return copies


def pack_kernel(
    ctx_hbm, lender_hbm, blocks_hbm, slot_hbm, q_hbm, send_ref, rows_ref,
    ctx_ref, lender_ref, blocks_ref, slot_ref, q_ref, regroup, count_ref, sems
):
    copies = start_copies(
        (q_hbm, ctx_hbm, lender_hbm, blocks_hbm, slot_hbm), (q_ref, ctx_ref, lender_ref, blocks_ref, slot_ref), sems
    )
    send_ref[:, META, :, :] = jnp.zeros((INSTANCES, 8, HEAD_SIZE), BF16)
    clear_counts(count_ref)
    for copy in copies:
        copy.wait()
    for step in range(STEPS):
        for head in range(HEADS):
            tile = q_ref[step, :, head * HEAD_SIZE : (head + 1) * HEAD_SIZE].astype(F32)
            regroup[pl.ds(step * HEADS + head, REQUESTS, stride=ROWS), :] = tile
    lane = lanes_of((8, HEAD_SIZE))
    first_row = lax.broadcasted_iota(jnp.int32, (8, HEAD_SIZE), 0) == 0
    for request in range(REQUESTS):
        rows = regroup[request * ROWS : (request + 1) * ROWS, :].astype(BF16)
        rows_ref[request] = rows
        tiles = regroup[request * ROWS : (request + 1) * ROWS, :].reshape(STEPS, HEADS, HEAD_SIZE).astype(BF16)
        earlier = blocks_ref[request, 0]
        for entry in range(1, ENTRIES):
            lender = lender_ref[request, entry]
            rank = next_rank(count_ref, lender)
            live, earlier = live_of(ctx_ref, blocks_ref, request, entry, earlier)
            send_ref[lender, pl.ds(rank * STEPS, STEPS), :, :] = tiles
            meta = send_ref[lender, META].astype(F32)
            meta = jnp.where(first_row & (lane == 2 * rank), slot_ref[request, entry].astype(F32), meta)
            meta = jnp.where(first_row & (lane == 2 * rank + 1), live.astype(F32), meta)
            send_ref[lender, META] = meta.astype(BF16)


def scores_of(query, keys):
    return lax.dot_general(query, keys, (((1,), (1,)), ((), ())), preferred_element_type=F32) * SCALE


def home_kernel(
    ctx_hbm, blocks_hbm, slot_hbm, fresh_hbm, pool_hbm, weight_hbm, rows_ref,
    pool_ref, weight_ref, part_ref, logsum_ref,
    ctx_ref, blocks_ref, slot_ref, fresh_ref, sems
):
    copies = start_copies(
        (ctx_hbm, blocks_hbm, slot_hbm, fresh_hbm, pool_hbm, weight_hbm),
        (ctx_ref, blocks_ref, slot_ref, fresh_ref, pool_ref, weight_ref),
        sems,
    )
    for copy in copies[:-1]:
        copy.wait()
    token = lanes_of((ROWS, SPAN))
    fresh_token = lanes_of((ROWS, STEPS))
    step_of_row = lax.broadcasted_iota(jnp.int32, (ROWS, STEPS), 0) // HEADS
    fresh_seen = fresh_token <= step_of_row
    cached, fresh, values, fresh_values = [], [], [], []
    for request in range(REQUESTS):
        live, _ = live_of(ctx_ref, blocks_ref, request, 0, 0)
        slot = slot_ref[request, 0]
        query = rows_ref[request]
        keys = pool_ref[pl.ds(slot, MOST_BLOCKS), 0].reshape(SPAN, HEAD_SIZE)
        values.append(pool_ref[pl.ds(slot, MOST_BLOCKS), 1].reshape(SPAN, HEAD_SIZE))
        fresh_values.append(fresh_ref[request, :, 1, :].astype(F32))
        cached.append(jnp.where(token < live, scores_of(query, keys), -1e30))
        fresh.append(jnp.where(fresh_seen, scores_of(query, fresh_ref[request, :, 0, :]), -1e30))
    for request in range(REQUESTS):
        top = jnp.maximum(
            jnp.max(cached[request], axis=1, keepdims=True), jnp.max(fresh[request], axis=1, keepdims=True)
        )
        cached_expits = jnp.exp(cached[request] - top)
        fresh_expits = jnp.exp(fresh[request] - top)
        totals = jnp.sum(cached_expits, axis=1, keepdims=True) + jnp.sum(fresh_expits, axis=1, keepdims=True)
        out = jnp.dot(cached_expits.astype(BF16), values[request], preferred_element_type=F32)
        rounded = fresh_expits.astype(BF16).astype(F32)
        for index in range(STEPS):
            out = out + rounded[:, index : index + 1] * fresh_values[request][index : index + 1, :]
        part_ref[request] = (out / totals).astype(BF16)
        logsum_ref[request] = jnp.broadcast_to(top + jnp.log(totals), (ROWS, HEAD_SIZE))
    copies[-1].wait()


def lent_kernel(got_ref, pool_ref, back_ref, meta_vector, meta_ref, item_ref, sem):
    meta_vector[...] = jnp.sum(got_ref[:, META].astype(F32), axis=1).astype(jnp.int32)
    copy = pltpu.make_async_copy(meta_vector, meta_ref, sem)
    copy.start()
    back_ref[:, META, :, :] = jnp.zeros((INSTANCES, 8, HEAD_SIZE), BF16)
    copy.wait()

    def compact(index, found):
        live = meta_ref[index // SLOTS, 2 * (index % SLOTS) + 1]
        item_ref[found] = index
        return found + (live > 0).astype(jnp.int32)

    lax.fori_loop(0, INSTANCES * SLOTS, compact, 0, unroll=8)
    token = lanes_of((ROWS, SPAN))
    lane = lanes_of((8, HEAD_SIZE))

    @pl.loop(0, LENT // GROUP)
    def _(group):
        items = [item_ref[group * GROUP + member] for member in range(GROUP)]
        source = [item // SLOTS for item in items]
        rank = [item % SLOTS for item in items]
        scores, values = [], []
        for member in range(GROUP):
            slot = meta_ref[source[member], 2 * rank[member]]
            live = meta_ref[source[member], 2 * rank[member] + 1]
            query = got_ref[source[member], pl.ds(rank[member] * STEPS, STEPS)]
            query = query.astype(F32).reshape(ROWS, HEAD_SIZE).astype(BF16)
            keys = pool_ref[pl.ds(slot, MOST_BLOCKS), 0].reshape(SPAN, HEAD_SIZE)
            values.append(pool_ref[pl.ds(slot, MOST_BLOCKS), 1].reshape(SPAN, HEAD_SIZE))
            scores.append(jnp.where(token < live, scores_of(query, keys), -1e30))
        parts, logsums = [], []
        for member in range(GROUP):
            top = jnp.max(scores[member], axis=1, keepdims=True)
            expits = jnp.exp(scores[member] - top)
            totals = jnp.sum(expits, axis=1, keepdims=True)
            out = jnp.dot(expits.astype(BF16), values[member], preferred_element_type=F32)
            parts.append(out / totals)
            logsums.append(jnp.broadcast_to(top + jnp.log(totals), (ROWS, HEAD_SIZE)))
        for member in range(GROUP):
            back_ref[source[member], pl.ds(rank[member] * STEPS, STEPS)] = (
                parts[member].reshape(STEPS, HEADS, HEAD_SIZE).astype(BF16)
            )
            high = logsums[member].astype(BF16).astype(F32)
            middle = (logsums[member] - high).astype(BF16).astype(F32)
            low = logsums[member] - high - middle
            at = lane - 9 * rank[member]
            block = back_ref[source[member], META].astype(F32)
            for step in range(STEPS):
                for place, piece in enumerate((high, middle, low)):
                    block = jnp.where(at == 3 * step + place, piece[step * HEADS : (step + 1) * HEADS], block)
            back_ref[source[member], META] = block.astype(BF16)


def merge_kernel(
    lender_hbm, back_ref, part_ref, logsum_ref, weight_ref, attention_ref, terms_ref, merged, count_ref, lender_ref, sem
):
    copy = pltpu.make_async_copy(lender_hbm, lender_ref, sem)
    copy.start()
    clear_counts(count_ref)
    copy.wait()
    lane = lanes_of((8, HEAD_SIZE))
    for request in range(REQUESTS):
        logsums = [logsum_ref[request]]
        parts = [part_ref[request].astype(F32)]
        for entry in range(1, ENTRIES):
            lender = lender_ref[request, entry]
            rank = next_rank(count_ref, lender)
            parts.append(
                back_ref[lender, pl.ds(rank * STEPS, STEPS)].astype(F32).reshape(ROWS, HEAD_SIZE)
            )
            block = back_ref[lender, META].astype(F32)
            at = lane - 9 * rank
            columns = []
            for step in range(STEPS):
                mine = (at >= 3 * step) & (at < 3 * step + 3)
                columns.append(
                    jnp.broadcast_to(
                        jnp.sum(jnp.where(mine, block, 0.0), axis=1, keepdims=True), (HEADS, HEAD_SIZE)
                    )
                )
            logsums.append(jnp.concatenate(columns, axis=0))
        highest = functools.reduce(jnp.maximum, logsums)
        weights = [jnp.exp(logsum - highest) for logsum in logsums]
        total = functools.reduce(jnp.add, weights)
        blended = functools.reduce(jnp.add, [weight * part for weight, part in zip(weights, parts)])
        merged[request * ROWS : (request + 1) * ROWS, :] = blended / total
    for step in range(STEPS):
        for head in range(HEADS):
            tile = merged[pl.ds(step * HEADS + head, REQUESTS, stride=ROWS), :]
            attention_ref[step * REQUESTS : (step + 1) * REQUESTS, head * HEAD_SIZE : (head + 1) * HEAD_SIZE] = tile
    project(attention_ref, weight_ref, terms_ref, 1)


def project(attention_ref, weight_ref, terms_ref, other_core):
    attention = attention_ref[...].astype(BF16)
    place = lax.axis_index("tp")
    core = lax.rem(place + other_core, CORES)

    @pl.loop(0, CHIPS)
    def _(ahead):
        part = lax.rem(place // CORES + ahead, CHIPS) * CORES + core
        columns = pl.ds(pl.multiple_of(part * WIDTH, WIDTH), WIDTH)
        terms = jnp.dot(attention, weight_ref[:, columns], preferred_element_type=F32)
        terms_ref[ahead] = terms.astype(terms_ref.dtype)


def own_kernel(attention_ref, weight_ref, terms_ref, out_ref):
    out_ref[...] = attention_ref[...].reshape(STEPS, REQUESTS, HEADS * HEAD_SIZE).astype(BF16)
    project(attention_ref, weight_ref, terms_ref, 0)


def pair_kernel(mine_ref, other_ref, *sum_refs):
    for ahead, sum_ref in enumerate(sum_refs):
        sum_ref[...] = (mine_ref[ahead] + other_ref[ahead].astype(F32)).astype(sum_ref.dtype)


def total_kernel(own_ref, *refs):
    total = own_ref[...]
    for ref in refs[:-1]:
        total = total + ref[...].astype(F32)
    refs[-1][...] = total.astype(BF16)


def local(
    queries, new_kv, key_value_pool, ctx_len, entry_lender, entry_blocks, entry_slot, out_weight
):
    message = pltpu.VMEM((INSTANCES, META + 1, 8, HEAD_SIZE), BF16)
    rows = pltpu.VMEM((REQUESTS, ROWS, HEAD_SIZE), BF16)
    ctx_space = pltpu.SMEM((REQUESTS,), jnp.int32)
    entry_space = pltpu.SMEM((REQUESTS, ENTRIES), jnp.int32)
    send, query_rows = pl.pallas_call(
        pack_kernel,
        out_shape=(message, rows),
        in_specs=[HBM_SPEC] * 5,
        out_specs=(VMEM_SPEC, VMEM_SPEC),
        scratch_shapes=[
            ctx_space, entry_space, entry_space, entry_space,
            pltpu.VMEM((STEPS, REQUESTS, HEADS * HEAD_SIZE), BF16),
            pltpu.VMEM((REQUESTS * ROWS, HEAD_SIZE), F32),
            pltpu.SMEM((INSTANCES,), jnp.int32),
            pltpu.SemaphoreType.DMA((5,)),
        ],
        compiler_params=pltpu.CompilerParams(vmem_limit_bytes=4 * 2**20),
        name="pack",
    )(*map(in_hbm, (ctx_len, entry_lender, entry_blocks, entry_slot, queries.transpose(1, 0, 2))))
    got = lax.all_to_all(send, "inst", split_axis=0, concat_axis=0, tiled=True)
    pool, weight, home_part, home_logsum = pl.pallas_call(
        home_kernel,
        out_shape=(
            pltpu.VMEM(key_value_pool.shape, BF16),
            pltpu.VMEM(out_weight.shape, BF16),
            rows,
            pltpu.VMEM((REQUESTS, ROWS, HEAD_SIZE), F32),
        ),
        in_specs=[HBM_SPEC] * 6 + [VMEM_SPEC],
        out_specs=(VMEM_SPEC,) * 4,
        scratch_shapes=[
            ctx_space, entry_space, entry_space,
            pltpu.VMEM((REQUESTS, STEPS, 2, HEAD_SIZE), BF16),
            pltpu.SemaphoreType.DMA((6,)),
        ],
        compiler_params=pltpu.CompilerParams(vmem_limit_bytes=16 * 2**20),
        cost_estimate=pl.CostEstimate(flops=10**8, bytes_accessed=12 * 10**6, transcendentals=0),
        name="home",
    )(
        *map(in_hbm, (ctx_len, entry_blocks, entry_slot, new_kv.transpose(0, 2, 1, 3), key_value_pool, out_weight)),
        query_rows,
    )
    back = pl.pallas_call(
        lent_kernel,
        out_shape=message,
        in_specs=[VMEM_SPEC] * 2,
        out_specs=VMEM_SPEC,
        scratch_shapes=[
            pltpu.VMEM((INSTANCES, HEAD_SIZE), jnp.int32),
            pltpu.SMEM((INSTANCES, HEAD_SIZE), jnp.int32),
            pltpu.SMEM((INSTANCES * SLOTS + 1,), jnp.int32),
            pltpu.SemaphoreType.DMA(()),
        ],
        compiler_params=pltpu.CompilerParams(vmem_limit_bytes=12 * 2**20),
        name="lent",
    )(got, pool)
    back = lax.all_to_all(back, "inst", split_axis=0, concat_axis=0, tiled=True)
    merged, terms = pl.pallas_call(
        merge_kernel,
        out_shape=(pltpu.VMEM((ROWS, HEADS * HEAD_SIZE), F32), pltpu.VMEM((CHIPS, ROWS, WIDTH), BF16)),
        in_specs=[HBM_SPEC] + [VMEM_SPEC] * 4,
        out_specs=(VMEM_SPEC, VMEM_SPEC),
        scratch_shapes=[
            pltpu.VMEM((REQUESTS * ROWS, HEAD_SIZE), F32),
            pltpu.SMEM((INSTANCES,), jnp.int32),
            entry_space,
            pltpu.SemaphoreType.DMA(()),
        ],
        compiler_params=pltpu.CompilerParams(vmem_limit_bytes=16 * 2**20),
        name="merge",
    )(in_hbm(entry_lender), back, home_part, home_logsum, weight)
    swap = [(place, place ^ 1) for place in range(TP)]
    other = lax.ppermute(terms, "tp", swap)
    mine, attention = pl.pallas_call(
        own_kernel,
        out_shape=(
            pltpu.VMEM((CHIPS, ROWS, WIDTH), F32),
            jax.ShapeDtypeStruct((STEPS, REQUESTS, HEADS * HEAD_SIZE), BF16),
        ),
        in_specs=[VMEM_SPEC] * 2,
        out_specs=(VMEM_SPEC, VMEM_SPEC),
        compiler_params=pltpu.CompilerParams(vmem_limit_bytes=16 * 2**20),
        cost_estimate=pl.CostEstimate(flops=10**8, bytes_accessed=4 * 10**6, transcendentals=0),
        name="own",
    )(merged, weight)
    sums = pl.pallas_call(
        pair_kernel,
        out_shape=[pltpu.VMEM((ROWS, WIDTH), F32)] + [pltpu.VMEM((ROWS, WIDTH), BF16)] * 3,
        in_specs=[VMEM_SPEC] * 2,
        out_specs=[VMEM_SPEC] * CHIPS,
        compiler_params=pltpu.CompilerParams(vmem_limit_bytes=4 * 2**20),
        name="pair",
    )(mine, other)
    arrived = []
    for ahead in (2, 1, 3):
        shift = [(place, (place + CORES * ahead) % TP) for place in range(TP)]
        arrived.append(lax.ppermute(sums[ahead], "tp", shift))
    projected = pl.pallas_call(
        total_kernel,
        out_shape=jax.ShapeDtypeStruct((ROWS, WIDTH), BF16),
        in_specs=[VMEM_SPEC] * CHIPS,
        out_specs=VMEM_SPEC,
        compiler_params=pltpu.CompilerParams(vmem_limit_bytes=4 * 2**20),
        name="total",
    )(sums[0], *arrived)
    return (attention.transpose(1, 0, 2), projected.reshape(STEPS, REQUESTS, -1).transpose(1, 0, 2))


def solution(mesh):
    return jax.shard_map(
        local,
        mesh=mesh,
        in_specs=(
            P("inst", None, "tp"),
            P("inst", None, None, "tp"),
            P("inst", None, None, "tp"),
            P("inst"),
            P("inst", None),
            P("inst", None),
            P("inst", None),
            P("tp", None),
        ),
        out_specs=(P("inst", None, "tp"), P("inst", None, "tp")),
        check_vma=False,
    )
```

```python
import functools
import math

import jax
import jax.numpy as jnp
from jax import lax
from jax.experimental import pallas as pl
from jax.experimental.pallas import tpu as pltpu
from jax.sharding import PartitionSpec as P

HEAD_SIZE = 128
MOST_BLOCKS = 3
STEPS = 3
HEADS = 8
REQUESTS = 8
ENTRIES = 5
INSTANCES = 32
SLOTS = 2
BLOCK_TOKENS = 64
SPAN = MOST_BLOCKS * BLOCK_TOKENS
ROWS = STEPS * HEADS
LENT = REQUESTS * (ENTRIES - 1)
TP = 8
CORES = 2
POOL = 120
POOL_PIECE = 30
CHIPS = TP // CORES
WIDTH = 512
GROUP = 8
META = SLOTS * STEPS
SCALE = 1.0 / math.sqrt(HEAD_SIZE)
F32 = jnp.float32
BF16 = jnp.bfloat16
VMEM_SPEC = pl.BlockSpec(memory_space=pltpu.VMEM)
HBM_SPEC = pl.BlockSpec(memory_space=pltpu.HBM)


def in_hbm(array):
    return pltpu.with_memory_space_constraint(array, pltpu.HBM)


def lanes_of(shape):
    return lax.broadcasted_iota(jnp.int32, shape, len(shape) - 1)


def clear_counts(count_ref):
    for index in range(INSTANCES):
        count_ref[index] = 0


def next_rank(count_ref, lender):
    rank = count_ref[lender]
    count_ref[lender] = rank + 1
    return rank


def live_of(ctx_ref, blocks_ref, request, entry, earlier):
    blocks = blocks_ref[request, entry]
    live = jnp.clip(ctx_ref[request] - BLOCK_TOKENS * earlier, 0, BLOCK_TOKENS * blocks)
    return live, earlier + blocks


def start_copies(sources, targets, sems):
    copies = [pltpu.make_async_copy(*pair, sems.at[index]) for index, pair in enumerate(zip(sources, targets))]
    for copy in copies:
        copy.start()
    return copies


def pack_kernel(
    ctx_hbm, lender_hbm, blocks_hbm, slot_hbm, q_hbm, send_ref, rows_ref,
    ctx_ref, lender_ref, blocks_ref, slot_ref, q_ref, regroup, count_ref, sems
):
    copies = start_copies(
        (q_hbm, ctx_hbm, lender_hbm, blocks_hbm, slot_hbm), (q_ref, ctx_ref, lender_ref, blocks_ref, slot_ref), sems
    )
    send_ref[:, META, :, :] = jnp.zeros((INSTANCES, 8, HEAD_SIZE), BF16)
    clear_counts(count_ref)
    for copy in copies:
        copy.wait()
    for step in range(STEPS):
        for head in range(HEADS):
            tile = q_ref[step, :, head * HEAD_SIZE : (head + 1) * HEAD_SIZE].astype(F32)
            regroup[pl.ds(step * HEADS + head, REQUESTS, stride=ROWS), :] = tile
    lane = lanes_of((8, HEAD_SIZE))
    first_row = lax.broadcasted_iota(jnp.int32, (8, HEAD_SIZE), 0) == 0
    for request in range(REQUESTS):
        rows = regroup[request * ROWS : (request + 1) * ROWS, :].astype(BF16)
        rows_ref[request] = rows
        tiles = regroup[request * ROWS : (request + 1) * ROWS, :].reshape(STEPS, HEADS, HEAD_SIZE).astype(BF16)
        earlier = blocks_ref[request, 0]
        for entry in range(1, ENTRIES):
            lender = lender_ref[request, entry]
            rank = next_rank(count_ref, lender)
            live, earlier = live_of(ctx_ref, blocks_ref, request, entry, earlier)
            send_ref[lender, pl.ds(rank * STEPS, STEPS), :, :] = tiles
            meta = send_ref[lender, META].astype(F32)
            meta = jnp.where(first_row & (lane == 2 * rank), slot_ref[request, entry].astype(F32), meta)
            meta = jnp.where(first_row & (lane == 2 * rank + 1), live.astype(F32), meta)
            send_ref[lender, META] = meta.astype(BF16)


def scores_of(query, keys):
    return lax.dot_general(query, keys, (((1,), (1,)), ((), ())), preferred_element_type=F32) * SCALE


def home_kernel(
    ctx_hbm, blocks_hbm, slot_hbm, fresh_hbm, pool_hbm, rows_ref,
    part_ref, logsum_ref,
    ctx_ref, blocks_ref, slot_ref, fresh_ref, pool_ref, sems, pool_sems
):
    copies = start_copies(
        (ctx_hbm, blocks_hbm, slot_hbm, fresh_hbm), (ctx_ref, blocks_ref, slot_ref, fresh_ref), sems
    )
    for copy in copies:
        copy.wait()
    copies = start_copies(
        [pool_hbm.at[pl.ds(slot_ref[request, 0], MOST_BLOCKS)] for request in range(REQUESTS)],
        [pool_ref.at[request] for request in range(REQUESTS)],
        pool_sems,
    )
    token = lanes_of((ROWS, SPAN))
    fresh_token = lanes_of((ROWS, STEPS))
    step_of_row = lax.broadcasted_iota(jnp.int32, (ROWS, STEPS), 0) // HEADS
    fresh_seen = fresh_token <= step_of_row
    cached, fresh, values, fresh_values = [], [], [], []
    for request in range(REQUESTS):
        live, _ = live_of(ctx_ref, blocks_ref, request, 0, 0)
        copies[request].wait()
        query = rows_ref[request]
        keys = pool_ref[request, :, 0].reshape(SPAN, HEAD_SIZE)
        values.append(pool_ref[request, :, 1].reshape(SPAN, HEAD_SIZE))
        fresh_values.append(fresh_ref[request, :, 1, :].astype(F32))
        cached.append(jnp.where(token < live, scores_of(query, keys), -1e30))
        fresh.append(jnp.where(fresh_seen, scores_of(query, fresh_ref[request, :, 0, :]), -1e30))
    for request in range(REQUESTS):
        top = jnp.maximum(
            jnp.max(cached[request], axis=1, keepdims=True), jnp.max(fresh[request], axis=1, keepdims=True)
        )
        cached_expits = jnp.exp(cached[request] - top)
        fresh_expits = jnp.exp(fresh[request] - top)
        totals = jnp.sum(cached_expits, axis=1, keepdims=True) + jnp.sum(fresh_expits, axis=1, keepdims=True)
        out = jnp.dot(cached_expits.astype(BF16), values[request], preferred_element_type=F32)
        rounded = fresh_expits.astype(BF16).astype(F32)
        for index in range(STEPS):
            out = out + rounded[:, index : index + 1] * fresh_values[request][index : index + 1, :]
        part_ref[request] = (out / totals).astype(BF16)
        logsum_ref[request] = jnp.broadcast_to(top + jnp.log(totals), (ROWS, HEAD_SIZE))


def lent_kernel(got_ref, pool_hbm, back_ref, pool_ref, meta_vector, meta_ref, item_ref, sem, pool_sems):
    pieces = [pl.ds(piece * POOL_PIECE, POOL_PIECE) for piece in range(POOL // POOL_PIECE)]
    copies = start_copies(
        [pool_hbm.at[piece] for piece in pieces], [pool_ref.at[piece] for piece in pieces], pool_sems
    )
    meta_vector[...] = jnp.sum(got_ref[:, META].astype(F32), axis=1).astype(jnp.int32)
    copy = pltpu.make_async_copy(meta_vector, meta_ref, sem)
    copy.start()
    back_ref[:, META, :, :] = jnp.zeros((INSTANCES, 8, HEAD_SIZE), BF16)
    copy.wait()

    def compact(index, found):
        live = meta_ref[index // SLOTS, 2 * (index % SLOTS) + 1]
        item_ref[found] = index
        return found + (live > 0).astype(jnp.int32)

    lax.fori_loop(0, INSTANCES * SLOTS, compact, 0, unroll=8)
    for copy in copies:
        copy.wait()
    token = lanes_of((ROWS, SPAN))
    lane = lanes_of((8, HEAD_SIZE))

    @pl.loop(0, LENT // GROUP)
    def _(group):
        items = [item_ref[group * GROUP + member] for member in range(GROUP)]
        source = [item // SLOTS for item in items]
        rank = [item % SLOTS for item in items]
        scores, values = [], []
        for member in range(GROUP):
            slot = meta_ref[source[member], 2 * rank[member]]
            live = meta_ref[source[member], 2 * rank[member] + 1]
            query = got_ref[source[member], pl.ds(rank[member] * STEPS, STEPS)]
            query = query.astype(F32).reshape(ROWS, HEAD_SIZE).astype(BF16)
            keys = pool_ref[pl.ds(slot, MOST_BLOCKS), 0].reshape(SPAN, HEAD_SIZE)
            values.append(pool_ref[pl.ds(slot, MOST_BLOCKS), 1].reshape(SPAN, HEAD_SIZE))
            scores.append(jnp.where(token < live, scores_of(query, keys), -1e30))
        parts, logsums = [], []
        for member in range(GROUP):
            top = jnp.max(scores[member], axis=1, keepdims=True)
            expits = jnp.exp(scores[member] - top)
            totals = jnp.sum(expits, axis=1, keepdims=True)
            out = jnp.dot(expits.astype(BF16), values[member], preferred_element_type=F32)
            parts.append(out / totals)
            logsums.append(jnp.broadcast_to(top + jnp.log(totals), (ROWS, HEAD_SIZE)))
        for member in range(GROUP):
            back_ref[source[member], pl.ds(rank[member] * STEPS, STEPS)] = (
                parts[member].reshape(STEPS, HEADS, HEAD_SIZE).astype(BF16)
            )
            high = logsums[member].astype(BF16).astype(F32)
            middle = (logsums[member] - high).astype(BF16).astype(F32)
            low = logsums[member] - high - middle
            at = lane - 9 * rank[member]
            block = back_ref[source[member], META].astype(F32)
            for step in range(STEPS):
                for place, piece in enumerate((high, middle, low)):
                    block = jnp.where(at == 3 * step + place, piece[step * HEADS : (step + 1) * HEADS], block)
            back_ref[source[member], META] = block.astype(BF16)


def merge_kernel(
    lender_hbm, back_ref, part_ref, logsum_ref, weight_hbm,
    attention_ref, terms_ref,
    merged, count_ref, lender_ref, weight_ref, sem, weight_sems
):
    copies = start_weights(weight_hbm, weight_ref, weight_sems, 1)
    copy = pltpu.make_async_copy(lender_hbm, lender_ref, sem)
    copy.start()
    clear_counts(count_ref)
    copy.wait()
    lane = lanes_of((8, HEAD_SIZE))
    for request in range(REQUESTS):
        logsums = [logsum_ref[request]]
        parts = [part_ref[request].astype(F32)]
        for entry in range(1, ENTRIES):
            lender = lender_ref[request, entry]
            rank = next_rank(count_ref, lender)
            parts.append(
                back_ref[lender, pl.ds(rank * STEPS, STEPS)].astype(F32).reshape(ROWS, HEAD_SIZE)
            )
            block = back_ref[lender, META].astype(F32)
            at = lane - 9 * rank
            columns = []
            for step in range(STEPS):
                mine = (at >= 3 * step) & (at < 3 * step + 3)
                columns.append(
                    jnp.broadcast_to(
                        jnp.sum(jnp.where(mine, block, 0.0), axis=1, keepdims=True), (HEADS, HEAD_SIZE)
                    )
                )
            logsums.append(jnp.concatenate(columns, axis=0))
        highest = functools.reduce(jnp.maximum, logsums)
        weights = [jnp.exp(logsum - highest) for logsum in logsums]
        total = functools.reduce(jnp.add, weights)
        blended = functools.reduce(jnp.add, [weight * part for weight, part in zip(weights, parts)])
        merged[request * ROWS : (request + 1) * ROWS, :] = blended / total
    for step in range(STEPS):
        for head in range(HEADS):
            tile = merged[pl.ds(step * HEADS + head, REQUESTS, stride=ROWS), :]
            attention_ref[step * REQUESTS : (step + 1) * REQUESTS, head * HEAD_SIZE : (head + 1) * HEAD_SIZE] = tile
    project(attention_ref, weight_ref, terms_ref, copies)


def start_weights(weight_hbm, weight_ref, sems, other_core):
    place = lax.axis_index("tp")
    core = lax.rem(place + other_core, CORES)
    parts = [lax.rem(place // CORES + ahead, CHIPS) * CORES + core for ahead in range(CHIPS)]
    return start_copies(
        [weight_hbm.at[:, pl.ds(pl.multiple_of(part * WIDTH, WIDTH), WIDTH)] for part in parts],
        [weight_ref.at[ahead] for ahead in range(CHIPS)],
        sems,
    )


def project(attention_ref, weight_ref, terms_ref, copies):
    attention = attention_ref[...].astype(BF16)
    for ahead in range(CHIPS):
        copies[ahead].wait()
        terms = jnp.dot(attention, weight_ref[ahead], preferred_element_type=F32)
        terms_ref[ahead] = terms.astype(terms_ref.dtype)


def own_kernel(attention_ref, weight_hbm, terms_ref, out_ref, weight_ref, weight_sems):
    copies = start_weights(weight_hbm, weight_ref, weight_sems, 0)
    out_ref[...] = attention_ref[...].reshape(STEPS, REQUESTS, HEADS * HEAD_SIZE).astype(BF16)
    project(attention_ref, weight_ref, terms_ref, copies)


def pair_kernel(mine_ref, other_ref, *sum_refs):
    for ahead, sum_ref in enumerate(sum_refs):
        sum_ref[...] = (mine_ref[ahead] + other_ref[ahead].astype(F32)).astype(sum_ref.dtype)


def total_kernel(own_ref, *refs):
    total = own_ref[...]
    for ref in refs[:-1]:
        total = total + ref[...].astype(F32)
    refs[-1][...] = total.astype(BF16)


def local(
    queries, new_kv, key_value_pool, ctx_len, entry_lender, entry_blocks, entry_slot, out_weight
):
    message = pltpu.VMEM((INSTANCES, META + 1, 8, HEAD_SIZE), BF16)
    rows = pltpu.VMEM((REQUESTS, ROWS, HEAD_SIZE), BF16)
    weight_space = pltpu.VMEM((CHIPS, HEADS * HEAD_SIZE, WIDTH), BF16)
    ctx_space = pltpu.SMEM((REQUESTS,), jnp.int32)
    entry_space = pltpu.SMEM((REQUESTS, ENTRIES), jnp.int32)
    send, query_rows = pl.pallas_call(
        pack_kernel,
        out_shape=(message, rows),
        in_specs=[HBM_SPEC] * 5,
        out_specs=(VMEM_SPEC, VMEM_SPEC),
        scratch_shapes=[
            ctx_space, entry_space, entry_space, entry_space,
            pltpu.VMEM((STEPS, REQUESTS, HEADS * HEAD_SIZE), BF16),
            pltpu.VMEM((REQUESTS * ROWS, HEAD_SIZE), F32),
            pltpu.SMEM((INSTANCES,), jnp.int32),
            pltpu.SemaphoreType.DMA((5,)),
        ],
        compiler_params=pltpu.CompilerParams(vmem_limit_bytes=4 * 2**20),
        name="pack",
    )(*map(in_hbm, (ctx_len, entry_lender, entry_blocks, entry_slot, queries.transpose(1, 0, 2))))
    got = lax.all_to_all(send, "inst", split_axis=0, concat_axis=0, tiled=True)
    home_part, home_logsum = pl.pallas_call(
        home_kernel,
        out_shape=(rows, pltpu.VMEM((REQUESTS, ROWS, HEAD_SIZE), F32)),
        in_specs=[HBM_SPEC] * 5 + [VMEM_SPEC],
        out_specs=(VMEM_SPEC,) * 2,
        scratch_shapes=[
            ctx_space, entry_space, entry_space,
            pltpu.VMEM((REQUESTS, STEPS, 2, HEAD_SIZE), BF16),
            pltpu.VMEM((REQUESTS, MOST_BLOCKS, 2, BLOCK_TOKENS, HEAD_SIZE), BF16),
            pltpu.SemaphoreType.DMA((4,)),
            pltpu.SemaphoreType.DMA((REQUESTS,)),
        ],
        compiler_params=pltpu.CompilerParams(vmem_limit_bytes=8 * 2**20),
        cost_estimate=pl.CostEstimate(flops=10**8, bytes_accessed=12 * 10**6, transcendentals=0),
        name="home",
    )(
        *map(in_hbm, (ctx_len, entry_blocks, entry_slot, new_kv.transpose(0, 2, 1, 3), key_value_pool)),
        query_rows,
    )
    back = pl.pallas_call(
        lent_kernel,
        out_shape=message,
        in_specs=[VMEM_SPEC, HBM_SPEC],
        out_specs=VMEM_SPEC,
        scratch_shapes=[
            pltpu.VMEM(key_value_pool.shape, BF16),
            pltpu.VMEM((INSTANCES, HEAD_SIZE), jnp.int32),
            pltpu.SMEM((INSTANCES, HEAD_SIZE), jnp.int32),
            pltpu.SMEM((INSTANCES * SLOTS + 1,), jnp.int32),
            pltpu.SemaphoreType.DMA(()),
            pltpu.SemaphoreType.DMA((POOL // POOL_PIECE,)),
        ],
        compiler_params=pltpu.CompilerParams(vmem_limit_bytes=12 * 2**20),
        name="lent",
    )(got, in_hbm(key_value_pool))
    back = lax.all_to_all(back, "inst", split_axis=0, concat_axis=0, tiled=True)
    merged, terms = pl.pallas_call(
        merge_kernel,
        out_shape=(pltpu.VMEM((ROWS, HEADS * HEAD_SIZE), F32), pltpu.VMEM((CHIPS, ROWS, WIDTH), BF16)),
        in_specs=[HBM_SPEC] + [VMEM_SPEC] * 3 + [HBM_SPEC],
        out_specs=(VMEM_SPEC, VMEM_SPEC),
        scratch_shapes=[
            pltpu.VMEM((REQUESTS * ROWS, HEAD_SIZE), F32),
            pltpu.SMEM((INSTANCES,), jnp.int32),
            entry_space,
            weight_space,
            pltpu.SemaphoreType.DMA(()),
            pltpu.SemaphoreType.DMA((CHIPS,)),
        ],
        compiler_params=pltpu.CompilerParams(vmem_limit_bytes=16 * 2**20),
        name="merge",
    )(in_hbm(entry_lender), back, home_part, home_logsum, in_hbm(out_weight))
    swap = [(place, place ^ 1) for place in range(TP)]
    other = lax.ppermute(terms, "tp", swap)
    mine, attention = pl.pallas_call(
        own_kernel,
        out_shape=(
            pltpu.VMEM((CHIPS, ROWS, WIDTH), F32),
            jax.ShapeDtypeStruct((STEPS, REQUESTS, HEADS * HEAD_SIZE), BF16),
        ),
        in_specs=[VMEM_SPEC, HBM_SPEC],
        out_specs=(VMEM_SPEC, VMEM_SPEC),
        scratch_shapes=[weight_space, pltpu.SemaphoreType.DMA((CHIPS,))],
        compiler_params=pltpu.CompilerParams(vmem_limit_bytes=16 * 2**20),
        cost_estimate=pl.CostEstimate(flops=10**8, bytes_accessed=4 * 10**6, transcendentals=0),
        name="own",
    )(merged, in_hbm(out_weight))
    sums = pl.pallas_call(
        pair_kernel,
        out_shape=[pltpu.VMEM((ROWS, WIDTH), F32)] + [pltpu.VMEM((ROWS, WIDTH), BF16)] * 3,
        in_specs=[VMEM_SPEC] * 2,
        out_specs=[VMEM_SPEC] * CHIPS,
        compiler_params=pltpu.CompilerParams(vmem_limit_bytes=4 * 2**20),
        name="pair",
    )(mine, other)
    arrived = []
    for ahead in (2, 1, 3):
        shift = [(place, (place + CORES * ahead) % TP) for place in range(TP)]
        arrived.append(lax.ppermute(sums[ahead], "tp", shift))
    projected = pl.pallas_call(
        total_kernel,
        out_shape=jax.ShapeDtypeStruct((ROWS, WIDTH), BF16),
        in_specs=[VMEM_SPEC] * CHIPS,
        out_specs=VMEM_SPEC,
        compiler_params=pltpu.CompilerParams(vmem_limit_bytes=4 * 2**20),
        name="total",
    )(sums[0], *arrived)
    return (attention.transpose(1, 0, 2), projected.reshape(STEPS, REQUESTS, -1).transpose(1, 0, 2))


def solution(mesh):
    return jax.shard_map(
        local,
        mesh=mesh,
        in_specs=(
            P("inst", None, "tp"),
            P("inst", None, None, "tp"),
            P("inst", None, None, "tp"),
            P("inst"),
            P("inst", None),
            P("inst", None),
            P("inst", None),
            P("tp", None),
        ),
        out_specs=(P("inst", None, "tp"), P("inst", None, "tp")),
        check_vma=False,
    )
```

```python
import functools
import math

import jax
import jax.numpy as jnp
from jax import lax
from jax.experimental import pallas as pl
from jax.experimental.pallas import tpu as pltpu
from jax.sharding import PartitionSpec as P

HEAD_SIZE = 128
MOST_BLOCKS = 3
STEPS = 3
HEADS = 8
REQUESTS = 8
ENTRIES = 5
INSTANCES = 32
SLOTS = 2
BLOCK_TOKENS = 64
SPAN = MOST_BLOCKS * BLOCK_TOKENS
ROWS = STEPS * HEADS
LENT = REQUESTS * (ENTRIES - 1)
TP = 8
CORES = 2
POOL = 120
POOL_PIECE = 60
CHIPS = TP // CORES
WIDTH = 512
FETCHED = 2
META = SLOTS * STEPS
SCALE = 1.0 / math.sqrt(HEAD_SIZE)
F32 = jnp.float32
BF16 = jnp.bfloat16
VMEM_SPEC = pl.BlockSpec(memory_space=pltpu.VMEM)
HBM_SPEC = pl.BlockSpec(memory_space=pltpu.HBM)


def in_hbm(array):
    return pltpu.with_memory_space_constraint(array, pltpu.HBM)


def lanes_of(shape):
    return lax.broadcasted_iota(jnp.int32, shape, len(shape) - 1)


def clear_counts(count_ref):
    for index in range(INSTANCES):
        count_ref[index] = 0


def next_rank(count_ref, lender):
    rank = count_ref[lender]
    count_ref[lender] = rank + 1
    return rank


def live_of(ctx_ref, blocks_ref, request, entry, earlier):
    blocks = blocks_ref[request, entry]
    live = jnp.clip(ctx_ref[request] - BLOCK_TOKENS * earlier, 0, BLOCK_TOKENS * blocks)
    return live, earlier + blocks


def start_copies(sources, targets, sems):
    copies = [pltpu.make_async_copy(*pair, sems.at[index]) for index, pair in enumerate(zip(sources, targets))]
    for copy in copies:
        copy.start()
    return copies


def pack_kernel(
    ctx_hbm, lender_hbm, blocks_hbm, slot_hbm, q_hbm, send_ref, rows_ref,
    ctx_ref, lender_ref, blocks_ref, slot_ref, q_ref, regroup, count_ref, sems
):
    copies = start_copies(
        (q_hbm, ctx_hbm, lender_hbm, blocks_hbm, slot_hbm), (q_ref, ctx_ref, lender_ref, blocks_ref, slot_ref), sems
    )
    send_ref[:, META, :, :] = jnp.zeros((INSTANCES, 8, HEAD_SIZE), BF16)
    clear_counts(count_ref)
    for copy in copies:
        copy.wait()
    for step in range(STEPS):
        for head in range(HEADS):
            tile = q_ref[step, :, head * HEAD_SIZE : (head + 1) * HEAD_SIZE].astype(F32)
            regroup[pl.ds(step * HEADS + head, REQUESTS, stride=ROWS), :] = tile
    lane = lanes_of((8, HEAD_SIZE))
    first_row = lax.broadcasted_iota(jnp.int32, (8, HEAD_SIZE), 0) == 0
    for request in range(REQUESTS):
        rows = regroup[request * ROWS : (request + 1) * ROWS, :].astype(BF16)
        rows_ref[request] = rows
        tiles = regroup[request * ROWS : (request + 1) * ROWS, :].reshape(STEPS, HEADS, HEAD_SIZE).astype(BF16)
        earlier = blocks_ref[request, 0]
        for entry in range(1, ENTRIES):
            lender = lender_ref[request, entry]
            rank = next_rank(count_ref, lender)
            live, earlier = live_of(ctx_ref, blocks_ref, request, entry, earlier)
            send_ref[lender, pl.ds(rank * STEPS, STEPS), :, :] = tiles
            meta = send_ref[lender, META].astype(F32)
            meta = jnp.where(first_row & (lane == 2 * rank), slot_ref[request, entry].astype(F32), meta)
            meta = jnp.where(first_row & (lane == 2 * rank + 1), live.astype(F32), meta)
            send_ref[lender, META] = meta.astype(BF16)


def scores_of(query, keys):
    return lax.dot_general(query, keys, (((1,), (1,)), ((), ())), preferred_element_type=F32) * SCALE


def home_kernel(
    ctx_hbm, blocks_hbm, slot_hbm, fresh_hbm, pool_hbm, rows_ref,
    part_ref, logsum_ref, keys_ref,
    ctx_ref, blocks_ref, slot_ref, fresh_ref, pool_ref, sems, pool_sems, keys_sem
):
    copies = start_copies(
        (ctx_hbm, blocks_hbm, slot_hbm, fresh_hbm), (ctx_ref, blocks_ref, slot_ref, fresh_ref), sems
    )
    for copy in copies:
        copy.wait()
    copies = start_copies(
        [pool_hbm.at[pl.ds(slot_ref[request, 0], MOST_BLOCKS)] for request in range(REQUESTS)],
        [pool_ref.at[request] for request in range(REQUESTS)],
        pool_sems,
    )
    all_keys = pltpu.make_async_copy(pool_hbm.at[:, 0], keys_ref, keys_sem)
    all_keys.start()
    token = lanes_of((ROWS, SPAN))
    fresh_token = lanes_of((ROWS, STEPS))
    step_of_row = lax.broadcasted_iota(jnp.int32, (ROWS, STEPS), 0) // HEADS
    fresh_seen = fresh_token <= step_of_row
    cached, fresh, values, fresh_values = [], [], [], []
    for request in range(REQUESTS):
        live, _ = live_of(ctx_ref, blocks_ref, request, 0, 0)
        copies[request].wait()
        query = rows_ref[request]
        keys = pool_ref[request, :, 0].reshape(SPAN, HEAD_SIZE)
        values.append(pool_ref[request, :, 1].reshape(SPAN, HEAD_SIZE))
        fresh_values.append(fresh_ref[request, :, 1, :].astype(F32))
        cached.append(jnp.where(token < live, scores_of(query, keys), -1e30))
        fresh.append(jnp.where(fresh_seen, scores_of(query, fresh_ref[request, :, 0, :]), -1e30))
    for request in range(REQUESTS):
        top = jnp.maximum(
            jnp.max(cached[request], axis=1, keepdims=True), jnp.max(fresh[request], axis=1, keepdims=True)
        )
        cached_expits = jnp.exp(cached[request] - top)
        fresh_expits = jnp.exp(fresh[request] - top)
        totals = jnp.sum(cached_expits, axis=1, keepdims=True) + jnp.sum(fresh_expits, axis=1, keepdims=True)
        out = jnp.dot(cached_expits.astype(BF16), values[request], preferred_element_type=F32)
        rounded = fresh_expits.astype(BF16).astype(F32)
        for index in range(STEPS):
            out = out + rounded[:, index : index + 1] * fresh_values[request][index : index + 1, :]
        part_ref[request] = (out / totals).astype(BF16)
        logsum_ref[request] = jnp.broadcast_to(top + jnp.log(totals), (ROWS, HEAD_SIZE))
    all_keys.wait()


def lent_kernel(
    got_ref, keys_ref, pool_hbm, back_ref, token_ref, values_ref, meta_vector, meta_ref, item_ref, sem, pool_sems
):
    pieces = [pl.ds(piece * POOL_PIECE, POOL_PIECE) for piece in range(POOL // POOL_PIECE)]
    copies = start_copies(
        [pool_hbm.at[piece, 1] for piece in pieces], [values_ref.at[piece] for piece in pieces], pool_sems
    )
    token_ref[...] = jnp.zeros_like(token_ref)
    meta_vector[...] = jnp.sum(got_ref[:, META].astype(F32), axis=1).astype(jnp.int32)
    copy = pltpu.make_async_copy(meta_vector, meta_ref, sem)
    copy.start()
    back_ref[:, META, :, :] = jnp.zeros((INSTANCES, 8, HEAD_SIZE), BF16)
    copy.wait()

    def compact(index, found):
        live = meta_ref[index // SLOTS, 2 * (index % SLOTS) + 1]
        item_ref[found] = index
        return found + (live > 0).astype(jnp.int32)

    lax.fori_loop(0, INSTANCES * SLOTS, compact, 0, unroll=INSTANCES * SLOTS)
    token = lanes_of((ROWS, SPAN))
    lane = lanes_of((8, HEAD_SIZE))
    items = [item_ref[member] for member in range(LENT)]
    source = [item // SLOTS for item in items]
    rank = [item % SLOTS for item in items]
    scores = []
    for member in range(LENT):
        slot = meta_ref[source[member], 2 * rank[member]]
        live = meta_ref[source[member], 2 * rank[member] + 1]
        query = got_ref[source[member], pl.ds(rank[member] * STEPS, STEPS)]
        query = query.astype(F32).reshape(ROWS, HEAD_SIZE).astype(BF16)
        keys = keys_ref[pl.ds(slot, MOST_BLOCKS)].reshape(SPAN, HEAD_SIZE)
        scores.append(jnp.where(token < live, scores_of(query, keys), -1e30))
    for copy in copies:
        copy.wait()
    parts, logsums = [], []
    for member in range(LENT):
        slot = meta_ref[source[member], 2 * rank[member]]
        values = values_ref[pl.ds(slot, MOST_BLOCKS)].reshape(SPAN, HEAD_SIZE)
        top = jnp.max(scores[member], axis=1, keepdims=True)
        expits = jnp.exp(scores[member] - top)
        totals = jnp.sum(expits, axis=1, keepdims=True)
        out = jnp.dot(expits.astype(BF16), values, preferred_element_type=F32)
        parts.append(out / totals)
        logsums.append(jnp.broadcast_to(top + jnp.log(totals), (ROWS, HEAD_SIZE)))
    for member in range(LENT):
        back_ref[source[member], pl.ds(rank[member] * STEPS, STEPS)] = (
            parts[member].reshape(STEPS, HEADS, HEAD_SIZE).astype(BF16)
        )
        high = logsums[member].astype(BF16).astype(F32)
        middle = (logsums[member] - high).astype(BF16).astype(F32)
        low = logsums[member] - high - middle
        at = lane - 9 * rank[member]
        block = back_ref[source[member], META].astype(F32)
        for step in range(STEPS):
            for place, piece in enumerate((high, middle, low)):
                block = jnp.where(at == 3 * step + place, piece[step * HEADS : (step + 1) * HEADS], block)
        back_ref[source[member], META] = block.astype(BF16)


def weight_columns(weight_hbm, other_core, ahead):
    place = lax.axis_index("tp")
    core = lax.rem(place + other_core, CORES)
    part = lax.rem(place // CORES + ahead, CHIPS) * CORES + core
    return weight_hbm.at[:, pl.ds(pl.multiple_of(part * WIDTH, WIDTH), WIDTH)]


def fetch_kernel(weight_hbm, token_ref, fetched_ref, sems):
    copies = start_copies(
        [weight_columns(weight_hbm, 1, ahead) for ahead in range(FETCHED)],
        [fetched_ref.at[ahead] for ahead in range(FETCHED)],
        sems,
    )
    for copy in copies:
        copy.wait()


def merge_kernel(
    lender_hbm, back_ref, part_ref, logsum_ref, fetched_ref, weight_hbm,
    attention_ref, terms_ref, own_ref,
    merged, count_ref, lender_ref, rest_ref, sem, rest_sems, own_sems
):
    copy = pltpu.make_async_copy(lender_hbm, lender_ref, sem)
    copy.start()
    rest = start_copies(
        [weight_columns(weight_hbm, 1, ahead) for ahead in range(FETCHED, CHIPS)],
        [rest_ref.at[ahead - FETCHED] for ahead in range(FETCHED, CHIPS)],
        rest_sems,
    )
    own = start_copies(
        [weight_columns(weight_hbm, 0, ahead) for ahead in range(CHIPS)],
        [own_ref.at[ahead] for ahead in range(CHIPS)],
        own_sems,
    )
    clear_counts(count_ref)
    copy.wait()
    lane = lanes_of((8, HEAD_SIZE))
    for request in range(REQUESTS):
        logsums = [logsum_ref[request]]
        parts = [part_ref[request].astype(F32)]
        for entry in range(1, ENTRIES):
            lender = lender_ref[request, entry]
            rank = next_rank(count_ref, lender)
            parts.append(
                back_ref[lender, pl.ds(rank * STEPS, STEPS)].astype(F32).reshape(ROWS, HEAD_SIZE)
            )
            block = back_ref[lender, META].astype(F32)
            at = lane - 9 * rank
            columns = []
            for step in range(STEPS):
                mine = (at >= 3 * step) & (at < 3 * step + 3)
                columns.append(
                    jnp.broadcast_to(
                        jnp.sum(jnp.where(mine, block, 0.0), axis=1, keepdims=True), (HEADS, HEAD_SIZE)
                    )
                )
            logsums.append(jnp.concatenate(columns, axis=0))
        highest = functools.reduce(jnp.maximum, logsums)
        weights = [jnp.exp(logsum - highest) for logsum in logsums]
        total = functools.reduce(jnp.add, weights)
        blended = functools.reduce(jnp.add, [weight * part for weight, part in zip(weights, parts)])
        merged[request * ROWS : (request + 1) * ROWS, :] = blended / total
    for step in range(STEPS):
        for head in range(HEADS):
            tile = merged[pl.ds(step * HEADS + head, REQUESTS, stride=ROWS), :]
            attention_ref[step * REQUESTS : (step + 1) * REQUESTS, head * HEAD_SIZE : (head + 1) * HEAD_SIZE] = tile
    attention = attention_ref[...].astype(BF16)
    for ahead in range(CHIPS):
        if ahead >= FETCHED:
            rest[ahead - FETCHED].wait()
        weight = fetched_ref[ahead] if ahead < FETCHED else rest_ref[ahead - FETCHED]
        terms_ref[ahead] = jnp.dot(attention, weight, preferred_element_type=F32).astype(BF16)
    for copy in own:
        copy.wait()


def own_kernel(attention_ref, weight_ref, terms_ref, out_ref):
    out_ref[...] = attention_ref[...].reshape(STEPS, REQUESTS, HEADS * HEAD_SIZE).astype(BF16)
    attention = attention_ref[...].astype(BF16)
    for ahead in range(CHIPS):
        terms_ref[ahead] = jnp.dot(attention, weight_ref[ahead], preferred_element_type=F32)


def pair_kernel(mine_ref, other_ref, *sum_refs):
    for ahead, sum_ref in enumerate(sum_refs):
        sum_ref[...] = (mine_ref[ahead] + other_ref[ahead].astype(F32)).astype(sum_ref.dtype)


def total_kernel(own_ref, *refs):
    total = own_ref[...]
    for ref in refs[:-1]:
        total = total + ref[...].astype(F32)
    refs[-1][...] = total.astype(BF16)


def local(
    queries, new_kv, key_value_pool, ctx_len, entry_lender, entry_blocks, entry_slot, out_weight
):
    message = pltpu.VMEM((INSTANCES, META + 1, 8, HEAD_SIZE), BF16)
    rows = pltpu.VMEM((REQUESTS, ROWS, HEAD_SIZE), BF16)
    weight_space = lambda count: pltpu.VMEM((count, HEADS * HEAD_SIZE, WIDTH), BF16)
    ctx_space = pltpu.SMEM((REQUESTS,), jnp.int32)
    entry_space = pltpu.SMEM((REQUESTS, ENTRIES), jnp.int32)
    send, query_rows = pl.pallas_call(
        pack_kernel,
        out_shape=(message, rows),
        in_specs=[HBM_SPEC] * 5,
        out_specs=(VMEM_SPEC, VMEM_SPEC),
        scratch_shapes=[
            ctx_space, entry_space, entry_space, entry_space,
            pltpu.VMEM((STEPS, REQUESTS, HEADS * HEAD_SIZE), BF16),
            pltpu.VMEM((REQUESTS * ROWS, HEAD_SIZE), F32),
            pltpu.SMEM((INSTANCES,), jnp.int32),
            pltpu.SemaphoreType.DMA((5,)),
        ],
        compiler_params=pltpu.CompilerParams(vmem_limit_bytes=4 * 2**20),
        name="pack",
    )(*map(in_hbm, (ctx_len, entry_lender, entry_blocks, entry_slot, queries.transpose(1, 0, 2))))
    got = lax.all_to_all(send, "inst", split_axis=0, concat_axis=0, tiled=True)
    home_part, home_logsum, keys = pl.pallas_call(
        home_kernel,
        out_shape=(
            rows,
            pltpu.VMEM((REQUESTS, ROWS, HEAD_SIZE), F32),
            pltpu.VMEM((POOL, BLOCK_TOKENS, HEAD_SIZE), BF16),
        ),
        in_specs=[HBM_SPEC] * 5 + [VMEM_SPEC],
        out_specs=(VMEM_SPEC,) * 3,
        scratch_shapes=[
            ctx_space, entry_space, entry_space,
            pltpu.VMEM((REQUESTS, STEPS, 2, HEAD_SIZE), BF16),
            pltpu.VMEM((REQUESTS, MOST_BLOCKS, 2, BLOCK_TOKENS, HEAD_SIZE), BF16),
            pltpu.SemaphoreType.DMA((4,)),
            pltpu.SemaphoreType.DMA((REQUESTS,)),
            pltpu.SemaphoreType.DMA(()),
        ],
        compiler_params=pltpu.CompilerParams(vmem_limit_bytes=8 * 2**20),
        cost_estimate=pl.CostEstimate(flops=10**8, bytes_accessed=12 * 10**6, transcendentals=0),
        name="home",
    )(
        *map(in_hbm, (ctx_len, entry_blocks, entry_slot, new_kv.transpose(0, 2, 1, 3), key_value_pool)),
        query_rows,
    )
    back, token = pl.pallas_call(
        lent_kernel,
        out_shape=(message, pltpu.VMEM((8, HEAD_SIZE), F32)),
        in_specs=[VMEM_SPEC, VMEM_SPEC, HBM_SPEC],
        out_specs=(VMEM_SPEC, VMEM_SPEC),
        scratch_shapes=[
            pltpu.VMEM((POOL, BLOCK_TOKENS, HEAD_SIZE), BF16),
            pltpu.VMEM((INSTANCES, HEAD_SIZE), jnp.int32),
            pltpu.SMEM((INSTANCES, HEAD_SIZE), jnp.int32),
            pltpu.SMEM((INSTANCES * SLOTS + 1,), jnp.int32),
            pltpu.SemaphoreType.DMA(()),
            pltpu.SemaphoreType.DMA((POOL // POOL_PIECE,)),
        ],
        compiler_params=pltpu.CompilerParams(vmem_limit_bytes=12 * 2**20),
        name="lent",
    )(got, keys, in_hbm(key_value_pool))
    back = lax.all_to_all(back, "inst", split_axis=0, concat_axis=0, tiled=True)
    fetched = pl.pallas_call(
        fetch_kernel,
        out_shape=weight_space(FETCHED),
        in_specs=[HBM_SPEC, VMEM_SPEC],
        out_specs=VMEM_SPEC,
        scratch_shapes=[pltpu.SemaphoreType.DMA((FETCHED,))],
        compiler_params=pltpu.CompilerParams(vmem_limit_bytes=4 * 2**20),
        cost_estimate=pl.CostEstimate(flops=10**6, bytes_accessed=4 * 10**6, transcendentals=0),
        name="fetch",
    )(in_hbm(out_weight), token)
    merged, terms, own_weight = pl.pallas_call(
        merge_kernel,
        out_shape=(
            pltpu.VMEM((ROWS, HEADS * HEAD_SIZE), F32),
            pltpu.VMEM((CHIPS, ROWS, WIDTH), BF16),
            weight_space(CHIPS),
        ),
        in_specs=[HBM_SPEC] + [VMEM_SPEC] * 4 + [HBM_SPEC],
        out_specs=(VMEM_SPEC,) * 3,
        scratch_shapes=[
            pltpu.VMEM((REQUESTS * ROWS, HEAD_SIZE), F32),
            pltpu.SMEM((INSTANCES,), jnp.int32),
            entry_space,
            weight_space(CHIPS - FETCHED),
            pltpu.SemaphoreType.DMA(()),
            pltpu.SemaphoreType.DMA((CHIPS - FETCHED,)),
            pltpu.SemaphoreType.DMA((CHIPS,)),
        ],
        compiler_params=pltpu.CompilerParams(vmem_limit_bytes=16 * 2**20),
        name="merge",
    )(in_hbm(entry_lender), back, home_part, home_logsum, fetched, in_hbm(out_weight))
    swap = [(place, place ^ 1) for place in range(TP)]
    other = lax.ppermute(terms, "tp", swap)
    mine, attention = pl.pallas_call(
        own_kernel,
        out_shape=(
            pltpu.VMEM((CHIPS, ROWS, WIDTH), F32),
            jax.ShapeDtypeStruct((STEPS, REQUESTS, HEADS * HEAD_SIZE), BF16),
        ),
        in_specs=[VMEM_SPEC] * 2,
        out_specs=(VMEM_SPEC, VMEM_SPEC),
        compiler_params=pltpu.CompilerParams(vmem_limit_bytes=16 * 2**20),
        cost_estimate=pl.CostEstimate(flops=10**8, bytes_accessed=4 * 10**6, transcendentals=0),
        name="own",
    )(merged, own_weight)
    sums = pl.pallas_call(
        pair_kernel,
        out_shape=[pltpu.VMEM((ROWS, WIDTH), F32)] + [pltpu.VMEM((ROWS, WIDTH), BF16)] * 3,
        in_specs=[VMEM_SPEC] * 2,
        out_specs=[VMEM_SPEC] * CHIPS,
        compiler_params=pltpu.CompilerParams(vmem_limit_bytes=4 * 2**20),
        name="pair",
    )(mine, other)
    arrived = []
    for ahead in (2, 1, 3):
        shift = [(place, (place + CORES * ahead) % TP) for place in range(TP)]
        arrived.append(lax.ppermute(sums[ahead], "tp", shift))
    projected = pl.pallas_call(
        total_kernel,
        out_shape=jax.ShapeDtypeStruct((ROWS, WIDTH), BF16),
        in_specs=[VMEM_SPEC] * CHIPS,
        out_specs=VMEM_SPEC,
        compiler_params=pltpu.CompilerParams(vmem_limit_bytes=4 * 2**20),
        name="total",
    )(sums[0], *arrived)
    return (attention.transpose(1, 0, 2), projected.reshape(STEPS, REQUESTS, -1).transpose(1, 0, 2))


def solution(mesh):
    return jax.shard_map(
        local,
        mesh=mesh,
        in_specs=(
            P("inst", None, "tp"),
            P("inst", None, None, "tp"),
            P("inst", None, None, "tp"),
            P("inst"),
            P("inst", None),
            P("inst", None),
            P("inst", None),
            P("tp", None),
        ),
        out_specs=(P("inst", None, "tp"), P("inst", None, "tp")),
        check_vma=False,
    )
```

```python
import functools
import math

import jax
import jax.numpy as jnp
from jax import lax
from jax.experimental import pallas as pl
from jax.experimental.pallas import tpu as pltpu
from jax.sharding import PartitionSpec as P

HEAD_SIZE = 128
MOST_BLOCKS = 3
STEPS = 3
HEADS = 8
REQUESTS = 8
ENTRIES = 5
INSTANCES = 32
SLOTS = 2
BLOCK_TOKENS = 64
SPAN = MOST_BLOCKS * BLOCK_TOKENS
ROWS = STEPS * HEADS
LENT = REQUESTS * (ENTRIES - 1)
TP = 8
CORES = 2
POOL = 120
POOL_PIECE = 60
CHIPS = TP // CORES
WIDTH = 512
FETCHED = 2
META = SLOTS * STEPS
SCALE = 1.0 / math.sqrt(HEAD_SIZE)
F32 = jnp.float32
BF16 = jnp.bfloat16
VMEM_SPEC = pl.BlockSpec(memory_space=pltpu.VMEM)
HBM_SPEC = pl.BlockSpec(memory_space=pltpu.HBM)


def in_hbm(array):
    return pltpu.with_memory_space_constraint(array, pltpu.HBM)


def lanes_of(shape):
    return lax.broadcasted_iota(jnp.int32, shape, len(shape) - 1)


def clear_counts(count_ref):
    for index in range(INSTANCES):
        count_ref[index] = 0


def next_rank(count_ref, lender):
    rank = count_ref[lender]
    count_ref[lender] = rank + 1
    return rank


def live_of(ctx_ref, blocks_ref, request, entry, earlier):
    blocks = blocks_ref[request, entry]
    live = jnp.clip(ctx_ref[request] - BLOCK_TOKENS * earlier, 0, BLOCK_TOKENS * blocks)
    return live, earlier + blocks


def start_copies(sources, targets, sems):
    copies = [pltpu.make_async_copy(*pair, sems.at[index]) for index, pair in enumerate(zip(sources, targets))]
    for copy in copies:
        copy.start()
    return copies


def pack_kernel(
    ctx_hbm, lender_hbm, blocks_hbm, slot_hbm, q_hbm, pool_hbm,
    send_ref, rows_ref, keys_ref,
    ctx_ref, lender_ref, blocks_ref, slot_ref, q_ref, regroup, count_ref, sems, keys_sem
):
    copies = start_copies(
        (q_hbm, ctx_hbm, lender_hbm, blocks_hbm, slot_hbm), (q_ref, ctx_ref, lender_ref, blocks_ref, slot_ref), sems
    )
    all_keys = pltpu.make_async_copy(pool_hbm.at[:, 0], keys_ref, keys_sem)
    all_keys.start()
    send_ref[:, META, :, :] = jnp.zeros((INSTANCES, 8, HEAD_SIZE), BF16)
    clear_counts(count_ref)
    for copy in copies:
        copy.wait()
    for step in range(STEPS):
        for head in range(HEADS):
            tile = q_ref[step, :, head * HEAD_SIZE : (head + 1) * HEAD_SIZE].astype(F32)
            regroup[pl.ds(step * HEADS + head, REQUESTS, stride=ROWS), :] = tile
    lane = lanes_of((8, HEAD_SIZE)) - 2 * SLOTS * lax.axis_index("inst")
    first_row = lax.broadcasted_iota(jnp.int32, (8, HEAD_SIZE), 0) == 0
    for request in range(REQUESTS):
        rows = regroup[request * ROWS : (request + 1) * ROWS, :].astype(BF16)
        rows_ref[request] = rows
        tiles = regroup[request * ROWS : (request + 1) * ROWS, :].reshape(STEPS, HEADS, HEAD_SIZE).astype(BF16)
        earlier = blocks_ref[request, 0]
        for entry in range(1, ENTRIES):
            lender = lender_ref[request, entry]
            rank = next_rank(count_ref, lender)
            live, earlier = live_of(ctx_ref, blocks_ref, request, entry, earlier)
            send_ref[lender, pl.ds(rank * STEPS, STEPS), :, :] = tiles
            meta = send_ref[lender, META].astype(F32)
            meta = jnp.where(first_row & (lane == 2 * rank), slot_ref[request, entry].astype(F32), meta)
            meta = jnp.where(first_row & (lane == 2 * rank + 1), live.astype(F32), meta)
            send_ref[lender, META] = meta.astype(BF16)
    all_keys.wait()


def weight_columns(weight_hbm, other_core, ahead):
    place = lax.axis_index("tp")
    core = lax.rem(place + other_core, CORES)
    part = lax.rem(place // CORES + ahead, CHIPS) * CORES + core
    return weight_hbm.at[:, pl.ds(pl.multiple_of(part * WIDTH, WIDTH), WIDTH)]


def scores_of(query, keys):
    return lax.dot_general(query, keys, (((1,), (1,)), ((), ())), preferred_element_type=F32) * SCALE


def home_kernel(
    ctx_hbm, blocks_hbm, slot_hbm, fresh_hbm, pool_hbm, weight_hbm, rows_ref, token_ref,
    part_ref, logsum_ref, fetched_ref,
    ctx_ref, blocks_ref, slot_ref, fresh_ref, pool_ref, sems, pool_sems, weight_sems
):
    copies = start_copies(
        (ctx_hbm, blocks_hbm, slot_hbm, fresh_hbm), (ctx_ref, blocks_ref, slot_ref, fresh_ref), sems
    )
    for copy in copies:
        copy.wait()
    copies = start_copies(
        [pool_hbm.at[pl.ds(slot_ref[request, 0], MOST_BLOCKS)] for request in range(REQUESTS)],
        [pool_ref.at[request] for request in range(REQUESTS)],
        pool_sems,
    )
    weights = start_copies(
        [weight_columns(weight_hbm, 1, ahead) for ahead in range(FETCHED)],
        [fetched_ref.at[ahead] for ahead in range(FETCHED)],
        weight_sems,
    )
    token = lanes_of((ROWS, SPAN))
    fresh_token = lanes_of((ROWS, STEPS))
    step_of_row = lax.broadcasted_iota(jnp.int32, (ROWS, STEPS), 0) // HEADS
    fresh_seen = fresh_token <= step_of_row
    cached, fresh, values, fresh_values = [], [], [], []
    for request in range(REQUESTS):
        live, _ = live_of(ctx_ref, blocks_ref, request, 0, 0)
        copies[request].wait()
        query = rows_ref[request]
        keys = pool_ref[request, :, 0].reshape(SPAN, HEAD_SIZE)
        values.append(pool_ref[request, :, 1].reshape(SPAN, HEAD_SIZE))
        fresh_values.append(fresh_ref[request, :, 1, :].astype(F32))
        cached.append(jnp.where(token < live, scores_of(query, keys), -1e30))
        fresh.append(jnp.where(fresh_seen, scores_of(query, fresh_ref[request, :, 0, :]), -1e30))
    for request in range(REQUESTS):
        top = jnp.maximum(
            jnp.max(cached[request], axis=1, keepdims=True), jnp.max(fresh[request], axis=1, keepdims=True)
        )
        cached_expits = jnp.exp(cached[request] - top)
        fresh_expits = jnp.exp(fresh[request] - top)
        totals = jnp.sum(cached_expits, axis=1, keepdims=True) + jnp.sum(fresh_expits, axis=1, keepdims=True)
        out = jnp.dot(cached_expits.astype(BF16), values[request], preferred_element_type=F32)
        rounded = fresh_expits.astype(BF16).astype(F32)
        for index in range(STEPS):
            out = out + rounded[:, index : index + 1] * fresh_values[request][index : index + 1, :]
        part_ref[request] = (out / totals).astype(BF16)
        logsum_ref[request] = jnp.broadcast_to(top + jnp.log(totals), (ROWS, HEAD_SIZE))
    for copy in weights:
        copy.wait()


def lent_kernel(
    got_ref, keys_ref, pool_hbm, back_ref, token_ref, values_ref, meta_vector, meta_ref, item_ref, sem, pool_sems
):
    pieces = [pl.ds(piece * POOL_PIECE, POOL_PIECE) for piece in range(POOL // POOL_PIECE)]
    copies = start_copies(
        [pool_hbm.at[piece, 1] for piece in pieces], [values_ref.at[piece] for piece in pieces], pool_sems
    )
    token_ref[...] = jnp.zeros_like(token_ref)
    meta_vector[...] = jnp.sum(got_ref[:, META].astype(F32), axis=0).astype(jnp.int32)
    copy = pltpu.make_async_copy(meta_vector, meta_ref, sem)
    copy.start()
    back_ref[:, META, :, :] = jnp.zeros((INSTANCES, 8, HEAD_SIZE), BF16)
    copy.wait()

    def compact(index, found):
        live = meta_ref[0, 2 * index + 1]
        item_ref[found] = index
        return found + (live > 0).astype(jnp.int32)

    lax.fori_loop(0, INSTANCES * SLOTS, compact, 0, unroll=INSTANCES * SLOTS)
    token = lanes_of((ROWS, SPAN))
    lane = lanes_of((8, HEAD_SIZE))
    items = [item_ref[member] for member in range(LENT)]
    source = [item // SLOTS for item in items]
    rank = [item % SLOTS for item in items]
    scores = []
    for member in range(LENT):
        slot = meta_ref[0, 2 * items[member]]
        live = meta_ref[0, 2 * items[member] + 1]
        query = got_ref[source[member], pl.ds(rank[member] * STEPS, STEPS)]
        query = query.astype(F32).reshape(ROWS, HEAD_SIZE).astype(BF16)
        keys = keys_ref[pl.ds(slot, MOST_BLOCKS)].reshape(SPAN, HEAD_SIZE)
        scores.append(jnp.where(token < live, scores_of(query, keys), -1e30))
    for copy in copies:
        copy.wait()
    parts, logsums = [], []
    for member in range(LENT):
        slot = meta_ref[0, 2 * items[member]]
        values = values_ref[pl.ds(slot, MOST_BLOCKS)].reshape(SPAN, HEAD_SIZE)
        top = jnp.max(scores[member], axis=1, keepdims=True)
        expits = jnp.exp(scores[member] - top)
        totals = jnp.sum(expits, axis=1, keepdims=True)
        out = jnp.dot(expits.astype(BF16), values, preferred_element_type=F32)
        parts.append(out / totals)
        logsums.append(jnp.broadcast_to(top + jnp.log(totals), (ROWS, HEAD_SIZE)))
    for member in range(LENT):
        back_ref[source[member], pl.ds(rank[member] * STEPS, STEPS)] = (
            parts[member].reshape(STEPS, HEADS, HEAD_SIZE).astype(BF16)
        )
        high = logsums[member].astype(BF16).astype(F32)
        middle = (logsums[member] - high).astype(BF16).astype(F32)
        low = logsums[member] - high - middle
        at = lane - 9 * rank[member]
        block = back_ref[source[member], META].astype(F32)
        for step in range(STEPS):
            for place, piece in enumerate((high, middle, low)):
                block = jnp.where(at == 3 * step + place, piece[step * HEADS : (step + 1) * HEADS], block)
        back_ref[source[member], META] = block.astype(BF16)


def merge_kernel(
    lender_hbm, back_ref, part_ref, logsum_ref, fetched_ref, weight_hbm,
    attention_ref, terms_ref, own_ref,
    merged, count_ref, lender_ref, rest_ref, sem, rest_sems, own_sems
):
    copy = pltpu.make_async_copy(lender_hbm, lender_ref, sem)
    copy.start()
    rest = start_copies(
        [weight_columns(weight_hbm, 1, ahead) for ahead in range(FETCHED, CHIPS)],
        [rest_ref.at[ahead - FETCHED] for ahead in range(FETCHED, CHIPS)],
        rest_sems,
    )
    own = start_copies(
        [weight_columns(weight_hbm, 0, ahead) for ahead in range(CHIPS)],
        [own_ref.at[ahead] for ahead in range(CHIPS)],
        own_sems,
    )
    clear_counts(count_ref)
    copy.wait()
    lane = lanes_of((8, HEAD_SIZE))
    for request in range(REQUESTS):
        logsums = [logsum_ref[request]]
        parts = [part_ref[request].astype(F32)]
        for entry in range(1, ENTRIES):
            lender = lender_ref[request, entry]
            rank = next_rank(count_ref, lender)
            parts.append(
                back_ref[lender, pl.ds(rank * STEPS, STEPS)].astype(F32).reshape(ROWS, HEAD_SIZE)
            )
            block = back_ref[lender, META].astype(F32)
            at = lane - 9 * rank
            columns = []
            for step in range(STEPS):
                mine = (at >= 3 * step) & (at < 3 * step + 3)
                columns.append(
                    jnp.broadcast_to(
                        jnp.sum(jnp.where(mine, block, 0.0), axis=1, keepdims=True), (HEADS, HEAD_SIZE)
                    )
                )
            logsums.append(jnp.concatenate(columns, axis=0))
        highest = functools.reduce(jnp.maximum, logsums)
        weights = [jnp.exp(logsum - highest) for logsum in logsums]
        total = functools.reduce(jnp.add, weights)
        blended = functools.reduce(jnp.add, [weight * part for weight, part in zip(weights, parts)])
        merged[request * ROWS : (request + 1) * ROWS, :] = blended / total
    for step in range(STEPS):
        for head in range(HEADS):
            tile = merged[pl.ds(step * HEADS + head, REQUESTS, stride=ROWS), :]
            attention_ref[step * REQUESTS : (step + 1) * REQUESTS, head * HEAD_SIZE : (head + 1) * HEAD_SIZE] = tile
    attention = attention_ref[...].astype(BF16)
    for ahead in range(CHIPS):
        if ahead >= FETCHED:
            rest[ahead - FETCHED].wait()
        weight = fetched_ref[ahead] if ahead < FETCHED else rest_ref[ahead - FETCHED]
        terms_ref[ahead] = jnp.dot(attention, weight, preferred_element_type=F32).astype(BF16)
    for copy in own:
        copy.wait()


def own_kernel(attention_ref, weight_ref, terms_ref, out_ref):
    out_ref[...] = attention_ref[...].reshape(STEPS, REQUESTS, HEADS * HEAD_SIZE).astype(BF16)
    attention = attention_ref[...].astype(BF16)
    for ahead in range(CHIPS):
        terms_ref[ahead] = jnp.dot(attention, weight_ref[ahead], preferred_element_type=F32)


def pair_kernel(mine_ref, other_ref, *sum_refs):
    for ahead, sum_ref in enumerate(sum_refs):
        sum_ref[...] = (mine_ref[ahead] + other_ref[ahead].astype(F32)).astype(sum_ref.dtype)


def total_kernel(own_ref, *refs):
    total = own_ref[...]
    for ref in refs[:-1]:
        total = total + ref[...].astype(F32)
    refs[-1][...] = total.astype(BF16)


def local(
    queries, new_kv, key_value_pool, ctx_len, entry_lender, entry_blocks, entry_slot, out_weight
):
    message = pltpu.VMEM((INSTANCES, META + 1, 8, HEAD_SIZE), BF16)
    rows = pltpu.VMEM((REQUESTS, ROWS, HEAD_SIZE), BF16)
    weight_space = lambda count: pltpu.VMEM((count, HEADS * HEAD_SIZE, WIDTH), BF16)
    ctx_space = pltpu.SMEM((REQUESTS,), jnp.int32)
    entry_space = pltpu.SMEM((REQUESTS, ENTRIES), jnp.int32)
    pool_half = pltpu.VMEM((POOL, BLOCK_TOKENS, HEAD_SIZE), BF16)
    send, query_rows, keys = pl.pallas_call(
        pack_kernel,
        out_shape=(message, rows, pool_half),
        in_specs=[HBM_SPEC] * 6,
        out_specs=(VMEM_SPEC,) * 3,
        scratch_shapes=[
            ctx_space, entry_space, entry_space, entry_space,
            pltpu.VMEM((STEPS, REQUESTS, HEADS * HEAD_SIZE), BF16),
            pltpu.VMEM((REQUESTS * ROWS, HEAD_SIZE), F32),
            pltpu.SMEM((INSTANCES,), jnp.int32),
            pltpu.SemaphoreType.DMA((5,)),
            pltpu.SemaphoreType.DMA(()),
        ],
        compiler_params=pltpu.CompilerParams(vmem_limit_bytes=8 * 2**20),
        name="pack",
    )(*map(in_hbm, (ctx_len, entry_lender, entry_blocks, entry_slot, queries.transpose(1, 0, 2), key_value_pool)))
    got = lax.all_to_all(send, "inst", split_axis=0, concat_axis=0, tiled=True)
    back, token = pl.pallas_call(
        lent_kernel,
        out_shape=(message, pltpu.VMEM((8, HEAD_SIZE), F32)),
        in_specs=[VMEM_SPEC, VMEM_SPEC, HBM_SPEC],
        out_specs=(VMEM_SPEC, VMEM_SPEC),
        scratch_shapes=[
            pool_half,
            pltpu.VMEM((8, HEAD_SIZE), jnp.int32),
            pltpu.SMEM((8, HEAD_SIZE), jnp.int32),
            pltpu.SMEM((INSTANCES * SLOTS + 1,), jnp.int32),
            pltpu.SemaphoreType.DMA(()),
            pltpu.SemaphoreType.DMA((POOL // POOL_PIECE,)),
        ],
        compiler_params=pltpu.CompilerParams(vmem_limit_bytes=12 * 2**20),
        name="lent",
    )(got, keys, in_hbm(key_value_pool))
    back = lax.all_to_all(back, "inst", split_axis=0, concat_axis=0, tiled=True)
    home_part, home_logsum, fetched = pl.pallas_call(
        home_kernel,
        out_shape=(
            rows,
            pltpu.VMEM((REQUESTS, ROWS, HEAD_SIZE), F32),
            weight_space(FETCHED),
        ),
        in_specs=[HBM_SPEC] * 6 + [VMEM_SPEC] * 2,
        out_specs=(VMEM_SPEC,) * 3,
        scratch_shapes=[
            ctx_space, entry_space, entry_space,
            pltpu.VMEM((REQUESTS, STEPS, 2, HEAD_SIZE), BF16),
            pltpu.VMEM((REQUESTS, MOST_BLOCKS, 2, BLOCK_TOKENS, HEAD_SIZE), BF16),
            pltpu.SemaphoreType.DMA((4,)),
            pltpu.SemaphoreType.DMA((REQUESTS,)),
            pltpu.SemaphoreType.DMA((FETCHED,)),
        ],
        compiler_params=pltpu.CompilerParams(vmem_limit_bytes=8 * 2**20),
        cost_estimate=pl.CostEstimate(flops=10**8, bytes_accessed=12 * 10**6, transcendentals=0),
        name="home",
    )(
        *map(in_hbm, (ctx_len, entry_blocks, entry_slot, new_kv.transpose(0, 2, 1, 3), key_value_pool, out_weight)),
        query_rows,
        token,
    )
    merged, terms, own_weight = pl.pallas_call(
        merge_kernel,
        out_shape=(
            pltpu.VMEM((ROWS, HEADS * HEAD_SIZE), F32),
            pltpu.VMEM((CHIPS, ROWS, WIDTH), BF16),
            weight_space(CHIPS),
        ),
        in_specs=[HBM_SPEC] + [VMEM_SPEC] * 4 + [HBM_SPEC],
        out_specs=(VMEM_SPEC,) * 3,
        scratch_shapes=[
            pltpu.VMEM((REQUESTS * ROWS, HEAD_SIZE), F32),
            pltpu.SMEM((INSTANCES,), jnp.int32),
            entry_space,
            weight_space(CHIPS - FETCHED),
            pltpu.SemaphoreType.DMA(()),
            pltpu.SemaphoreType.DMA((CHIPS - FETCHED,)),
            pltpu.SemaphoreType.DMA((CHIPS,)),
        ],
        compiler_params=pltpu.CompilerParams(vmem_limit_bytes=16 * 2**20),
        name="merge",
    )(in_hbm(entry_lender), back, home_part, home_logsum, fetched, in_hbm(out_weight))
    swap = [(place, place ^ 1) for place in range(TP)]
    other = lax.ppermute(terms, "tp", swap)
    mine, attention = pl.pallas_call(
        own_kernel,
        out_shape=(
            pltpu.VMEM((CHIPS, ROWS, WIDTH), F32),
            jax.ShapeDtypeStruct((STEPS, REQUESTS, HEADS * HEAD_SIZE), BF16),
        ),
        in_specs=[VMEM_SPEC] * 2,
        out_specs=(VMEM_SPEC, VMEM_SPEC),
        compiler_params=pltpu.CompilerParams(vmem_limit_bytes=16 * 2**20),
        cost_estimate=pl.CostEstimate(flops=10**8, bytes_accessed=4 * 10**6, transcendentals=0),
        name="own",
    )(merged, own_weight)
    sums = pl.pallas_call(
        pair_kernel,
        out_shape=[pltpu.VMEM((ROWS, WIDTH), F32)] + [pltpu.VMEM((ROWS, WIDTH), BF16)] * 3,
        in_specs=[VMEM_SPEC] * 2,
        out_specs=[VMEM_SPEC] * CHIPS,
        compiler_params=pltpu.CompilerParams(vmem_limit_bytes=4 * 2**20),
        name="pair",
    )(mine, other)
    arrived = []
    for ahead in (2, 1, 3):
        shift = [(place, (place + CORES * ahead) % TP) for place in range(TP)]
        arrived.append(lax.ppermute(sums[ahead], "tp", shift))
    projected = pl.pallas_call(
        total_kernel,
        out_shape=jax.ShapeDtypeStruct((ROWS, WIDTH), BF16),
        in_specs=[VMEM_SPEC] * CHIPS,
        out_specs=VMEM_SPEC,
        compiler_params=pltpu.CompilerParams(vmem_limit_bytes=4 * 2**20),
        name="total",
    )(sums[0], *arrived)
    return (attention.transpose(1, 0, 2), projected.reshape(STEPS, REQUESTS, -1).transpose(1, 0, 2))


def solution(mesh):
    return jax.shard_map(
        local,
        mesh=mesh,
        in_specs=(
            P("inst", None, "tp"),
            P("inst", None, None, "tp"),
            P("inst", None, None, "tp"),
            P("inst"),
            P("inst", None),
            P("inst", None),
            P("inst", None),
            P("tp", None),
        ),
        out_specs=(P("inst", None, "tp"), P("inst", None, "tp")),
        check_vma=False,
    )
```

```python
import functools
import math

import jax
import jax.numpy as jnp
from jax import lax
from jax.experimental import pallas as pl
from jax.experimental.pallas import tpu as pltpu
from jax.sharding import PartitionSpec as P

HEAD_SIZE = 128
MOST_BLOCKS = 3
STEPS = 3
HEADS = 8
REQUESTS = 8
ENTRIES = 5
INSTANCES = 32
SLOTS = 2
BLOCK_TOKENS = 64
SPAN = MOST_BLOCKS * BLOCK_TOKENS
ROWS = STEPS * HEADS
LENT = REQUESTS * (ENTRIES - 1)
TP = 8
CORES = 2
POOL = 120
POOL_PIECE = 60
CHIPS = TP // CORES
WIDTH = 512
FETCHED = 2
META = SLOTS * STEPS
SCALE = 1.0 / math.sqrt(HEAD_SIZE)
F32 = jnp.float32
BF16 = jnp.bfloat16
VMEM_SPEC = pl.BlockSpec(memory_space=pltpu.VMEM)
HBM_SPEC = pl.BlockSpec(memory_space=pltpu.HBM)


def in_hbm(array):
    return pltpu.with_memory_space_constraint(array, pltpu.HBM)


def lanes_of(shape):
    return lax.broadcasted_iota(jnp.int32, shape, len(shape) - 1)


def clear_counts(count_ref):
    for index in range(INSTANCES):
        count_ref[index] = 0


def next_rank(count_ref, lender):
    rank = count_ref[lender]
    count_ref[lender] = rank + 1
    return rank


def live_of(ctx_ref, blocks_ref, request, entry, earlier):
    blocks = blocks_ref[request, entry]
    live = jnp.clip(ctx_ref[request] - BLOCK_TOKENS * earlier, 0, BLOCK_TOKENS * blocks)
    return live, earlier + blocks


def start_copies(sources, targets, sems):
    copies = [pltpu.make_async_copy(*pair, sems.at[index]) for index, pair in enumerate(zip(sources, targets))]
    for copy in copies:
        copy.start()
    return copies


def pack_kernel(
    ctx_hbm, lender_hbm, blocks_hbm, slot_hbm, q_hbm, pool_hbm,
    send_ref, rows_ref, keys_ref,
    ctx_ref, lender_ref, blocks_ref, slot_ref, q_ref, regroup, count_ref, sems, keys_sem
):
    copies = start_copies(
        (q_hbm, ctx_hbm, lender_hbm, blocks_hbm, slot_hbm), (q_ref, ctx_ref, lender_ref, blocks_ref, slot_ref), sems
    )
    all_keys = pltpu.make_async_copy(pool_hbm.at[:, 0], keys_ref, keys_sem)
    all_keys.start()
    send_ref[:, META, :, :] = jnp.zeros((INSTANCES, 8, HEAD_SIZE), BF16)
    clear_counts(count_ref)
    for copy in copies:
        copy.wait()
    for step in range(STEPS):
        for head in range(HEADS):
            tile = q_ref[step, :, head * HEAD_SIZE : (head + 1) * HEAD_SIZE].astype(F32)
            regroup[pl.ds(step * HEADS + head, REQUESTS, stride=ROWS), :] = tile
    lane = lanes_of((8, HEAD_SIZE)) - 2 * SLOTS * lax.axis_index("inst")
    first_row = lax.broadcasted_iota(jnp.int32, (8, HEAD_SIZE), 0) == 0
    for request in range(REQUESTS):
        rows = regroup[request * ROWS : (request + 1) * ROWS, :].astype(BF16)
        rows_ref[request] = rows
        tiles = regroup[request * ROWS : (request + 1) * ROWS, :].reshape(STEPS, HEADS, HEAD_SIZE).astype(BF16)
        earlier = blocks_ref[request, 0]
        for entry in range(1, ENTRIES):
            lender = lender_ref[request, entry]
            rank = next_rank(count_ref, lender)
            live, earlier = live_of(ctx_ref, blocks_ref, request, entry, earlier)
            send_ref[lender, pl.ds(rank * STEPS, STEPS), :, :] = tiles
            meta = send_ref[lender, META].astype(F32)
            meta = jnp.where(first_row & (lane == 2 * rank), slot_ref[request, entry].astype(F32), meta)
            meta = jnp.where(first_row & (lane == 2 * rank + 1), live.astype(F32), meta)
            send_ref[lender, META] = meta.astype(BF16)
    all_keys.wait()


def weight_columns(weight_hbm, other_core, ahead):
    place = lax.axis_index("tp")
    core = lax.rem(place + other_core, CORES)
    part = lax.bitwise_xor(place // CORES, ahead) * CORES + core
    return weight_hbm.at[:, pl.ds(pl.multiple_of(part * WIDTH, WIDTH), WIDTH)]


def scores_of(query, keys):
    return lax.dot_general(query, keys, (((1,), (1,)), ((), ())), preferred_element_type=F32) * SCALE


def home_kernel(
    ctx_hbm, blocks_hbm, slot_hbm, fresh_hbm, pool_hbm, weight_hbm, rows_ref, token_ref,
    part_ref, logsum_ref, fetched_ref,
    ctx_ref, blocks_ref, slot_ref, fresh_ref, pool_ref, sems, pool_sems, weight_sems
):
    copies = start_copies(
        (ctx_hbm, blocks_hbm, slot_hbm, fresh_hbm), (ctx_ref, blocks_ref, slot_ref, fresh_ref), sems
    )
    for copy in copies:
        copy.wait()
    copies = start_copies(
        [pool_hbm.at[pl.ds(slot_ref[request, 0], MOST_BLOCKS)] for request in range(REQUESTS)],
        [pool_ref.at[request] for request in range(REQUESTS)],
        pool_sems,
    )
    weights = start_copies(
        [weight_columns(weight_hbm, 1, ahead) for ahead in range(FETCHED)],
        [fetched_ref.at[ahead] for ahead in range(FETCHED)],
        weight_sems,
    )
    token = lanes_of((ROWS, SPAN))
    fresh_token = lanes_of((ROWS, STEPS))
    step_of_row = lax.broadcasted_iota(jnp.int32, (ROWS, STEPS), 0) // HEADS
    fresh_seen = fresh_token <= step_of_row
    cached, fresh, values, fresh_values = [], [], [], []
    for request in range(REQUESTS):
        live, _ = live_of(ctx_ref, blocks_ref, request, 0, 0)
        copies[request].wait()
        query = rows_ref[request]
        keys = pool_ref[request, :, 0].reshape(SPAN, HEAD_SIZE)
        values.append(pool_ref[request, :, 1].reshape(SPAN, HEAD_SIZE))
        fresh_values.append(fresh_ref[request, :, 1, :].astype(F32))
        cached.append(jnp.where(token < live, scores_of(query, keys), -1e30))
        fresh.append(jnp.where(fresh_seen, scores_of(query, fresh_ref[request, :, 0, :]), -1e30))
    for request in range(REQUESTS):
        top = jnp.maximum(
            jnp.max(cached[request], axis=1, keepdims=True), jnp.max(fresh[request], axis=1, keepdims=True)
        )
        cached_expits = jnp.exp(cached[request] - top)
        fresh_expits = jnp.exp(fresh[request] - top)
        totals = jnp.sum(cached_expits, axis=1, keepdims=True) + jnp.sum(fresh_expits, axis=1, keepdims=True)
        out = jnp.dot(cached_expits.astype(BF16), values[request], preferred_element_type=F32)
        rounded = fresh_expits.astype(BF16).astype(F32)
        for index in range(STEPS):
            out = out + rounded[:, index : index + 1] * fresh_values[request][index : index + 1, :]
        part_ref[request] = (out / totals).astype(BF16)
        logsum_ref[request] = jnp.broadcast_to(top + jnp.log(totals), (ROWS, HEAD_SIZE))
    for copy in weights:
        copy.wait()


def lent_kernel(
    got_ref, keys_ref, pool_hbm, back_ref, token_ref, values_ref, meta_vector, meta_ref, item_ref, sem, pool_sems
):
    pieces = [pl.ds(piece * POOL_PIECE, POOL_PIECE) for piece in range(POOL // POOL_PIECE)]
    copies = start_copies(
        [pool_hbm.at[piece, 1] for piece in pieces], [values_ref.at[piece] for piece in pieces], pool_sems
    )
    token_ref[...] = jnp.zeros_like(token_ref)
    meta_vector[...] = jnp.sum(got_ref[:, META].astype(F32), axis=0).astype(jnp.int32)
    copy = pltpu.make_async_copy(meta_vector, meta_ref, sem)
    copy.start()
    back_ref[:, META, :, :] = jnp.zeros((INSTANCES, 8, HEAD_SIZE), BF16)
    copy.wait()

    def compact(index, found):
        live = meta_ref[0, 2 * index + 1]
        item_ref[found] = index
        return found + (live > 0).astype(jnp.int32)

    lax.fori_loop(0, INSTANCES * SLOTS, compact, 0, unroll=INSTANCES * SLOTS)
    token = lanes_of((ROWS, SPAN))
    lane = lanes_of((8, HEAD_SIZE))
    items = [item_ref[member] for member in range(LENT)]
    source = [item // SLOTS for item in items]
    rank = [item % SLOTS for item in items]
    scores = []
    for member in range(LENT):
        slot = meta_ref[0, 2 * items[member]]
        live = meta_ref[0, 2 * items[member] + 1]
        query = got_ref[source[member], pl.ds(rank[member] * STEPS, STEPS)]
        query = query.astype(F32).reshape(ROWS, HEAD_SIZE).astype(BF16)
        keys = keys_ref[pl.ds(slot, MOST_BLOCKS)].reshape(SPAN, HEAD_SIZE)
        scores.append(jnp.where(token < live, scores_of(query, keys), -1e30))
    for copy in copies:
        copy.wait()
    parts, logsums = [], []
    for member in range(LENT):
        slot = meta_ref[0, 2 * items[member]]
        values = values_ref[pl.ds(slot, MOST_BLOCKS)].reshape(SPAN, HEAD_SIZE)
        top = jnp.max(scores[member], axis=1, keepdims=True)
        expits = jnp.exp(scores[member] - top)
        totals = jnp.sum(expits, axis=1, keepdims=True)
        out = jnp.dot(expits.astype(BF16), values, preferred_element_type=F32)
        parts.append(out / totals)
        logsums.append(jnp.broadcast_to(top + jnp.log(totals), (ROWS, HEAD_SIZE)))
    for member in range(LENT):
        back_ref[source[member], pl.ds(rank[member] * STEPS, STEPS)] = (
            parts[member].reshape(STEPS, HEADS, HEAD_SIZE).astype(BF16)
        )
        high = logsums[member].astype(BF16).astype(F32)
        middle = (logsums[member] - high).astype(BF16).astype(F32)
        low = logsums[member] - high - middle
        at = lane - 9 * rank[member]
        block = back_ref[source[member], META].astype(F32)
        for step in range(STEPS):
            for place, piece in enumerate((high, middle, low)):
                block = jnp.where(at == 3 * step + place, piece[step * HEADS : (step + 1) * HEADS], block)
        back_ref[source[member], META] = block.astype(BF16)


def merge_kernel(
    lender_hbm, back_ref, part_ref, logsum_ref, fetched_ref, weight_hbm,
    attention_ref, terms_ref, own_ref,
    merged, count_ref, lender_ref, rest_ref, sem, rest_sems, own_sems
):
    copy = pltpu.make_async_copy(lender_hbm, lender_ref, sem)
    copy.start()
    rest = start_copies(
        [weight_columns(weight_hbm, 1, ahead) for ahead in range(FETCHED, CHIPS)],
        [rest_ref.at[ahead - FETCHED] for ahead in range(FETCHED, CHIPS)],
        rest_sems,
    )
    own = start_copies(
        [weight_columns(weight_hbm, 0, ahead) for ahead in range(CHIPS)],
        [own_ref.at[ahead] for ahead in range(CHIPS)],
        own_sems,
    )
    clear_counts(count_ref)
    copy.wait()
    lane = lanes_of((8, HEAD_SIZE))
    for request in range(REQUESTS):
        logsums = [logsum_ref[request]]
        parts = [part_ref[request].astype(F32)]
        for entry in range(1, ENTRIES):
            lender = lender_ref[request, entry]
            rank = next_rank(count_ref, lender)
            parts.append(
                back_ref[lender, pl.ds(rank * STEPS, STEPS)].astype(F32).reshape(ROWS, HEAD_SIZE)
            )
            block = back_ref[lender, META].astype(F32)
            at = lane - 9 * rank
            columns = []
            for step in range(STEPS):
                mine = (at >= 3 * step) & (at < 3 * step + 3)
                columns.append(
                    jnp.broadcast_to(
                        jnp.sum(jnp.where(mine, block, 0.0), axis=1, keepdims=True), (HEADS, HEAD_SIZE)
                    )
                )
            logsums.append(jnp.concatenate(columns, axis=0))
        highest = functools.reduce(jnp.maximum, logsums)
        weights = [jnp.exp(logsum - highest) for logsum in logsums]
        total = functools.reduce(jnp.add, weights)
        blended = functools.reduce(jnp.add, [weight * part for weight, part in zip(weights, parts)])
        merged[request * ROWS : (request + 1) * ROWS, :] = blended / total
    for step in range(STEPS):
        for head in range(HEADS):
            tile = merged[pl.ds(step * HEADS + head, REQUESTS, stride=ROWS), :]
            attention_ref[step * REQUESTS : (step + 1) * REQUESTS, head * HEAD_SIZE : (head + 1) * HEAD_SIZE] = tile
    attention = attention_ref[...].astype(BF16)
    for ahead in range(CHIPS):
        if ahead >= FETCHED:
            rest[ahead - FETCHED].wait()
        weight = fetched_ref[ahead] if ahead < FETCHED else rest_ref[ahead - FETCHED]
        terms_ref[ahead] = jnp.dot(attention, weight, preferred_element_type=F32).astype(BF16)
    for copy in own:
        copy.wait()


def own_kernel(attention_ref, weight_ref, terms_ref):
    attention = attention_ref[...].astype(BF16)
    for ahead in range(CHIPS):
        terms_ref[ahead] = jnp.dot(attention, weight_ref[ahead], preferred_element_type=F32)


def pair_kernel(mine_ref, other_ref, *sum_refs):
    for ahead, sum_ref in enumerate(sum_refs):
        sum_ref[...] = (mine_ref[ahead] + other_ref[ahead].astype(F32)).astype(sum_ref.dtype)


def total_kernel(merged_ref, own_ref, *refs):
    attention_ref, projected_ref = refs[-2:]
    attention_ref[...] = merged_ref[...].reshape(STEPS, REQUESTS, HEADS * HEAD_SIZE).astype(BF16)
    total = own_ref[...]
    for ref in refs[:-2]:
        total = total + ref[...].astype(F32)
    projected_ref[...] = total.astype(BF16)


def local(
    queries, new_kv, key_value_pool, ctx_len, entry_lender, entry_blocks, entry_slot, out_weight
):
    message = pltpu.VMEM((INSTANCES, META + 1, 8, HEAD_SIZE), BF16)
    rows = pltpu.VMEM((REQUESTS, ROWS, HEAD_SIZE), BF16)
    weight_space = lambda count: pltpu.VMEM((count, HEADS * HEAD_SIZE, WIDTH), BF16)
    ctx_space = pltpu.SMEM((REQUESTS,), jnp.int32)
    entry_space = pltpu.SMEM((REQUESTS, ENTRIES), jnp.int32)
    pool_half = pltpu.VMEM((POOL, BLOCK_TOKENS, HEAD_SIZE), BF16)
    send, query_rows, keys = pl.pallas_call(
        pack_kernel,
        out_shape=(message, rows, pool_half),
        in_specs=[HBM_SPEC] * 6,
        out_specs=(VMEM_SPEC,) * 3,
        scratch_shapes=[
            ctx_space, entry_space, entry_space, entry_space,
            pltpu.VMEM((STEPS, REQUESTS, HEADS * HEAD_SIZE), BF16),
            pltpu.VMEM((REQUESTS * ROWS, HEAD_SIZE), F32),
            pltpu.SMEM((INSTANCES,), jnp.int32),
            pltpu.SemaphoreType.DMA((5,)),
            pltpu.SemaphoreType.DMA(()),
        ],
        compiler_params=pltpu.CompilerParams(vmem_limit_bytes=8 * 2**20),
        name="pack",
    )(*map(in_hbm, (ctx_len, entry_lender, entry_blocks, entry_slot, queries.transpose(1, 0, 2), key_value_pool)))
    got = lax.all_to_all(send, "inst", split_axis=0, concat_axis=0, tiled=True)
    back, token = pl.pallas_call(
        lent_kernel,
        out_shape=(message, pltpu.VMEM((8, HEAD_SIZE), F32)),
        in_specs=[VMEM_SPEC, VMEM_SPEC, HBM_SPEC],
        out_specs=(VMEM_SPEC, VMEM_SPEC),
        scratch_shapes=[
            pool_half,
            pltpu.VMEM((8, HEAD_SIZE), jnp.int32),
            pltpu.SMEM((8, HEAD_SIZE), jnp.int32),
            pltpu.SMEM((INSTANCES * SLOTS + 1,), jnp.int32),
            pltpu.SemaphoreType.DMA(()),
            pltpu.SemaphoreType.DMA((POOL // POOL_PIECE,)),
        ],
        compiler_params=pltpu.CompilerParams(vmem_limit_bytes=12 * 2**20),
        name="lent",
    )(got, keys, in_hbm(key_value_pool))
    back = lax.all_to_all(back, "inst", split_axis=0, concat_axis=0, tiled=True)
    home_part, home_logsum, fetched = pl.pallas_call(
        home_kernel,
        out_shape=(
            rows,
            pltpu.VMEM((REQUESTS, ROWS, HEAD_SIZE), F32),
            weight_space(FETCHED),
        ),
        in_specs=[HBM_SPEC] * 6 + [VMEM_SPEC] * 2,
        out_specs=(VMEM_SPEC,) * 3,
        scratch_shapes=[
            ctx_space, entry_space, entry_space,
            pltpu.VMEM((REQUESTS, STEPS, 2, HEAD_SIZE), BF16),
            pltpu.VMEM((REQUESTS, MOST_BLOCKS, 2, BLOCK_TOKENS, HEAD_SIZE), BF16),
            pltpu.SemaphoreType.DMA((4,)),
            pltpu.SemaphoreType.DMA((REQUESTS,)),
            pltpu.SemaphoreType.DMA((FETCHED,)),
        ],
        compiler_params=pltpu.CompilerParams(vmem_limit_bytes=8 * 2**20),
        cost_estimate=pl.CostEstimate(flops=10**8, bytes_accessed=12 * 10**6, transcendentals=0),
        name="home",
    )(
        *map(in_hbm, (ctx_len, entry_blocks, entry_slot, new_kv.transpose(0, 2, 1, 3), key_value_pool, out_weight)),
        query_rows,
        token,
    )
    merged, terms, own_weight = pl.pallas_call(
        merge_kernel,
        out_shape=(
            pltpu.VMEM((ROWS, HEADS * HEAD_SIZE), F32),
            pltpu.VMEM((CHIPS, ROWS, WIDTH), BF16),
            weight_space(CHIPS),
        ),
        in_specs=[HBM_SPEC] + [VMEM_SPEC] * 4 + [HBM_SPEC],
        out_specs=(VMEM_SPEC,) * 3,
        scratch_shapes=[
            pltpu.VMEM((REQUESTS * ROWS, HEAD_SIZE), F32),
            pltpu.SMEM((INSTANCES,), jnp.int32),
            entry_space,
            weight_space(CHIPS - FETCHED),
            pltpu.SemaphoreType.DMA(()),
            pltpu.SemaphoreType.DMA((CHIPS - FETCHED,)),
            pltpu.SemaphoreType.DMA((CHIPS,)),
        ],
        compiler_params=pltpu.CompilerParams(vmem_limit_bytes=16 * 2**20),
        name="merge",
    )(in_hbm(entry_lender), back, home_part, home_logsum, fetched, in_hbm(out_weight))
    swap = [(place, place ^ 1) for place in range(TP)]
    other = lax.ppermute(terms, "tp", swap)
    mine = pl.pallas_call(
        own_kernel,
        out_shape=pltpu.VMEM((CHIPS, ROWS, WIDTH), F32),
        in_specs=[VMEM_SPEC] * 2,
        out_specs=VMEM_SPEC,
        compiler_params=pltpu.CompilerParams(vmem_limit_bytes=16 * 2**20),
        cost_estimate=pl.CostEstimate(flops=10**8, bytes_accessed=4 * 10**6, transcendentals=0),
        name="own",
    )(merged, own_weight)
    sums = pl.pallas_call(
        pair_kernel,
        out_shape=[pltpu.VMEM((ROWS, WIDTH), F32)] + [pltpu.VMEM((ROWS, WIDTH), BF16)] * 3,
        in_specs=[VMEM_SPEC] * 2,
        out_specs=[VMEM_SPEC] * CHIPS,
        compiler_params=pltpu.CompilerParams(vmem_limit_bytes=4 * 2**20),
        name="pair",
    )(mine, other)
    arrived = []
    for ahead in (3, 2, 1):
        swap = [(place, place ^ (CORES * ahead)) for place in range(TP)]
        arrived.append(lax.ppermute(sums[ahead], "tp", swap))
    attention, projected = pl.pallas_call(
        total_kernel,
        out_shape=(
            jax.ShapeDtypeStruct((STEPS, REQUESTS, HEADS * HEAD_SIZE), BF16),
            jax.ShapeDtypeStruct((ROWS, WIDTH), BF16),
        ),
        in_specs=[VMEM_SPEC] * (CHIPS + 1),
        out_specs=(VMEM_SPEC, VMEM_SPEC),
        compiler_params=pltpu.CompilerParams(vmem_limit_bytes=4 * 2**20),
        name="total",
    )(merged, sums[0], *arrived)
    return (attention.transpose(1, 0, 2), projected.reshape(STEPS, REQUESTS, -1).transpose(1, 0, 2))


def solution(mesh):
    return jax.shard_map(
        local,
        mesh=mesh,
        in_specs=(
            P("inst", None, "tp"),
            P("inst", None, None, "tp"),
            P("inst", None, None, "tp"),
            P("inst"),
            P("inst", None),
            P("inst", None),
            P("inst", None),
            P("tp", None),
        ),
        out_specs=(P("inst", None, "tp"), P("inst", None, "tp")),
        check_vma=False,
    )
```

```python
import functools
import math

import jax
import jax.numpy as jnp
from jax import lax
from jax.experimental import pallas as pl
from jax.experimental.pallas import tpu as pltpu
from jax.sharding import PartitionSpec as P

HEAD_SIZE = 128
MOST_BLOCKS = 3
STEPS = 3
HEADS = 8
REQUESTS = 8
ENTRIES = 5
INSTANCES = 32
SLOTS = 2
BLOCK_TOKENS = 64
SPAN = MOST_BLOCKS * BLOCK_TOKENS
ROWS = STEPS * HEADS
LENT = REQUESTS * (ENTRIES - 1)
TP = 8
CORES = 2
POOL = 120
POOL_PIECE = 60
CHIPS = TP // CORES
WIDTH = 512
FETCHED = 2
META = SLOTS * ROWS
MESSAGE_ROWS = META + 2
SCALE = 1.0 / math.sqrt(HEAD_SIZE)
F32 = jnp.float32
BF16 = jnp.bfloat16
VMEM_SPEC = pl.BlockSpec(memory_space=pltpu.VMEM)
HBM_SPEC = pl.BlockSpec(memory_space=pltpu.HBM)


def in_hbm(array):
    return pltpu.with_memory_space_constraint(array, pltpu.HBM)


def lanes_of(shape):
    return lax.broadcasted_iota(jnp.int32, shape, len(shape) - 1)


def by_rows(message_ref):
    return message_ref.reshape(INSTANCES, MESSAGE_ROWS, HEAD_SIZE)


def slot_rows(rank):
    return pl.ds(pl.multiple_of(rank * ROWS, ROWS), ROWS)


def rows_of(shape):
    return lax.broadcasted_iota(jnp.int32, shape, 0)


def clear_counts(count_ref):
    for index in range(INSTANCES):
        count_ref[index] = 0


def next_rank(count_ref, lender):
    rank = count_ref[lender]
    count_ref[lender] = rank + 1
    return rank


def live_of(ctx_ref, blocks_ref, request, entry, earlier):
    blocks = blocks_ref[request, entry]
    live = jnp.clip(ctx_ref[request] - BLOCK_TOKENS * earlier, 0, BLOCK_TOKENS * blocks)
    return live, earlier + blocks


def start_copies(sources, targets, sems):
    copies = [pltpu.make_async_copy(*pair, sems.at[index]) for index, pair in enumerate(zip(sources, targets))]
    for copy in copies:
        copy.start()
    return copies


def pack_kernel(
    ctx_hbm, lender_hbm, blocks_hbm, slot_hbm, q_hbm, pool_hbm,
    send_ref, rows_ref, keys_ref,
    ctx_ref, lender_ref, blocks_ref, slot_ref, q_ref, regroup, count_ref, sems, keys_sem
):
    copies = start_copies(
        (q_hbm, ctx_hbm, lender_hbm, blocks_hbm, slot_hbm), (q_ref, ctx_ref, lender_ref, blocks_ref, slot_ref), sems
    )
    all_keys = pltpu.make_async_copy(pool_hbm.at[:, 0], keys_ref, keys_sem)
    all_keys.start()
    send_ref = by_rows(send_ref)
    send_ref[:, META:, :] = jnp.zeros((INSTANCES, 2, HEAD_SIZE), BF16)
    clear_counts(count_ref)
    for copy in copies:
        copy.wait()
    for step in range(STEPS):
        for head in range(HEADS):
            tile = q_ref[step, :, head * HEAD_SIZE : (head + 1) * HEAD_SIZE].astype(F32)
            regroup[pl.ds(step * HEADS + head, REQUESTS, stride=ROWS), :] = tile
    lane = lanes_of((2, HEAD_SIZE)) - 2 * SLOTS * lax.axis_index("inst")
    first_row = rows_of((2, HEAD_SIZE)) == 0
    for request in range(REQUESTS):
        rows = regroup[request * ROWS : (request + 1) * ROWS, :].astype(BF16)
        rows_ref[request] = rows
        earlier = blocks_ref[request, 0]
        for entry in range(1, ENTRIES):
            lender = lender_ref[request, entry]
            rank = next_rank(count_ref, lender)
            live, earlier = live_of(ctx_ref, blocks_ref, request, entry, earlier)
            send_ref[lender, slot_rows(rank), :] = rows
            meta = send_ref[lender, META:, :].astype(F32)
            meta = jnp.where(first_row & (lane == 2 * rank), slot_ref[request, entry].astype(F32), meta)
            meta = jnp.where(first_row & (lane == 2 * rank + 1), live.astype(F32), meta)
            send_ref[lender, META:, :] = meta.astype(BF16)
    all_keys.wait()


def weight_columns(weight_hbm, other_core, ahead):
    place = lax.axis_index("tp")
    core = lax.rem(place + other_core, CORES)
    part = lax.bitwise_xor(place // CORES, ahead) * CORES + core
    return weight_hbm.at[:, pl.ds(pl.multiple_of(part * WIDTH, WIDTH), WIDTH)]


def scores_of(query, keys):
    return lax.dot_general(query, keys, (((1,), (1,)), ((), ())), preferred_element_type=F32) * SCALE


def home_kernel(
    ctx_hbm, blocks_hbm, slot_hbm, fresh_hbm, pool_hbm, weight_hbm, rows_ref, token_ref,
    part_ref, logsum_ref, fetched_ref,
    ctx_ref, blocks_ref, slot_ref, fresh_ref, pool_ref, sems, pool_sems, weight_sems
):
    copies = start_copies(
        (ctx_hbm, blocks_hbm, slot_hbm, fresh_hbm), (ctx_ref, blocks_ref, slot_ref, fresh_ref), sems
    )
    for copy in copies:
        copy.wait()
    copies = start_copies(
        [pool_hbm.at[pl.ds(slot_ref[request, 0], MOST_BLOCKS)] for request in range(REQUESTS)],
        [pool_ref.at[request] for request in range(REQUESTS)],
        pool_sems,
    )
    weights = start_copies(
        [weight_columns(weight_hbm, 1, ahead) for ahead in range(FETCHED)],
        [fetched_ref.at[ahead] for ahead in range(FETCHED)],
        weight_sems,
    )
    token = lanes_of((ROWS, SPAN))
    fresh_token = lanes_of((ROWS, STEPS))
    step_of_row = lax.broadcasted_iota(jnp.int32, (ROWS, STEPS), 0) // HEADS
    fresh_seen = fresh_token <= step_of_row
    cached, fresh, values, fresh_values = [], [], [], []
    for request in range(REQUESTS):
        live, _ = live_of(ctx_ref, blocks_ref, request, 0, 0)
        copies[request].wait()
        query = rows_ref[request]
        keys = pool_ref[request, :, 0].reshape(SPAN, HEAD_SIZE)
        values.append(pool_ref[request, :, 1].reshape(SPAN, HEAD_SIZE))
        fresh_values.append(fresh_ref[request, :, 1, :].astype(F32))
        cached.append(jnp.where(token < live, scores_of(query, keys), -1e30))
        fresh.append(jnp.where(fresh_seen, scores_of(query, fresh_ref[request, :, 0, :]), -1e30))
    for request in range(REQUESTS):
        top = jnp.maximum(
            jnp.max(cached[request], axis=1, keepdims=True), jnp.max(fresh[request], axis=1, keepdims=True)
        )
        cached_expits = jnp.exp(cached[request] - top)
        fresh_expits = jnp.exp(fresh[request] - top)
        totals = jnp.sum(cached_expits, axis=1, keepdims=True) + jnp.sum(fresh_expits, axis=1, keepdims=True)
        out = jnp.dot(cached_expits.astype(BF16), values[request], preferred_element_type=F32)
        rounded = fresh_expits.astype(BF16).astype(F32)
        for index in range(STEPS):
            out = out + rounded[:, index : index + 1] * fresh_values[request][index : index + 1, :]
        part_ref[request] = (out / totals).astype(BF16)
        logsum_ref[request] = jnp.broadcast_to(top + jnp.log(totals), (ROWS, HEAD_SIZE))
    for copy in weights:
        copy.wait()


def lent_kernel(
    got_ref, keys_ref, pool_hbm, back_ref, token_ref, values_ref, meta_vector, meta_ref, item_ref, sem, pool_sems
):
    pieces = [pl.ds(piece * POOL_PIECE, POOL_PIECE) for piece in range(POOL // POOL_PIECE)]
    copies = start_copies(
        [pool_hbm.at[piece, 1] for piece in pieces], [values_ref.at[piece] for piece in pieces], pool_sems
    )
    token_ref[...] = jnp.zeros_like(token_ref)
    got_ref, back_ref = by_rows(got_ref), by_rows(back_ref)
    meta_vector[...] = jnp.sum(got_ref[:, META:, :].astype(F32), axis=0).astype(jnp.int32)
    copy = pltpu.make_async_copy(meta_vector, meta_ref, sem)
    copy.start()
    back_ref[:, META:, :] = jnp.zeros((INSTANCES, 2, HEAD_SIZE), BF16)
    copy.wait()

    def compact(index, found):
        live = meta_ref[0, 2 * index + 1]
        item_ref[found] = index
        return found + (live > 0).astype(jnp.int32)

    lax.fori_loop(0, INSTANCES * SLOTS, compact, 0, unroll=INSTANCES * SLOTS)
    token = lanes_of((ROWS, SPAN))
    place = lanes_of((ROWS, HEAD_SIZE)) - rows_of((ROWS, HEAD_SIZE))
    slot_row = rows_of((SLOTS, HEAD_SIZE))
    items = [item_ref[member] for member in range(LENT)]
    source = [item // SLOTS for item in items]
    rank = [item % SLOTS for item in items]
    scores = []
    for member in range(LENT):
        slot = meta_ref[0, 2 * items[member]]
        live = meta_ref[0, 2 * items[member] + 1]
        query = got_ref[source[member], slot_rows(rank[member]), :]
        keys = keys_ref[pl.ds(slot, MOST_BLOCKS)].reshape(SPAN, HEAD_SIZE)
        scores.append(jnp.where(token < live, scores_of(query, keys), -1e30))
    for copy in copies:
        copy.wait()
    parts, logsums = [], []
    for member in range(LENT):
        slot = meta_ref[0, 2 * items[member]]
        values = values_ref[pl.ds(slot, MOST_BLOCKS)].reshape(SPAN, HEAD_SIZE)
        top = jnp.max(scores[member], axis=1, keepdims=True)
        expits = jnp.exp(scores[member] - top)
        totals = jnp.sum(expits, axis=1, keepdims=True)
        out = jnp.dot(expits.astype(BF16), values, preferred_element_type=F32)
        parts.append(out / totals)
        logsums.append(jnp.broadcast_to(top + jnp.log(totals), (ROWS, HEAD_SIZE)))
    for member in range(LENT):
        back_ref[source[member], slot_rows(rank[member]), :] = parts[member].astype(BF16)
        high = logsums[member].astype(BF16).astype(F32)
        middle = (logsums[member] - high).astype(BF16).astype(F32)
        low = logsums[member] - high - middle
        spread = jnp.where(place == 0, high, 0.0)
        spread = jnp.where(place == ROWS, middle, spread)
        spread = jnp.where(place == 2 * ROWS, low, spread)
        line = jnp.sum(spread, axis=0, keepdims=True)
        block = back_ref[source[member], META:, :].astype(F32)
        back_ref[source[member], META:, :] = jnp.where(slot_row == rank[member], line, block).astype(BF16)


def merge_kernel(
    lender_hbm, back_ref, part_ref, logsum_ref, fetched_ref, weight_hbm,
    attention_ref, terms_ref, own_ref,
    merged, count_ref, lender_ref, rest_ref, sem, rest_sems, own_sems
):
    copy = pltpu.make_async_copy(lender_hbm, lender_ref, sem)
    copy.start()
    rest = start_copies(
        [weight_columns(weight_hbm, 1, ahead) for ahead in range(FETCHED, CHIPS)],
        [rest_ref.at[ahead - FETCHED] for ahead in range(FETCHED, CHIPS)],
        rest_sems,
    )
    own = start_copies(
        [weight_columns(weight_hbm, 0, ahead) for ahead in range(CHIPS)],
        [own_ref.at[ahead] for ahead in range(CHIPS)],
        own_sems,
    )
    clear_counts(count_ref)
    copy.wait()
    back_ref = by_rows(back_ref)
    place = lanes_of((ROWS, HEAD_SIZE)) - rows_of((ROWS, HEAD_SIZE))
    mine = (place == 0) | (place == ROWS) | (place == 2 * ROWS)
    slot_row = rows_of((SLOTS, HEAD_SIZE))
    for request in range(REQUESTS):
        logsums = [logsum_ref[request]]
        parts = [part_ref[request].astype(F32)]
        for entry in range(1, ENTRIES):
            lender = lender_ref[request, entry]
            rank = next_rank(count_ref, lender)
            parts.append(back_ref[lender, slot_rows(rank), :].astype(F32))
            block = back_ref[lender, META:, :].astype(F32)
            line = jnp.sum(jnp.where(slot_row == rank, block, 0.0), axis=0, keepdims=True)
            logsum = jnp.sum(jnp.where(mine, line, 0.0), axis=1, keepdims=True)
            logsums.append(jnp.broadcast_to(logsum, (ROWS, HEAD_SIZE)))
        highest = functools.reduce(jnp.maximum, logsums)
        weights = [jnp.exp(logsum - highest) for logsum in logsums]
        total = functools.reduce(jnp.add, weights)
        blended = functools.reduce(jnp.add, [weight * part for weight, part in zip(weights, parts)])
        merged[request * ROWS : (request + 1) * ROWS, :] = blended / total
    for step in range(STEPS):
        for head in range(HEADS):
            tile = merged[pl.ds(step * HEADS + head, REQUESTS, stride=ROWS), :]
            attention_ref[step * REQUESTS : (step + 1) * REQUESTS, head * HEAD_SIZE : (head + 1) * HEAD_SIZE] = tile
    attention = attention_ref[...].astype(BF16)
    for ahead in range(CHIPS):
        if ahead >= FETCHED:
            rest[ahead - FETCHED].wait()
        weight = fetched_ref[ahead] if ahead < FETCHED else rest_ref[ahead - FETCHED]
        terms_ref[ahead] = jnp.dot(attention, weight, preferred_element_type=F32).astype(BF16)
    for copy in own:
        copy.wait()


def own_kernel(attention_ref, weight_ref, terms_ref):
    attention = attention_ref[...].astype(BF16)
    for ahead in range(CHIPS):
        terms_ref[ahead] = jnp.dot(attention, weight_ref[ahead], preferred_element_type=F32)


def pair_kernel(mine_ref, other_ref, *sum_refs):
    for ahead, sum_ref in enumerate(sum_refs):
        sum_ref[...] = (mine_ref[ahead] + other_ref[ahead].astype(F32)).astype(sum_ref.dtype)


def total_kernel(merged_ref, own_ref, *refs):
    attention_ref, projected_ref = refs[-2:]
    attention_ref[...] = merged_ref[...].reshape(STEPS, REQUESTS, HEADS * HEAD_SIZE).astype(BF16)
    total = own_ref[...]
    for ref in refs[:-2]:
        total = total + ref[...].astype(F32)
    projected_ref[...] = total.astype(BF16)


def local(
    queries, new_kv, key_value_pool, ctx_len, entry_lender, entry_blocks, entry_slot, out_weight
):
    message = pltpu.VMEM((INSTANCES, MESSAGE_ROWS // 2, 2, HEAD_SIZE), BF16)
    rows = pltpu.VMEM((REQUESTS, ROWS, HEAD_SIZE), BF16)
    weight_space = lambda count: pltpu.VMEM((count, HEADS * HEAD_SIZE, WIDTH), BF16)
    ctx_space = pltpu.SMEM((REQUESTS,), jnp.int32)
    entry_space = pltpu.SMEM((REQUESTS, ENTRIES), jnp.int32)
    pool_half = pltpu.VMEM((POOL, BLOCK_TOKENS, HEAD_SIZE), BF16)
    send, query_rows, keys = pl.pallas_call(
        pack_kernel,
        out_shape=(message, rows, pool_half),
        in_specs=[HBM_SPEC] * 6,
        out_specs=(VMEM_SPEC,) * 3,
        scratch_shapes=[
            ctx_space, entry_space, entry_space, entry_space,
            pltpu.VMEM((STEPS, REQUESTS, HEADS * HEAD_SIZE), BF16),
            pltpu.VMEM((REQUESTS * ROWS, HEAD_SIZE), F32),
            pltpu.SMEM((INSTANCES,), jnp.int32),
            pltpu.SemaphoreType.DMA((5,)),
            pltpu.SemaphoreType.DMA(()),
        ],
        compiler_params=pltpu.CompilerParams(vmem_limit_bytes=8 * 2**20),
        name="pack",
    )(*map(in_hbm, (ctx_len, entry_lender, entry_blocks, entry_slot, queries.transpose(1, 0, 2), key_value_pool)))
    got = lax.all_to_all(send, "inst", split_axis=0, concat_axis=0, tiled=True)
    back, token = pl.pallas_call(
        lent_kernel,
        out_shape=(message, pltpu.VMEM((8, HEAD_SIZE), F32)),
        in_specs=[VMEM_SPEC, VMEM_SPEC, HBM_SPEC],
        out_specs=(VMEM_SPEC, VMEM_SPEC),
        scratch_shapes=[
            pool_half,
            pltpu.VMEM((SLOTS, HEAD_SIZE), jnp.int32),
            pltpu.SMEM((SLOTS, HEAD_SIZE), jnp.int32),
            pltpu.SMEM((INSTANCES * SLOTS + 1,), jnp.int32),
            pltpu.SemaphoreType.DMA(()),
            pltpu.SemaphoreType.DMA((POOL // POOL_PIECE,)),
        ],
        compiler_params=pltpu.CompilerParams(vmem_limit_bytes=12 * 2**20),
        name="lent",
    )(got, keys, in_hbm(key_value_pool))
    back = lax.all_to_all(back, "inst", split_axis=0, concat_axis=0, tiled=True)
    home_part, home_logsum, fetched = pl.pallas_call(
        home_kernel,
        out_shape=(
            rows,
            pltpu.VMEM((REQUESTS, ROWS, HEAD_SIZE), F32),
            weight_space(FETCHED),
        ),
        in_specs=[HBM_SPEC] * 6 + [VMEM_SPEC] * 2,
        out_specs=(VMEM_SPEC,) * 3,
        scratch_shapes=[
            ctx_space, entry_space, entry_space,
            pltpu.VMEM((REQUESTS, STEPS, 2, HEAD_SIZE), BF16),
            pltpu.VMEM((REQUESTS, MOST_BLOCKS, 2, BLOCK_TOKENS, HEAD_SIZE), BF16),
            pltpu.SemaphoreType.DMA((4,)),
            pltpu.SemaphoreType.DMA((REQUESTS,)),
            pltpu.SemaphoreType.DMA((FETCHED,)),
        ],
        compiler_params=pltpu.CompilerParams(vmem_limit_bytes=8 * 2**20),
        cost_estimate=pl.CostEstimate(flops=10**8, bytes_accessed=12 * 10**6, transcendentals=0),
        name="home",
    )(
        *map(in_hbm, (ctx_len, entry_blocks, entry_slot, new_kv.transpose(0, 2, 1, 3), key_value_pool, out_weight)),
        query_rows,
        token,
    )
    merged, terms, own_weight = pl.pallas_call(
        merge_kernel,
        out_shape=(
            pltpu.VMEM((ROWS, HEADS * HEAD_SIZE), F32),
            pltpu.VMEM((CHIPS, ROWS, WIDTH), BF16),
            weight_space(CHIPS),
        ),
        in_specs=[HBM_SPEC] + [VMEM_SPEC] * 4 + [HBM_SPEC],
        out_specs=(VMEM_SPEC,) * 3,
        scratch_shapes=[
            pltpu.VMEM((REQUESTS * ROWS, HEAD_SIZE), F32),
            pltpu.SMEM((INSTANCES,), jnp.int32),
            entry_space,
            weight_space(CHIPS - FETCHED),
            pltpu.SemaphoreType.DMA(()),
            pltpu.SemaphoreType.DMA((CHIPS - FETCHED,)),
            pltpu.SemaphoreType.DMA((CHIPS,)),
        ],
        compiler_params=pltpu.CompilerParams(vmem_limit_bytes=16 * 2**20),
        name="merge",
    )(in_hbm(entry_lender), back, home_part, home_logsum, fetched, in_hbm(out_weight))
    swap = [(place, place ^ 1) for place in range(TP)]
    other = lax.ppermute(terms, "tp", swap)
    mine = pl.pallas_call(
        own_kernel,
        out_shape=pltpu.VMEM((CHIPS, ROWS, WIDTH), F32),
        in_specs=[VMEM_SPEC] * 2,
        out_specs=VMEM_SPEC,
        compiler_params=pltpu.CompilerParams(vmem_limit_bytes=16 * 2**20),
        cost_estimate=pl.CostEstimate(flops=10**8, bytes_accessed=4 * 10**6, transcendentals=0),
        name="own",
    )(merged, own_weight)
    sums = pl.pallas_call(
        pair_kernel,
        out_shape=[pltpu.VMEM((ROWS, WIDTH), F32)] + [pltpu.VMEM((ROWS, WIDTH), BF16)] * 3,
        in_specs=[VMEM_SPEC] * 2,
        out_specs=[VMEM_SPEC] * CHIPS,
        compiler_params=pltpu.CompilerParams(vmem_limit_bytes=4 * 2**20),
        name="pair",
    )(mine, other)
    arrived = []
    for ahead in (3, 2, 1):
        swap = [(place, place ^ (CORES * ahead)) for place in range(TP)]
        arrived.append(lax.ppermute(sums[ahead], "tp", swap))
    attention, projected = pl.pallas_call(
        total_kernel,
        out_shape=(
            jax.ShapeDtypeStruct((STEPS, REQUESTS, HEADS * HEAD_SIZE), BF16),
            jax.ShapeDtypeStruct((ROWS, WIDTH), BF16),
        ),
        in_specs=[VMEM_SPEC] * (CHIPS + 1),
        out_specs=(VMEM_SPEC, VMEM_SPEC),
        compiler_params=pltpu.CompilerParams(vmem_limit_bytes=4 * 2**20),
        name="total",
    )(merged, sums[0], *arrived)
    return (attention.transpose(1, 0, 2), projected.reshape(STEPS, REQUESTS, -1).transpose(1, 0, 2))


def solution(mesh):
    return jax.shard_map(
        local,
        mesh=mesh,
        in_specs=(
            P("inst", None, "tp"),
            P("inst", None, None, "tp"),
            P("inst", None, None, "tp"),
            P("inst"),
            P("inst", None),
            P("inst", None),
            P("inst", None),
            P("tp", None),
        ),
        out_specs=(P("inst", None, "tp"), P("inst", None, "tp")),
        check_vma=False,
    )
```

```python
import functools
import math

import jax
import jax.numpy as jnp
from jax import lax
from jax.experimental import pallas as pl
from jax.experimental.pallas import tpu as pltpu
from jax.sharding import PartitionSpec as P

HEAD_SIZE = 128
MOST_BLOCKS = 3
STEPS = 3
HEADS = 8
REQUESTS = 8
ENTRIES = 5
INSTANCES = 32
SLOTS = 2
BLOCK_TOKENS = 64
SPAN = MOST_BLOCKS * BLOCK_TOKENS
ROWS = STEPS * HEADS
LENT = REQUESTS * (ENTRIES - 1)
TP = 8
CORES = 2
POOL = 120
POOL_PIECE = 60
CHIPS = TP // CORES
WIDTH = 512
DEPTH = 1024
FETCHED = 2816
META = SLOTS * ROWS
MESSAGE_ROWS = META + 2
SCALE = 1.0 / math.sqrt(HEAD_SIZE)
F32 = jnp.float32
BF16 = jnp.bfloat16
VMEM_SPEC = pl.BlockSpec(memory_space=pltpu.VMEM)
HBM_SPEC = pl.BlockSpec(memory_space=pltpu.HBM)


def in_hbm(array):
    return pltpu.with_memory_space_constraint(array, pltpu.HBM)


def lanes_of(shape):
    return lax.broadcasted_iota(jnp.int32, shape, len(shape) - 1)


def by_rows(message_ref):
    return message_ref.reshape(INSTANCES, MESSAGE_ROWS, HEAD_SIZE)


def slot_rows(rank):
    return pl.ds(pl.multiple_of(rank * ROWS, ROWS), ROWS)


def rows_of(shape):
    return lax.broadcasted_iota(jnp.int32, shape, 0)


def clear_counts(count_ref):
    for index in range(INSTANCES):
        count_ref[index] = 0


def next_rank(count_ref, lender):
    rank = count_ref[lender]
    count_ref[lender] = rank + 1
    return rank


def live_of(ctx_ref, blocks_ref, request, entry, earlier):
    blocks = blocks_ref[request, entry]
    live = jnp.clip(ctx_ref[request] - BLOCK_TOKENS * earlier, 0, BLOCK_TOKENS * blocks)
    return live, earlier + blocks


def start_copies(sources, targets, sems):
    copies = [pltpu.make_async_copy(*pair, sems.at[index]) for index, pair in enumerate(zip(sources, targets))]
    for copy in copies:
        copy.start()
    return copies


def pack_kernel(
    ctx_hbm, lender_hbm, blocks_hbm, slot_hbm, q_hbm, pool_hbm,
    send_ref, rows_ref, keys_ref,
    ctx_ref, lender_ref, blocks_ref, slot_ref, q_ref, regroup, count_ref, sems, keys_sem
):
    copies = start_copies(
        (q_hbm, ctx_hbm, lender_hbm, blocks_hbm, slot_hbm), (q_ref, ctx_ref, lender_ref, blocks_ref, slot_ref), sems
    )
    all_keys = pltpu.make_async_copy(pool_hbm.at[:, 0], keys_ref, keys_sem)
    all_keys.start()
    send_ref = by_rows(send_ref)
    send_ref[:, META:, :] = jnp.zeros((INSTANCES, 2, HEAD_SIZE), BF16)
    clear_counts(count_ref)
    for copy in copies:
        copy.wait()
    for step in range(STEPS):
        for head in range(HEADS):
            tile = q_ref[step, :, head * HEAD_SIZE : (head + 1) * HEAD_SIZE].astype(F32)
            regroup[pl.ds(step * HEADS + head, REQUESTS, stride=ROWS), :] = tile
    lane = lanes_of((2, HEAD_SIZE)) - 2 * SLOTS * lax.axis_index("inst")
    first_row = rows_of((2, HEAD_SIZE)) == 0
    for request in range(REQUESTS):
        rows = regroup[request * ROWS : (request + 1) * ROWS, :].astype(BF16)
        rows_ref[request] = rows
        earlier = blocks_ref[request, 0]
        for entry in range(1, ENTRIES):
            lender = lender_ref[request, entry]
            rank = next_rank(count_ref, lender)
            live, earlier = live_of(ctx_ref, blocks_ref, request, entry, earlier)
            send_ref[lender, slot_rows(rank), :] = rows
            meta = send_ref[lender, META:, :].astype(F32)
            meta = jnp.where(first_row & (lane == 2 * rank), slot_ref[request, entry].astype(F32), meta)
            meta = jnp.where(first_row & (lane == 2 * rank + 1), live.astype(F32), meta)
            send_ref[lender, META:, :] = meta.astype(BF16)
    all_keys.wait()


def weight_block(weight_hbm, other_core, ahead, rows):
    place = lax.axis_index("tp")
    core = lax.rem(place + other_core, CORES)
    part = lax.bitwise_xor(place // CORES, ahead) * CORES + core
    return weight_hbm.at[rows, pl.ds(pl.multiple_of(part * WIDTH, WIDTH), WIDTH)]


def start_stack(weight_hbm, target, first, last, sems):
    sources, targets = [], []
    for ahead in range(CHIPS):
        low, high = max(first, ahead * DEPTH), min(last, (ahead + 1) * DEPTH)
        if low < high:
            sources.append(weight_block(weight_hbm, 1, ahead, pl.ds(low - ahead * DEPTH, high - low)))
            targets.append(target.at[pl.ds(low - first, high - low)])
    return start_copies(sources, targets, sems)


def scores_of(query, keys):
    return lax.dot_general(query, keys, (((1,), (1,)), ((), ())), preferred_element_type=F32) * SCALE


def home_kernel(
    ctx_hbm, blocks_hbm, slot_hbm, fresh_hbm, pool_hbm, weight_hbm, rows_ref, token_ref,
    part_ref, logsum_ref, fetched_ref,
    ctx_ref, blocks_ref, slot_ref, fresh_ref, pool_ref, sems, pool_sems, weight_sems
):
    copies = start_copies(
        (ctx_hbm, blocks_hbm, slot_hbm, fresh_hbm), (ctx_ref, blocks_ref, slot_ref, fresh_ref), sems
    )
    for copy in copies:
        copy.wait()
    copies = start_copies(
        [pool_hbm.at[pl.ds(slot_ref[request, 0], MOST_BLOCKS)] for request in range(REQUESTS)],
        [pool_ref.at[request] for request in range(REQUESTS)],
        pool_sems,
    )
    weights = start_stack(weight_hbm, fetched_ref, 0, FETCHED, weight_sems)
    token = lanes_of((ROWS, SPAN))
    place = lanes_of((ROWS, HEAD_SIZE)) - rows_of((ROWS, HEAD_SIZE))
    fresh_token = lanes_of((ROWS, STEPS))
    step_of_row = lax.broadcasted_iota(jnp.int32, (ROWS, STEPS), 0) // HEADS
    fresh_seen = fresh_token <= step_of_row
    cached, fresh, values, fresh_values = [], [], [], []
    for request in range(REQUESTS):
        live, _ = live_of(ctx_ref, blocks_ref, request, 0, 0)
        copies[request].wait()
        query = rows_ref[request]
        keys = pool_ref[request, :, 0].reshape(SPAN, HEAD_SIZE)
        values.append(pool_ref[request, :, 1].reshape(SPAN, HEAD_SIZE))
        fresh_values.append(fresh_ref[request, :, 1, :].astype(F32))
        cached.append(jnp.where(token < live, scores_of(query, keys), -1e30))
        fresh.append(jnp.where(fresh_seen, scores_of(query, fresh_ref[request, :, 0, :]), -1e30))
    for request in range(REQUESTS):
        top = jnp.maximum(
            jnp.max(cached[request], axis=1, keepdims=True), jnp.max(fresh[request], axis=1, keepdims=True)
        )
        cached_expits = jnp.exp(cached[request] - top)
        fresh_expits = jnp.exp(fresh[request] - top)
        totals = jnp.sum(cached_expits, axis=1, keepdims=True) + jnp.sum(fresh_expits, axis=1, keepdims=True)
        out = jnp.dot(cached_expits.astype(BF16), values[request], preferred_element_type=F32)
        rounded = fresh_expits.astype(BF16).astype(F32)
        for index in range(STEPS):
            out = out + rounded[:, index : index + 1] * fresh_values[request][index : index + 1, :]
        part_ref[request] = (out / totals).astype(BF16)
        logsum = jnp.broadcast_to(top + jnp.log(totals), (ROWS, HEAD_SIZE))
        logsum_ref[request : request + 1, :] = jnp.sum(jnp.where(place == 0, logsum, 0.0), axis=0, keepdims=True)
    for copy in weights:
        copy.wait()


def lent_kernel(
    got_ref, keys_ref, pool_hbm, back_ref, token_ref, values_ref, meta_vector, meta_ref, item_ref, sem, pool_sems
):
    pieces = [pl.ds(piece * POOL_PIECE, POOL_PIECE) for piece in range(POOL // POOL_PIECE)]
    copies = start_copies(
        [pool_hbm.at[piece, 1] for piece in pieces], [values_ref.at[piece] for piece in pieces], pool_sems
    )
    token_ref[...] = jnp.zeros_like(token_ref)
    got_ref, back_ref = by_rows(got_ref), by_rows(back_ref)
    meta_vector[...] = jnp.sum(got_ref[:, META:, :].astype(F32), axis=0).astype(jnp.int32)
    copy = pltpu.make_async_copy(meta_vector, meta_ref, sem)
    copy.start()
    back_ref[:, META:, :] = jnp.zeros((INSTANCES, 2, HEAD_SIZE), BF16)
    copy.wait()

    def compact(index, found):
        live = meta_ref[0, 2 * index + 1]
        item_ref[found] = index
        return found + (live > 0).astype(jnp.int32)

    lax.fori_loop(0, INSTANCES * SLOTS, compact, 0, unroll=INSTANCES * SLOTS)
    token = lanes_of((2 * ROWS, SPAN))
    first = rows_of((2 * ROWS, SPAN)) < ROWS
    place = lanes_of((ROWS, HEAD_SIZE)) - rows_of((ROWS, HEAD_SIZE))
    slot_row = rows_of((SLOTS, HEAD_SIZE))
    items = [item_ref[member] for member in range(LENT)]
    source = [item // SLOTS for item in items]
    rank = [item % SLOTS for item in items]
    slots = [meta_ref[0, 2 * item] for item in items]
    empty = jnp.zeros((ROWS, HEAD_SIZE), F32)

    def span_of(ref, slot):
        return ref[pl.ds(slot, MOST_BLOCKS)].reshape(SPAN, HEAD_SIZE)

    scores = []
    for left in range(0, LENT, 2):
        pair = (left, left + 1)
        queries = [got_ref[source[member], slot_rows(rank[member]), :].astype(F32) for member in pair]
        queries = jnp.concatenate(
            [jnp.concatenate([queries[0], empty], axis=1), jnp.concatenate([empty, queries[1]], axis=1)], axis=0
        )
        keys = jnp.concatenate([span_of(keys_ref, slots[member]) for member in pair], axis=1)
        live = [meta_ref[0, 2 * items[member] + 1] for member in pair]
        live = jnp.where(first, live[0], live[1])
        scores.append(jnp.where(token < live, scores_of(queries.astype(BF16), keys), -1e30))
    for copy in copies:
        copy.wait()
    parts, logsums = [], []
    for left in range(0, LENT, 2):
        values = jnp.concatenate([span_of(values_ref, slots[member]) for member in (left, left + 1)], axis=1)
        top = jnp.max(scores[left // 2], axis=1, keepdims=True)
        expits = jnp.exp(scores[left // 2] - top)
        totals = jnp.sum(expits, axis=1, keepdims=True)
        out = jnp.dot(expits.astype(BF16), values, preferred_element_type=F32)
        logsum = jnp.broadcast_to(top + jnp.log(totals), (2 * ROWS, HEAD_SIZE))
        for half in range(2):
            rows = slice(half * ROWS, (half + 1) * ROWS)
            parts.append(out[rows, half * HEAD_SIZE : (half + 1) * HEAD_SIZE] / totals[rows])
            logsums.append(logsum[rows])
    for member in range(LENT):
        back_ref[source[member], slot_rows(rank[member]), :] = parts[member].astype(BF16)
        high = logsums[member].astype(BF16).astype(F32)
        middle = (logsums[member] - high).astype(BF16).astype(F32)
        low = logsums[member] - high - middle
        spread = jnp.where(place == 0, high, 0.0)
        spread = jnp.where(place == ROWS, middle, spread)
        spread = jnp.where(place == 2 * ROWS, low, spread)
        line = jnp.sum(spread, axis=0, keepdims=True)
        block = back_ref[source[member], META:, :].astype(F32)
        back_ref[source[member], META:, :] = jnp.where(slot_row == rank[member], line, block).astype(BF16)


def merge_kernel(
    lender_hbm, back_ref, part_ref, logsum_ref, fetched_ref, weight_hbm,
    attention_ref, terms_ref, own_ref,
    merged, count_ref, lender_ref, rest_ref, sem, rest_sems, own_sems
):
    copy = pltpu.make_async_copy(lender_hbm, lender_ref, sem)
    copy.start()
    rest = start_stack(weight_hbm, rest_ref, FETCHED, CHIPS * DEPTH, rest_sems)
    own = start_copies(
        [weight_block(weight_hbm, 0, ahead, pl.ds(0, DEPTH)) for ahead in range(CHIPS)],
        [own_ref.at[ahead] for ahead in range(CHIPS)],
        own_sems,
    )
    clear_counts(count_ref)
    copy.wait()
    back_ref = by_rows(back_ref)
    place = lanes_of((ROWS, HEAD_SIZE)) - rows_of((ROWS, HEAD_SIZE))
    mine = (place == 0) | (place == ROWS) | (place == 2 * ROWS)
    slot_row = rows_of((SLOTS, HEAD_SIZE))
    for request in range(REQUESTS):
        logsum = jnp.where(place == 0, logsum_ref[request : request + 1, :], 0.0)
        logsums = [jnp.broadcast_to(jnp.sum(logsum, axis=1, keepdims=True), (ROWS, HEAD_SIZE))]
        parts = [part_ref[request].astype(F32)]
        for entry in range(1, ENTRIES):
            lender = lender_ref[request, entry]
            rank = next_rank(count_ref, lender)
            parts.append(back_ref[lender, slot_rows(rank), :].astype(F32))
            block = back_ref[lender, META:, :].astype(F32)
            line = jnp.sum(jnp.where(slot_row == rank, block, 0.0), axis=0, keepdims=True)
            logsum = jnp.sum(jnp.where(mine, line, 0.0), axis=1, keepdims=True)
            logsums.append(jnp.broadcast_to(logsum, (ROWS, HEAD_SIZE)))
        highest = functools.reduce(jnp.maximum, logsums)
        weights = [jnp.exp(logsum - highest) for logsum in logsums]
        total = functools.reduce(jnp.add, weights)
        blended = functools.reduce(jnp.add, [weight * part for weight, part in zip(weights, parts)])
        merged[request * ROWS : (request + 1) * ROWS, :] = blended / total
    for step in range(STEPS):
        for head in range(HEADS):
            tile = merged[pl.ds(step * HEADS + head, REQUESTS, stride=ROWS), :]
            attention_ref[step * REQUESTS : (step + 1) * REQUESTS, head * HEAD_SIZE : (head + 1) * HEAD_SIZE] = tile
    attention = attention_ref[...].astype(BF16)
    waiting = list(rest)
    for ahead in range(CHIPS):
        early = min(max(FETCHED - ahead * DEPTH, 0), DEPTH)
        terms = jnp.zeros((ROWS, WIDTH), F32)
        if early:
            block = fetched_ref[ahead * DEPTH : ahead * DEPTH + early, :]
            terms += jnp.dot(attention[:, :early], block, preferred_element_type=F32)
        if early < DEPTH:
            waiting.pop(0).wait()
            block = rest_ref[ahead * DEPTH + early - FETCHED : (ahead + 1) * DEPTH - FETCHED, :]
            terms += jnp.dot(attention[:, early:], block, preferred_element_type=F32)
        terms_ref[ahead] = terms.astype(BF16)
    for copy in own:
        copy.wait()


def own_kernel(attention_ref, weight_ref, terms_ref):
    attention = attention_ref[...].astype(BF16)
    for ahead in range(CHIPS):
        terms_ref[ahead] = jnp.dot(attention, weight_ref[ahead], preferred_element_type=F32)


def pair_kernel(mine_ref, other_ref, *sum_refs):
    for ahead, sum_ref in enumerate(sum_refs):
        sum_ref[...] = (mine_ref[ahead] + other_ref[ahead].astype(F32)).astype(sum_ref.dtype)


def total_kernel(merged_ref, own_ref, *refs):
    attention_ref, projected_ref = refs[-2:]
    attention_ref[...] = merged_ref[...].reshape(STEPS, REQUESTS, HEADS * HEAD_SIZE).astype(BF16)
    total = own_ref[...]
    for ref in refs[:-2]:
        total = total + ref[...].astype(F32)
    projected_ref[...] = total.astype(BF16)


def local(
    queries, new_kv, key_value_pool, ctx_len, entry_lender, entry_blocks, entry_slot, out_weight
):
    message = pltpu.VMEM((INSTANCES, MESSAGE_ROWS // 2, 2, HEAD_SIZE), BF16)
    rows = pltpu.VMEM((REQUESTS, ROWS, HEAD_SIZE), BF16)
    weight_space = lambda count: pltpu.VMEM((count, WIDTH), BF16)
    ctx_space = pltpu.SMEM((REQUESTS,), jnp.int32)
    entry_space = pltpu.SMEM((REQUESTS, ENTRIES), jnp.int32)
    pool_half = pltpu.VMEM((POOL, BLOCK_TOKENS, HEAD_SIZE), BF16)
    send, query_rows, keys = pl.pallas_call(
        pack_kernel,
        out_shape=(message, rows, pool_half),
        in_specs=[HBM_SPEC] * 6,
        out_specs=(VMEM_SPEC,) * 3,
        scratch_shapes=[
            ctx_space, entry_space, entry_space, entry_space,
            pltpu.VMEM((STEPS, REQUESTS, HEADS * HEAD_SIZE), BF16),
            pltpu.VMEM((REQUESTS * ROWS, HEAD_SIZE), F32),
            pltpu.SMEM((INSTANCES,), jnp.int32),
            pltpu.SemaphoreType.DMA((5,)),
            pltpu.SemaphoreType.DMA(()),
        ],
        compiler_params=pltpu.CompilerParams(vmem_limit_bytes=8 * 2**20),
        name="pack",
    )(*map(in_hbm, (ctx_len, entry_lender, entry_blocks, entry_slot, queries.transpose(1, 0, 2), key_value_pool)))
    got = lax.all_to_all(send, "inst", split_axis=0, concat_axis=0, tiled=True)
    back, token = pl.pallas_call(
        lent_kernel,
        out_shape=(message, pltpu.VMEM((8, HEAD_SIZE), F32)),
        in_specs=[VMEM_SPEC, VMEM_SPEC, HBM_SPEC],
        out_specs=(VMEM_SPEC, VMEM_SPEC),
        scratch_shapes=[
            pool_half,
            pltpu.VMEM((SLOTS, HEAD_SIZE), jnp.int32),
            pltpu.SMEM((SLOTS, HEAD_SIZE), jnp.int32),
            pltpu.SMEM((INSTANCES * SLOTS + 1,), jnp.int32),
            pltpu.SemaphoreType.DMA(()),
            pltpu.SemaphoreType.DMA((POOL // POOL_PIECE,)),
        ],
        compiler_params=pltpu.CompilerParams(vmem_limit_bytes=12 * 2**20),
        name="lent",
    )(got, keys, in_hbm(key_value_pool))
    back = lax.all_to_all(back, "inst", split_axis=0, concat_axis=0, tiled=True)
    home_part, home_logsum, fetched = pl.pallas_call(
        home_kernel,
        out_shape=(
            rows,
            pltpu.VMEM((REQUESTS, HEAD_SIZE), F32),
            weight_space(FETCHED),
        ),
        in_specs=[HBM_SPEC] * 6 + [VMEM_SPEC] * 2,
        out_specs=(VMEM_SPEC,) * 3,
        scratch_shapes=[
            ctx_space, entry_space, entry_space,
            pltpu.VMEM((REQUESTS, STEPS, 2, HEAD_SIZE), BF16),
            pltpu.VMEM((REQUESTS, MOST_BLOCKS, 2, BLOCK_TOKENS, HEAD_SIZE), BF16),
            pltpu.SemaphoreType.DMA((4,)),
            pltpu.SemaphoreType.DMA((REQUESTS,)),
            pltpu.SemaphoreType.DMA((CHIPS,)),
        ],
        compiler_params=pltpu.CompilerParams(vmem_limit_bytes=8 * 2**20),
        cost_estimate=pl.CostEstimate(flops=10**8, bytes_accessed=12 * 10**6, transcendentals=0),
        name="home",
    )(
        *map(in_hbm, (ctx_len, entry_blocks, entry_slot, new_kv.transpose(0, 2, 1, 3), key_value_pool, out_weight)),
        query_rows,
        token,
    )
    merged, terms, own_weight = pl.pallas_call(
        merge_kernel,
        out_shape=(
            pltpu.VMEM((ROWS, HEADS * HEAD_SIZE), F32),
            pltpu.VMEM((CHIPS, ROWS, WIDTH), BF16),
            pltpu.VMEM((CHIPS, DEPTH, WIDTH), BF16),
        ),
        in_specs=[HBM_SPEC] + [VMEM_SPEC] * 4 + [HBM_SPEC],
        out_specs=(VMEM_SPEC,) * 3,
        scratch_shapes=[
            pltpu.VMEM((REQUESTS * ROWS, HEAD_SIZE), F32),
            pltpu.SMEM((INSTANCES,), jnp.int32),
            entry_space,
            weight_space(CHIPS * DEPTH - FETCHED),
            pltpu.SemaphoreType.DMA(()),
            pltpu.SemaphoreType.DMA((CHIPS,)),
            pltpu.SemaphoreType.DMA((CHIPS,)),
        ],
        compiler_params=pltpu.CompilerParams(vmem_limit_bytes=16 * 2**20),
        name="merge",
    )(in_hbm(entry_lender), back, home_part, home_logsum, fetched, in_hbm(out_weight))
    swap = [(place, place ^ 1) for place in range(TP)]
    other = lax.ppermute(terms, "tp", swap)
    mine = pl.pallas_call(
        own_kernel,
        out_shape=pltpu.VMEM((CHIPS, ROWS, WIDTH), F32),
        in_specs=[VMEM_SPEC] * 2,
        out_specs=VMEM_SPEC,
        compiler_params=pltpu.CompilerParams(vmem_limit_bytes=16 * 2**20),
        cost_estimate=pl.CostEstimate(flops=10**8, bytes_accessed=4 * 10**6, transcendentals=0),
        name="own",
    )(merged, own_weight)
    sums = pl.pallas_call(
        pair_kernel,
        out_shape=[pltpu.VMEM((ROWS, WIDTH), F32)] + [pltpu.VMEM((ROWS, WIDTH), BF16)] * 3,
        in_specs=[VMEM_SPEC] * 2,
        out_specs=[VMEM_SPEC] * CHIPS,
        compiler_params=pltpu.CompilerParams(vmem_limit_bytes=4 * 2**20),
        name="pair",
    )(mine, other)
    arrived = []
    for ahead in (3, 2, 1):
        swap = [(place, place ^ (CORES * ahead)) for place in range(TP)]
        arrived.append(lax.ppermute(sums[ahead], "tp", swap))
    attention, projected = pl.pallas_call(
        total_kernel,
        out_shape=(
            jax.ShapeDtypeStruct((STEPS, REQUESTS, HEADS * HEAD_SIZE), BF16),
            jax.ShapeDtypeStruct((ROWS, WIDTH), BF16),
        ),
        in_specs=[VMEM_SPEC] * (CHIPS + 1),
        out_specs=(VMEM_SPEC, VMEM_SPEC),
        compiler_params=pltpu.CompilerParams(vmem_limit_bytes=4 * 2**20),
        name="total",
    )(merged, sums[0], *arrived)
    return (attention.transpose(1, 0, 2), projected.reshape(STEPS, REQUESTS, -1).transpose(1, 0, 2))


def solution(mesh):
    return jax.shard_map(
        local,
        mesh=mesh,
        in_specs=(
            P("inst", None, "tp"),
            P("inst", None, None, "tp"),
            P("inst", None, None, "tp"),
            P("inst"),
            P("inst", None),
            P("inst", None),
            P("inst", None),
            P("tp", None),
        ),
        out_specs=(P("inst", None, "tp"), P("inst", None, "tp")),
        check_vma=False,
    )
```

```python
import functools
import math

import jax
import jax.numpy as jnp
from jax import lax
from jax.experimental import pallas as pl
from jax.experimental.pallas import tpu as pltpu
from jax.sharding import PartitionSpec as P

HEAD_SIZE = 128
MOST_BLOCKS = 3
STEPS = 3
HEADS = 8
REQUESTS = 8
ENTRIES = 5
INSTANCES = 32
SLOTS = 2
BLOCK_TOKENS = 64
SPAN = MOST_BLOCKS * BLOCK_TOKENS
ROWS = STEPS * HEADS
LENT = REQUESTS * (ENTRIES - 1)
TP = 8
CORES = 2
POOL = 120
POOL_PIECE = 60
CHIPS = TP // CORES
WIDTH = 512
DEPTH = 1024
FETCHED = 2816
META = SLOTS * ROWS
MESSAGE_ROWS = META + 2
SCALE = 1.0 / math.sqrt(HEAD_SIZE)
F32 = jnp.float32
BF16 = jnp.bfloat16
VMEM_SPEC = pl.BlockSpec(memory_space=pltpu.VMEM)
HBM_SPEC = pl.BlockSpec(memory_space=pltpu.HBM)


def in_hbm(array):
    return pltpu.with_memory_space_constraint(array, pltpu.HBM)


def lanes_of(shape):
    return lax.broadcasted_iota(jnp.int32, shape, len(shape) - 1)


def by_rows(message_ref):
    return message_ref.reshape(INSTANCES, MESSAGE_ROWS, HEAD_SIZE)


def slot_rows(rank):
    return pl.ds(pl.multiple_of(rank * ROWS, ROWS), ROWS)


def rows_of(shape):
    return lax.broadcasted_iota(jnp.int32, shape, 0)


def clear_counts(count_ref):
    for index in range(INSTANCES):
        count_ref[index] = 0


def next_rank(count_ref, lender):
    rank = count_ref[lender]
    count_ref[lender] = rank + 1
    return rank


def live_of(ctx_ref, blocks_ref, request, entry, earlier):
    blocks = blocks_ref[request, entry]
    live = jnp.clip(ctx_ref[request] - BLOCK_TOKENS * earlier, 0, BLOCK_TOKENS * blocks)
    return live, earlier + blocks


def start_copies(sources, targets, sems):
    copies = [pltpu.make_async_copy(*pair, sems.at[index]) for index, pair in enumerate(zip(sources, targets))]
    for copy in copies:
        copy.start()
    return copies


def scores_of(query, keys):
    return lax.dot_general(query, keys, (((1,), (1,)), ((), ())), preferred_element_type=F32) * SCALE


def on_early_core():
    return lax.rem(lax.axis_index("tp"), CORES) == 0


def attend_home(
    ctx_ref, blocks_ref, slot_ref, fresh_ref, pool_hbm, rows_ref, part_ref, logsum_ref, pool_ref, pool_sems
):
    copies = start_copies(
        [pool_hbm.at[pl.ds(slot_ref[request, 0], MOST_BLOCKS)] for request in range(REQUESTS)],
        [pool_ref.at[request] for request in range(REQUESTS)],
        pool_sems,
    )
    token = lanes_of((ROWS, SPAN))
    place = lanes_of((ROWS, HEAD_SIZE)) - rows_of((ROWS, HEAD_SIZE))
    fresh_token = lanes_of((ROWS, STEPS))
    step_of_row = lax.broadcasted_iota(jnp.int32, (ROWS, STEPS), 0) // HEADS
    fresh_seen = fresh_token <= step_of_row
    cached, fresh, values, fresh_values = [], [], [], []
    for request in range(REQUESTS):
        live, _ = live_of(ctx_ref, blocks_ref, request, 0, 0)
        copies[request].wait()
        query = rows_ref[request]
        keys = pool_ref[request, :, 0].reshape(SPAN, HEAD_SIZE)
        values.append(pool_ref[request, :, 1].reshape(SPAN, HEAD_SIZE))
        fresh_values.append(fresh_ref[request, :, 1, :].astype(F32))
        cached.append(jnp.where(token < live, scores_of(query, keys), -1e30))
        fresh.append(jnp.where(fresh_seen, scores_of(query, fresh_ref[request, :, 0, :]), -1e30))
    for request in range(REQUESTS):
        top = jnp.maximum(
            jnp.max(cached[request], axis=1, keepdims=True), jnp.max(fresh[request], axis=1, keepdims=True)
        )
        cached_expits = jnp.exp(cached[request] - top)
        fresh_expits = jnp.exp(fresh[request] - top)
        totals = jnp.sum(cached_expits, axis=1, keepdims=True) + jnp.sum(fresh_expits, axis=1, keepdims=True)
        out = jnp.dot(cached_expits.astype(BF16), values[request], preferred_element_type=F32)
        rounded = fresh_expits.astype(BF16).astype(F32)
        for index in range(STEPS):
            out = out + rounded[:, index : index + 1] * fresh_values[request][index : index + 1, :]
        part_ref[request] = (out / totals).astype(BF16)
        logsum = jnp.broadcast_to(top + jnp.log(totals), (ROWS, HEAD_SIZE))
        logsum_ref[request : request + 1, :] = jnp.sum(jnp.where(place == 0, logsum, 0.0), axis=0, keepdims=True)


def pack_kernel(
    ctx_hbm, lender_hbm, blocks_hbm, slot_hbm, q_hbm, fresh_hbm, pool_hbm,
    send_ref, rows_ref, keys_ref, part_ref, logsum_ref,
    ctx_ref, lender_ref, blocks_ref, slot_ref, q_ref, fresh_ref, regroup, count_ref, pool_ref, sems, keys_sem, pool_sems
):
    copies = start_copies(
        (q_hbm, ctx_hbm, lender_hbm, blocks_hbm, slot_hbm, fresh_hbm),
        (q_ref, ctx_ref, lender_ref, blocks_ref, slot_ref, fresh_ref),
        sems,
    )
    all_keys = pltpu.make_async_copy(pool_hbm.at[:, 0], keys_ref, keys_sem)
    all_keys.start()
    send_ref = by_rows(send_ref)
    send_ref[:, META:, :] = jnp.zeros((INSTANCES, 2, HEAD_SIZE), BF16)
    clear_counts(count_ref)
    for copy in copies:
        copy.wait()
    for step in range(STEPS):
        for head in range(HEADS):
            tile = q_ref[step, :, head * HEAD_SIZE : (head + 1) * HEAD_SIZE].astype(F32)
            regroup[pl.ds(step * HEADS + head, REQUESTS, stride=ROWS), :] = tile
    lane = lanes_of((2, HEAD_SIZE)) - 2 * SLOTS * lax.axis_index("inst")
    first_row = rows_of((2, HEAD_SIZE)) == 0
    for request in range(REQUESTS):
        rows = regroup[request * ROWS : (request + 1) * ROWS, :].astype(BF16)
        rows_ref[request] = rows
        earlier = blocks_ref[request, 0]
        for entry in range(1, ENTRIES):
            lender = lender_ref[request, entry]
            rank = next_rank(count_ref, lender)
            live, earlier = live_of(ctx_ref, blocks_ref, request, entry, earlier)
            send_ref[lender, slot_rows(rank), :] = rows
            meta = send_ref[lender, META:, :].astype(F32)
            meta = jnp.where(first_row & (lane == 2 * rank), slot_ref[request, entry].astype(F32), meta)
            meta = jnp.where(first_row & (lane == 2 * rank + 1), live.astype(F32), meta)
            send_ref[lender, META:, :] = meta.astype(BF16)

    @pl.when(on_early_core())
    def _():
        attend_home(
            ctx_ref, blocks_ref, slot_ref, fresh_ref, pool_hbm, rows_ref, part_ref, logsum_ref, pool_ref, pool_sems
        )

    all_keys.wait()


def weight_block(weight_hbm, other_core, ahead, rows):
    place = lax.axis_index("tp")
    core = lax.rem(place + other_core, CORES)
    part = lax.bitwise_xor(place // CORES, ahead) * CORES + core
    return weight_hbm.at[rows, pl.ds(pl.multiple_of(part * WIDTH, WIDTH), WIDTH)]


def start_stack(weight_hbm, target, first, last, sems):
    sources, targets = [], []
    for ahead in range(CHIPS):
        low, high = max(first, ahead * DEPTH), min(last, (ahead + 1) * DEPTH)
        if low < high:
            sources.append(weight_block(weight_hbm, 1, ahead, pl.ds(low - ahead * DEPTH, high - low)))
            targets.append(target.at[pl.ds(low - first, high - low)])
    return start_copies(sources, targets, sems)


def home_kernel(
    ctx_hbm, blocks_hbm, slot_hbm, fresh_hbm, pool_hbm, weight_hbm, rows_ref, early_part_ref, early_logsum_ref, token_ref,
    part_ref, logsum_ref, fetched_ref,
    ctx_ref, blocks_ref, slot_ref, fresh_ref, pool_ref, sems, pool_sems, weight_sems
):
    weights = start_stack(weight_hbm, fetched_ref, 0, FETCHED, weight_sems)

    @pl.when(on_early_core())
    def _():
        part_ref[...] = early_part_ref[...]
        logsum_ref[...] = early_logsum_ref[...]

    @pl.when(jnp.logical_not(on_early_core()))
    def _():
        copies = start_copies(
            (ctx_hbm, blocks_hbm, slot_hbm, fresh_hbm), (ctx_ref, blocks_ref, slot_ref, fresh_ref), sems
        )
        for copy in copies:
            copy.wait()
        attend_home(
            ctx_ref, blocks_ref, slot_ref, fresh_ref, pool_hbm, rows_ref, part_ref, logsum_ref, pool_ref, pool_sems
        )

    for copy in weights:
        copy.wait()


def lent_kernel(
    got_ref, keys_ref, pool_hbm, back_ref, token_ref, values_ref, meta_vector, meta_ref, item_ref, sem, pool_sems
):
    pieces = [pl.ds(piece * POOL_PIECE, POOL_PIECE) for piece in range(POOL // POOL_PIECE)]
    copies = start_copies(
        [pool_hbm.at[piece, 1] for piece in pieces], [values_ref.at[piece] for piece in pieces], pool_sems
    )
    token_ref[...] = jnp.zeros_like(token_ref)
    got_ref, back_ref = by_rows(got_ref), by_rows(back_ref)
    meta_vector[...] = jnp.sum(got_ref[:, META:, :].astype(F32), axis=0).astype(jnp.int32)
    copy = pltpu.make_async_copy(meta_vector, meta_ref, sem)
    copy.start()
    back_ref[:, META:, :] = jnp.zeros((INSTANCES, 2, HEAD_SIZE), BF16)
    copy.wait()

    def compact(index, found):
        live = meta_ref[0, 2 * index + 1]
        item_ref[found] = index
        return found + (live > 0).astype(jnp.int32)

    lax.fori_loop(0, INSTANCES * SLOTS, compact, 0, unroll=INSTANCES * SLOTS)
    token = lanes_of((2 * ROWS, SPAN))
    first = rows_of((2 * ROWS, SPAN)) < ROWS
    place = lanes_of((ROWS, HEAD_SIZE)) - rows_of((ROWS, HEAD_SIZE))
    slot_row = rows_of((SLOTS, HEAD_SIZE))
    items = [item_ref[member] for member in range(LENT)]
    source = [item // SLOTS for item in items]
    rank = [item % SLOTS for item in items]
    slots = [meta_ref[0, 2 * item] for item in items]
    empty = jnp.zeros((ROWS, HEAD_SIZE), F32)

    def span_of(ref, slot):
        return ref[pl.ds(slot, MOST_BLOCKS)].reshape(SPAN, HEAD_SIZE)

    scores = []
    for left in range(0, LENT, 2):
        pair = (left, left + 1)
        queries = [got_ref[source[member], slot_rows(rank[member]), :].astype(F32) for member in pair]
        queries = jnp.concatenate(
            [jnp.concatenate([queries[0], empty], axis=1), jnp.concatenate([empty, queries[1]], axis=1)], axis=0
        )
        keys = jnp.concatenate([span_of(keys_ref, slots[member]) for member in pair], axis=1)
        live = [meta_ref[0, 2 * items[member] + 1] for member in pair]
        live = jnp.where(first, live[0], live[1])
        scores.append(jnp.where(token < live, scores_of(queries.astype(BF16), keys), -1e30))
    for copy in copies:
        copy.wait()
    parts, logsums = [], []
    for left in range(0, LENT, 2):
        values = jnp.concatenate([span_of(values_ref, slots[member]) for member in (left, left + 1)], axis=1)
        top = jnp.max(scores[left // 2], axis=1, keepdims=True)
        expits = jnp.exp(scores[left // 2] - top)
        totals = jnp.sum(expits, axis=1, keepdims=True)
        out = jnp.dot(expits.astype(BF16), values, preferred_element_type=F32)
        logsum = jnp.broadcast_to(top + jnp.log(totals), (2 * ROWS, HEAD_SIZE))
        for half in range(2):
            rows = slice(half * ROWS, (half + 1) * ROWS)
            parts.append(out[rows, half * HEAD_SIZE : (half + 1) * HEAD_SIZE] / totals[rows])
            logsums.append(logsum[rows])
    for member in range(LENT):
        back_ref[source[member], slot_rows(rank[member]), :] = parts[member].astype(BF16)
        high = logsums[member].astype(BF16).astype(F32)
        middle = (logsums[member] - high).astype(BF16).astype(F32)
        low = logsums[member] - high - middle
        spread = jnp.where(place == 0, high, 0.0)
        spread = jnp.where(place == ROWS, middle, spread)
        spread = jnp.where(place == 2 * ROWS, low, spread)
        line = jnp.sum(spread, axis=0, keepdims=True)
        block = back_ref[source[member], META:, :].astype(F32)
        back_ref[source[member], META:, :] = jnp.where(slot_row == rank[member], line, block).astype(BF16)


def merge_kernel(
    lender_hbm, back_ref, part_ref, logsum_ref, fetched_ref, weight_hbm,
    attention_ref, terms_ref, own_ref,
    merged, count_ref, lender_ref, rest_ref, sem, rest_sems, own_sems
):
    copy = pltpu.make_async_copy(lender_hbm, lender_ref, sem)
    copy.start()
    rest = start_stack(weight_hbm, rest_ref, FETCHED, CHIPS * DEPTH, rest_sems)
    own = start_copies(
        [weight_block(weight_hbm, 0, ahead, pl.ds(0, DEPTH)) for ahead in range(CHIPS)],
        [own_ref.at[ahead] for ahead in range(CHIPS)],
        own_sems,
    )
    clear_counts(count_ref)
    copy.wait()
    back_ref = by_rows(back_ref)
    place = lanes_of((ROWS, HEAD_SIZE)) - rows_of((ROWS, HEAD_SIZE))
    mine = (place == 0) | (place == ROWS) | (place == 2 * ROWS)
    slot_row = rows_of((SLOTS, HEAD_SIZE))
    for request in range(REQUESTS):
        logsum = jnp.where(place == 0, logsum_ref[request : request + 1, :], 0.0)
        logsums = [jnp.broadcast_to(jnp.sum(logsum, axis=1, keepdims=True), (ROWS, HEAD_SIZE))]
        parts = [part_ref[request].astype(F32)]
        for entry in range(1, ENTRIES):
            lender = lender_ref[request, entry]
            rank = next_rank(count_ref, lender)
            parts.append(back_ref[lender, slot_rows(rank), :].astype(F32))
            block = back_ref[lender, META:, :].astype(F32)
            line = jnp.sum(jnp.where(slot_row == rank, block, 0.0), axis=0, keepdims=True)
            logsum = jnp.sum(jnp.where(mine, line, 0.0), axis=1, keepdims=True)
            logsums.append(jnp.broadcast_to(logsum, (ROWS, HEAD_SIZE)))
        highest = functools.reduce(jnp.maximum, logsums)
        weights = [jnp.exp(logsum - highest) for logsum in logsums]
        total = functools.reduce(jnp.add, weights)
        blended = functools.reduce(jnp.add, [weight * part for weight, part in zip(weights, parts)])
        merged[request * ROWS : (request + 1) * ROWS, :] = blended / total
    for step in range(STEPS):
        for head in range(HEADS):
            tile = merged[pl.ds(step * HEADS + head, REQUESTS, stride=ROWS), :]
            attention_ref[step * REQUESTS : (step + 1) * REQUESTS, head * HEAD_SIZE : (head + 1) * HEAD_SIZE] = tile
    attention = attention_ref[...].astype(BF16)
    waiting = list(rest)
    for ahead in range(CHIPS):
        early = min(max(FETCHED - ahead * DEPTH, 0), DEPTH)
        terms = jnp.zeros((ROWS, WIDTH), F32)
        if early:
            block = fetched_ref[ahead * DEPTH : ahead * DEPTH + early, :]
            terms += jnp.dot(attention[:, :early], block, preferred_element_type=F32)
        if early < DEPTH:
            waiting.pop(0).wait()
            block = rest_ref[ahead * DEPTH + early - FETCHED : (ahead + 1) * DEPTH - FETCHED, :]
            terms += jnp.dot(attention[:, early:], block, preferred_element_type=F32)
        terms_ref[ahead] = terms.astype(BF16)
    for copy in own:
        copy.wait()


def own_kernel(attention_ref, weight_ref, terms_ref):
    attention = attention_ref[...].astype(BF16)
    for ahead in range(CHIPS):
        terms_ref[ahead] = jnp.dot(attention, weight_ref[ahead], preferred_element_type=F32)


def pair_kernel(mine_ref, other_ref, *sum_refs):
    for ahead, sum_ref in enumerate(sum_refs):
        sum_ref[...] = (mine_ref[ahead] + other_ref[ahead].astype(F32)).astype(sum_ref.dtype)


def total_kernel(merged_ref, own_ref, *refs):
    attention_ref, projected_ref = refs[-2:]
    attention_ref[...] = merged_ref[...].reshape(STEPS, REQUESTS, HEADS * HEAD_SIZE).astype(BF16)
    total = own_ref[...]
    for ref in refs[:-2]:
        total = total + ref[...].astype(F32)
    projected_ref[...] = total.astype(BF16)


def local(
    queries, new_kv, key_value_pool, ctx_len, entry_lender, entry_blocks, entry_slot, out_weight
):
    message = pltpu.VMEM((INSTANCES, MESSAGE_ROWS // 2, 2, HEAD_SIZE), BF16)
    rows = pltpu.VMEM((REQUESTS, ROWS, HEAD_SIZE), BF16)
    weight_space = lambda count: pltpu.VMEM((count, WIDTH), BF16)
    logsums = pltpu.VMEM((REQUESTS, HEAD_SIZE), F32)
    ctx_space = pltpu.SMEM((REQUESTS,), jnp.int32)
    entry_space = pltpu.SMEM((REQUESTS, ENTRIES), jnp.int32)
    pool_half = pltpu.VMEM((POOL, BLOCK_TOKENS, HEAD_SIZE), BF16)
    fresh_space = pltpu.VMEM((REQUESTS, STEPS, 2, HEAD_SIZE), BF16)
    home_space = pltpu.VMEM((REQUESTS, MOST_BLOCKS, 2, BLOCK_TOKENS, HEAD_SIZE), BF16)
    fresh = new_kv.transpose(0, 2, 1, 3)
    send, query_rows, keys, early_part, early_logsum = pl.pallas_call(
        pack_kernel,
        out_shape=(message, rows, pool_half, rows, logsums),
        in_specs=[HBM_SPEC] * 7,
        out_specs=(VMEM_SPEC,) * 5,
        scratch_shapes=[
            ctx_space, entry_space, entry_space, entry_space,
            pltpu.VMEM((STEPS, REQUESTS, HEADS * HEAD_SIZE), BF16),
            fresh_space,
            pltpu.VMEM((REQUESTS * ROWS, HEAD_SIZE), F32),
            pltpu.SMEM((INSTANCES,), jnp.int32),
            home_space,
            pltpu.SemaphoreType.DMA((6,)),
            pltpu.SemaphoreType.DMA(()),
            pltpu.SemaphoreType.DMA((REQUESTS,)),
        ],
        compiler_params=pltpu.CompilerParams(vmem_limit_bytes=8 * 2**20),
        name="pack",
    )(*map(in_hbm, (ctx_len, entry_lender, entry_blocks, entry_slot, queries.transpose(1, 0, 2), fresh, key_value_pool)))
    got = lax.all_to_all(send, "inst", split_axis=0, concat_axis=0, tiled=True)
    back, token = pl.pallas_call(
        lent_kernel,
        out_shape=(message, pltpu.VMEM((8, HEAD_SIZE), F32)),
        in_specs=[VMEM_SPEC, VMEM_SPEC, HBM_SPEC],
        out_specs=(VMEM_SPEC, VMEM_SPEC),
        scratch_shapes=[
            pool_half,
            pltpu.VMEM((SLOTS, HEAD_SIZE), jnp.int32),
            pltpu.SMEM((SLOTS, HEAD_SIZE), jnp.int32),
            pltpu.SMEM((INSTANCES * SLOTS + 1,), jnp.int32),
            pltpu.SemaphoreType.DMA(()),
            pltpu.SemaphoreType.DMA((POOL // POOL_PIECE,)),
        ],
        compiler_params=pltpu.CompilerParams(vmem_limit_bytes=12 * 2**20),
        name="lent",
    )(got, keys, in_hbm(key_value_pool))
    back = lax.all_to_all(back, "inst", split_axis=0, concat_axis=0, tiled=True)
    home_part, home_logsum, fetched = pl.pallas_call(
        home_kernel,
        out_shape=(
            rows,
            logsums,
            weight_space(FETCHED),
        ),
        in_specs=[HBM_SPEC] * 6 + [VMEM_SPEC] * 4,
        out_specs=(VMEM_SPEC,) * 3,
        scratch_shapes=[
            ctx_space, entry_space, entry_space,
            fresh_space,
            home_space,
            pltpu.SemaphoreType.DMA((4,)),
            pltpu.SemaphoreType.DMA((REQUESTS,)),
            pltpu.SemaphoreType.DMA((CHIPS,)),
        ],
        compiler_params=pltpu.CompilerParams(vmem_limit_bytes=8 * 2**20),
        cost_estimate=pl.CostEstimate(flops=10**8, bytes_accessed=12 * 10**6, transcendentals=0),
        name="home",
    )(
        *map(in_hbm, (ctx_len, entry_blocks, entry_slot, fresh, key_value_pool, out_weight)),
        query_rows,
        early_part,
        early_logsum,
        token,
    )
    merged, terms, own_weight = pl.pallas_call(
        merge_kernel,
        out_shape=(
            pltpu.VMEM((ROWS, HEADS * HEAD_SIZE), F32),
            pltpu.VMEM((CHIPS, ROWS, WIDTH), BF16),
            pltpu.VMEM((CHIPS, DEPTH, WIDTH), BF16),
        ),
        in_specs=[HBM_SPEC] + [VMEM_SPEC] * 4 + [HBM_SPEC],
        out_specs=(VMEM_SPEC,) * 3,
        scratch_shapes=[
            pltpu.VMEM((REQUESTS * ROWS, HEAD_SIZE), F32),
            pltpu.SMEM((INSTANCES,), jnp.int32),
            entry_space,
            weight_space(CHIPS * DEPTH - FETCHED),
            pltpu.SemaphoreType.DMA(()),
            pltpu.SemaphoreType.DMA((CHIPS,)),
            pltpu.SemaphoreType.DMA((CHIPS,)),
        ],
        compiler_params=pltpu.CompilerParams(vmem_limit_bytes=16 * 2**20),
        name="merge",
    )(in_hbm(entry_lender), back, home_part, home_logsum, fetched, in_hbm(out_weight))
    swap = [(place, place ^ 1) for place in range(TP)]
    other = lax.ppermute(terms, "tp", swap)
    mine = pl.pallas_call(
        own_kernel,
        out_shape=pltpu.VMEM((CHIPS, ROWS, WIDTH), F32),
        in_specs=[VMEM_SPEC] * 2,
        out_specs=VMEM_SPEC,
        compiler_params=pltpu.CompilerParams(vmem_limit_bytes=16 * 2**20),
        cost_estimate=pl.CostEstimate(flops=10**8, bytes_accessed=4 * 10**6, transcendentals=0),
        name="own",
    )(merged, own_weight)
    sums = pl.pallas_call(
        pair_kernel,
        out_shape=[pltpu.VMEM((ROWS, WIDTH), F32)] + [pltpu.VMEM((ROWS, WIDTH), BF16)] * 3,
        in_specs=[VMEM_SPEC] * 2,
        out_specs=[VMEM_SPEC] * CHIPS,
        compiler_params=pltpu.CompilerParams(vmem_limit_bytes=4 * 2**20),
        name="pair",
    )(mine, other)
    arrived = []
    for ahead in (3, 2, 1):
        swap = [(place, place ^ (CORES * ahead)) for place in range(TP)]
        arrived.append(lax.ppermute(sums[ahead], "tp", swap))
    attention, projected = pl.pallas_call(
        total_kernel,
        out_shape=(
            jax.ShapeDtypeStruct((STEPS, REQUESTS, HEADS * HEAD_SIZE), BF16),
            jax.ShapeDtypeStruct((ROWS, WIDTH), BF16),
        ),
        in_specs=[VMEM_SPEC] * (CHIPS + 1),
        out_specs=(VMEM_SPEC, VMEM_SPEC),
        compiler_params=pltpu.CompilerParams(vmem_limit_bytes=4 * 2**20),
        name="total",
    )(merged, sums[0], *arrived)
    return (attention.transpose(1, 0, 2), projected.reshape(STEPS, REQUESTS, -1).transpose(1, 0, 2))


def solution(mesh):
    return jax.shard_map(
        local,
        mesh=mesh,
        in_specs=(
            P("inst", None, "tp"),
            P("inst", None, None, "tp"),
            P("inst", None, None, "tp"),
            P("inst"),
            P("inst", None),
            P("inst", None),
            P("inst", None),
            P("tp", None),
        ),
        out_specs=(P("inst", None, "tp"), P("inst", None, "tp")),
        check_vma=False,
    )
```

```python
import functools
import math

import jax
import jax.numpy as jnp
from jax import lax
from jax.experimental import pallas as pl
from jax.experimental.pallas import tpu as pltpu
from jax.sharding import PartitionSpec as P

HEAD_SIZE = 128
MOST_BLOCKS = 3
STEPS = 3
HEADS = 8
REQUESTS = 8
ENTRIES = 5
INSTANCES = 32
SLOTS = 2
BLOCK_TOKENS = 64
SPAN = MOST_BLOCKS * BLOCK_TOKENS
ROWS = STEPS * HEADS
LENT = REQUESTS * (ENTRIES - 1)
TP = 8
CORES = 2
POOL = 120
POOL_PIECE = 60
CHIPS = TP // CORES
WIDTH = 512
DEPTH = 1024
FETCHED = 2816
META = SLOTS * ROWS
MESSAGE_ROWS = META + 2
SCALE = 1.0 / math.sqrt(HEAD_SIZE)
LARGEST = 3e38
F32 = jnp.float32
BF16 = jnp.bfloat16
VMEM_SPEC = pl.BlockSpec(memory_space=pltpu.VMEM)
HBM_SPEC = pl.BlockSpec(memory_space=pltpu.HBM)


def in_hbm(array):
    return pltpu.with_memory_space_constraint(array, pltpu.HBM)


def lanes_of(shape):
    return lax.broadcasted_iota(jnp.int32, shape, len(shape) - 1)


def by_rows(message_ref):
    return message_ref.reshape(INSTANCES, MESSAGE_ROWS, HEAD_SIZE)


def slot_rows(rank):
    return pl.ds(pl.multiple_of(rank * ROWS, ROWS), ROWS)


def rows_of(shape):
    return lax.broadcasted_iota(jnp.int32, shape, 0)


def clear_counts(count_ref):
    for index in range(INSTANCES):
        count_ref[index] = 0


def next_rank(count_ref, lender):
    rank = count_ref[lender]
    count_ref[lender] = rank + 1
    return rank


def live_of(ctx_ref, blocks_ref, request, entry, earlier):
    blocks = blocks_ref[request, entry]
    live = jnp.clip(ctx_ref[request] - BLOCK_TOKENS * earlier, 0, BLOCK_TOKENS * blocks)
    return live, earlier + blocks


def start_copies(sources, targets, sems):
    copies = [pltpu.make_async_copy(*pair, sems.at[index]) for index, pair in enumerate(zip(sources, targets))]
    for copy in copies:
        copy.start()
    return copies


def scores_of(query, keys):
    return lax.dot_general(query, keys, (((1,), (1,)), ((), ())), preferred_element_type=F32) * SCALE


def on_early_core():
    return lax.rem(lax.axis_index("tp"), CORES) == 0


def attend_home(
    ctx_ref, blocks_ref, slot_ref, fresh_ref, pool_hbm, rows_ref, part_ref, logsum_ref, pool_ref, pool_sems
):
    copies = start_copies(
        [pool_hbm.at[pl.ds(slot_ref[request, 0], MOST_BLOCKS)] for request in range(REQUESTS)],
        [pool_ref.at[request] for request in range(REQUESTS)],
        pool_sems,
    )
    token = lanes_of((ROWS, SPAN))
    place = lanes_of((ROWS, HEAD_SIZE)) - rows_of((ROWS, HEAD_SIZE))
    fresh_token = lanes_of((ROWS, STEPS))
    step_of_row = lax.broadcasted_iota(jnp.int32, (ROWS, STEPS), 0) // HEADS
    fresh_seen = fresh_token <= step_of_row
    cached, fresh, values, fresh_values = [], [], [], []
    for request in range(REQUESTS):
        live, _ = live_of(ctx_ref, blocks_ref, request, 0, 0)
        copies[request].wait()
        query = rows_ref[request]
        keys = pool_ref[request, :, 0].reshape(SPAN, HEAD_SIZE)
        values.append(pool_ref[request, :, 1].reshape(SPAN, HEAD_SIZE))
        fresh_values.append(fresh_ref[request, :, 1, :].astype(F32))
        cached.append(jnp.where(token < live, scores_of(query, keys), -1e30))
        fresh.append(jnp.where(fresh_seen, scores_of(query, fresh_ref[request, :, 0, :]), -1e30))
    for request in range(REQUESTS):
        top = jnp.maximum(
            jnp.max(cached[request], axis=1, keepdims=True), jnp.max(fresh[request], axis=1, keepdims=True)
        )
        cached_expits = jnp.exp(cached[request] - top)
        fresh_expits = jnp.exp(fresh[request] - top)
        totals = jnp.sum(cached_expits, axis=1, keepdims=True) + jnp.sum(fresh_expits, axis=1, keepdims=True)
        out = jnp.dot(cached_expits.astype(BF16), values[request], preferred_element_type=F32)
        rounded = fresh_expits.astype(BF16).astype(F32)
        for index in range(STEPS):
            out = out + rounded[:, index : index + 1] * fresh_values[request][index : index + 1, :]
        part_ref[request] = (out / totals).astype(BF16)
        logsum = jnp.broadcast_to(top + jnp.log(totals), (ROWS, HEAD_SIZE))
        logsum_ref[request : request + 1, :] = jnp.sum(jnp.where(place == 0, logsum, 0.0), axis=0, keepdims=True)


def pack_kernel(
    ctx_hbm, lender_hbm, blocks_hbm, slot_hbm, q_hbm, fresh_hbm, pool_hbm,
    send_ref, rows_ref, keys_ref, part_ref, logsum_ref,
    ctx_ref, lender_ref, blocks_ref, slot_ref, q_ref, fresh_ref, regroup, count_ref, pool_ref, sems, keys_sem, pool_sems
):
    copies = start_copies(
        (q_hbm, ctx_hbm, lender_hbm, blocks_hbm, slot_hbm, fresh_hbm),
        (q_ref, ctx_ref, lender_ref, blocks_ref, slot_ref, fresh_ref),
        sems,
    )
    all_keys = pltpu.make_async_copy(pool_hbm.at[:, 0], keys_ref, keys_sem)
    all_keys.start()
    send_ref = by_rows(send_ref)
    send_ref[:, META:, :] = jnp.zeros((INSTANCES, 2, HEAD_SIZE), BF16)
    clear_counts(count_ref)
    for copy in copies:
        copy.wait()
    for step in range(STEPS):
        for head in range(HEADS):
            tile = q_ref[step, :, head * HEAD_SIZE : (head + 1) * HEAD_SIZE].astype(F32)
            regroup[pl.ds(step * HEADS + head, REQUESTS, stride=ROWS), :] = tile
    lane = lanes_of((2, HEAD_SIZE)) - 2 * SLOTS * lax.axis_index("inst")
    first_row = rows_of((2, HEAD_SIZE)) == 0
    for request in range(REQUESTS):
        rows = regroup[request * ROWS : (request + 1) * ROWS, :].astype(BF16)
        rows_ref[request] = rows
        earlier = blocks_ref[request, 0]
        for entry in range(1, ENTRIES):
            lender = lender_ref[request, entry]
            rank = next_rank(count_ref, lender)
            live, earlier = live_of(ctx_ref, blocks_ref, request, entry, earlier)
            send_ref[lender, slot_rows(rank), :] = rows
            meta = send_ref[lender, META:, :].astype(F32)
            meta = jnp.where(first_row & (lane == 2 * rank), slot_ref[request, entry].astype(F32), meta)
            meta = jnp.where(first_row & (lane == 2 * rank + 1), live.astype(F32), meta)
            send_ref[lender, META:, :] = meta.astype(BF16)

    @pl.when(on_early_core())
    def _():
        attend_home(
            ctx_ref, blocks_ref, slot_ref, fresh_ref, pool_hbm, rows_ref, part_ref, logsum_ref, pool_ref, pool_sems
        )

    all_keys.wait()


def weight_block(weight_hbm, other_core, ahead, rows):
    place = lax.axis_index("tp")
    core = lax.rem(place + other_core, CORES)
    part = lax.bitwise_xor(place // CORES, ahead) * CORES + core
    return weight_hbm.at[rows, pl.ds(pl.multiple_of(part * WIDTH, WIDTH), WIDTH)]


def start_stack(weight_hbm, target, first, last, sems):
    sources, targets = [], []
    for ahead in range(CHIPS):
        low, high = max(first, ahead * DEPTH), min(last, (ahead + 1) * DEPTH)
        if low < high:
            sources.append(weight_block(weight_hbm, 1, ahead, pl.ds(low - ahead * DEPTH, high - low)))
            targets.append(target.at[pl.ds(low - first, high - low)])
    return start_copies(sources, targets, sems)


def home_kernel(
    ctx_hbm, blocks_hbm, slot_hbm, fresh_hbm, pool_hbm, weight_hbm, rows_ref, early_part_ref, early_logsum_ref, token_ref,
    part_ref, logsum_ref, fetched_ref,
    ctx_ref, blocks_ref, slot_ref, fresh_ref, pool_ref, sems, pool_sems, weight_sems
):
    weights = start_stack(weight_hbm, fetched_ref, 0, FETCHED, weight_sems)

    @pl.when(on_early_core())
    def _():
        part_ref[...] = early_part_ref[...]
        logsum_ref[...] = early_logsum_ref[...]

    @pl.when(jnp.logical_not(on_early_core()))
    def _():
        copies = start_copies(
            (ctx_hbm, blocks_hbm, slot_hbm, fresh_hbm), (ctx_ref, blocks_ref, slot_ref, fresh_ref), sems
        )
        for copy in copies:
            copy.wait()
        attend_home(
            ctx_ref, blocks_ref, slot_ref, fresh_ref, pool_hbm, rows_ref, part_ref, logsum_ref, pool_ref, pool_sems
        )

    for copy in weights:
        copy.wait()


def lent_kernel(
    got_ref, keys_ref, pool_hbm, back_ref, token_ref, values_ref, meta_vector, meta_ref, item_ref, sem, pool_sems
):
    pieces = [pl.ds(piece * POOL_PIECE, POOL_PIECE) for piece in range(POOL // POOL_PIECE)]
    copies = start_copies(
        [pool_hbm.at[piece, 1] for piece in pieces], [values_ref.at[piece] for piece in pieces], pool_sems
    )
    token_ref[...] = jnp.zeros_like(token_ref)
    got_ref, back_ref = by_rows(got_ref), by_rows(back_ref)
    meta_vector[...] = jnp.sum(got_ref[:, META:, :].astype(F32), axis=0).astype(jnp.int32)
    copy = pltpu.make_async_copy(meta_vector, meta_ref, sem)
    copy.start()
    back_ref[:, META:, :] = jnp.zeros((INSTANCES, 2, HEAD_SIZE), BF16)
    copy.wait()

    def compact(index, found):
        live = meta_ref[0, 2 * index + 1]
        item_ref[found] = index
        return found + (live > 0).astype(jnp.int32)

    lax.fori_loop(0, INSTANCES * SLOTS, compact, 0, unroll=INSTANCES * SLOTS)
    token = lanes_of((2 * ROWS, SPAN))
    first = rows_of((2 * ROWS, SPAN)) < ROWS
    place = lanes_of((ROWS, HEAD_SIZE)) - rows_of((ROWS, HEAD_SIZE))
    slot_row = rows_of((SLOTS, HEAD_SIZE))
    items = [item_ref[member] for member in range(LENT)]
    source = [item // SLOTS for item in items]
    rank = [item % SLOTS for item in items]
    slots = [meta_ref[0, 2 * item] for item in items]
    empty = jnp.zeros((ROWS, HEAD_SIZE), F32)

    def span_of(ref, slot):
        return ref[pl.ds(slot, MOST_BLOCKS)].reshape(SPAN, HEAD_SIZE)

    scores = []
    for left in range(0, LENT, 2):
        pair = (left, left + 1)
        queries = [got_ref[source[member], slot_rows(rank[member]), :].astype(F32) for member in pair]
        queries = jnp.concatenate(
            [jnp.concatenate([queries[0], empty], axis=1), jnp.concatenate([empty, queries[1]], axis=1)], axis=0
        )
        keys = jnp.concatenate([span_of(keys_ref, slots[member]) for member in pair], axis=1)
        live = [meta_ref[0, 2 * items[member] + 1] for member in pair]
        live = jnp.where(first, live[0], live[1])
        scores.append(jnp.where(token < live, scores_of(queries.astype(BF16), keys), -1e30))
    for copy in copies:
        copy.wait()
    parts, logsums = [], []
    for left in range(0, LENT, 2):
        values = jnp.concatenate([span_of(values_ref, slots[member]) for member in (left, left + 1)], axis=1)
        top = jnp.max(scores[left // 2], axis=1, keepdims=True)
        expits = jnp.exp(scores[left // 2] - top)
        totals = jnp.sum(expits, axis=1, keepdims=True)
        out = jnp.dot(expits.astype(BF16), values, preferred_element_type=F32)
        logsum = jnp.broadcast_to(top + jnp.log(totals), (2 * ROWS, HEAD_SIZE))
        for half in range(2):
            rows = slice(half * ROWS, (half + 1) * ROWS)
            parts.append(out[rows, half * HEAD_SIZE : (half + 1) * HEAD_SIZE] / totals[rows])
            logsums.append(logsum[rows])
    for member in range(LENT):
        back_ref[source[member], slot_rows(rank[member]), :] = parts[member].astype(BF16)
        high = jnp.clip(logsums[member], -LARGEST, LARGEST).astype(BF16).astype(F32)
        middle = (logsums[member] - high).astype(BF16).astype(F32)
        low = logsums[member] - high - middle
        spread = jnp.where(place == 0, high, 0.0)
        spread = jnp.where(place == ROWS, middle, spread)
        spread = jnp.where(place == 2 * ROWS, low, spread)
        line = jnp.sum(spread, axis=0, keepdims=True)
        block = back_ref[source[member], META:, :].astype(F32)
        back_ref[source[member], META:, :] = jnp.where(slot_row == rank[member], line, block).astype(BF16)


def merge_kernel(
    lender_hbm, back_ref, part_ref, logsum_ref, fetched_ref, weight_hbm,
    attention_ref, terms_ref, own_ref,
    merged, count_ref, lender_ref, rest_ref, sem, rest_sems, own_sems
):
    copy = pltpu.make_async_copy(lender_hbm, lender_ref, sem)
    copy.start()
    rest = start_stack(weight_hbm, rest_ref, FETCHED, CHIPS * DEPTH, rest_sems)
    own = start_copies(
        [weight_block(weight_hbm, 0, ahead, pl.ds(0, DEPTH)) for ahead in range(CHIPS)],
        [own_ref.at[ahead] for ahead in range(CHIPS)],
        own_sems,
    )
    clear_counts(count_ref)
    copy.wait()
    back_ref = by_rows(back_ref)
    place = lanes_of((ROWS, HEAD_SIZE)) - rows_of((ROWS, HEAD_SIZE))
    mine = (place == 0) | (place == ROWS) | (place == 2 * ROWS)
    slot_row = rows_of((SLOTS, HEAD_SIZE))
    for request in range(REQUESTS):
        logsum = jnp.where(place == 0, logsum_ref[request : request + 1, :], 0.0)
        logsums = [jnp.broadcast_to(jnp.sum(logsum, axis=1, keepdims=True), (ROWS, HEAD_SIZE))]
        parts = [part_ref[request].astype(F32)]
        for entry in range(1, ENTRIES):
            lender = lender_ref[request, entry]
            rank = next_rank(count_ref, lender)
            parts.append(back_ref[lender, slot_rows(rank), :].astype(F32))
            block = back_ref[lender, META:, :].astype(F32)
            line = jnp.sum(jnp.where(slot_row == rank, block, 0.0), axis=0, keepdims=True)
            logsum = jnp.sum(jnp.where(mine, line, 0.0), axis=1, keepdims=True)
            logsums.append(jnp.broadcast_to(logsum, (ROWS, HEAD_SIZE)))
        highest = functools.reduce(jnp.maximum, logsums)
        weights = [jnp.exp(logsum - highest) for logsum in logsums]
        total = functools.reduce(jnp.add, weights)
        blended = functools.reduce(jnp.add, [weight * part for weight, part in zip(weights, parts)])
        merged[request * ROWS : (request + 1) * ROWS, :] = blended / total
    for step in range(STEPS):
        for head in range(HEADS):
            tile = merged[pl.ds(step * HEADS + head, REQUESTS, stride=ROWS), :]
            attention_ref[step * REQUESTS : (step + 1) * REQUESTS, head * HEAD_SIZE : (head + 1) * HEAD_SIZE] = tile
    attention = attention_ref[...].astype(BF16)
    waiting = list(rest)
    for ahead in range(CHIPS):
        early = min(max(FETCHED - ahead * DEPTH, 0), DEPTH)
        terms = jnp.zeros((ROWS, WIDTH), F32)
        if early:
            block = fetched_ref[ahead * DEPTH : ahead * DEPTH + early, :]
            terms += jnp.dot(attention[:, :early], block, preferred_element_type=F32)
        if early < DEPTH:
            waiting.pop(0).wait()
            block = rest_ref[ahead * DEPTH + early - FETCHED : (ahead + 1) * DEPTH - FETCHED, :]
            terms += jnp.dot(attention[:, early:], block, preferred_element_type=F32)
        terms_ref[ahead] = terms.astype(BF16)
    for copy in own:
        copy.wait()


def own_kernel(attention_ref, weight_ref, terms_ref):
    attention = attention_ref[...].astype(BF16)
    for ahead in range(CHIPS):
        terms_ref[ahead] = jnp.dot(attention, weight_ref[ahead], preferred_element_type=F32)


def pair_kernel(mine_ref, other_ref, *sum_refs):
    for ahead, sum_ref in enumerate(sum_refs):
        sum_ref[...] = (mine_ref[ahead] + other_ref[ahead].astype(F32)).astype(sum_ref.dtype)


def total_kernel(merged_ref, own_ref, *refs):
    attention_ref, projected_ref = refs[-2:]
    attention_ref[...] = merged_ref[...].reshape(STEPS, REQUESTS, HEADS * HEAD_SIZE).astype(BF16)
    total = own_ref[...]
    for ref in refs[:-2]:
        total = total + ref[...].astype(F32)
    projected_ref[...] = total.astype(BF16)


def local(
    queries, new_kv, key_value_pool, ctx_len, entry_lender, entry_blocks, entry_slot, out_weight
):
    message = pltpu.VMEM((INSTANCES, MESSAGE_ROWS // 2, 2, HEAD_SIZE), BF16)
    rows = pltpu.VMEM((REQUESTS, ROWS, HEAD_SIZE), BF16)
    weight_space = lambda count: pltpu.VMEM((count, WIDTH), BF16)
    logsums = pltpu.VMEM((REQUESTS, HEAD_SIZE), F32)
    ctx_space = pltpu.SMEM((REQUESTS,), jnp.int32)
    entry_space = pltpu.SMEM((REQUESTS, ENTRIES), jnp.int32)
    pool_half = pltpu.VMEM((POOL, BLOCK_TOKENS, HEAD_SIZE), BF16)
    fresh_space = pltpu.VMEM((REQUESTS, STEPS, 2, HEAD_SIZE), BF16)
    home_space = pltpu.VMEM((REQUESTS, MOST_BLOCKS, 2, BLOCK_TOKENS, HEAD_SIZE), BF16)
    fresh = new_kv.transpose(0, 2, 1, 3)
    send, query_rows, keys, early_part, early_logsum = pl.pallas_call(
        pack_kernel,
        out_shape=(message, rows, pool_half, rows, logsums),
        in_specs=[HBM_SPEC] * 7,
        out_specs=(VMEM_SPEC,) * 5,
        scratch_shapes=[
            ctx_space, entry_space, entry_space, entry_space,
            pltpu.VMEM((STEPS, REQUESTS, HEADS * HEAD_SIZE), BF16),
            fresh_space,
            pltpu.VMEM((REQUESTS * ROWS, HEAD_SIZE), F32),
            pltpu.SMEM((INSTANCES,), jnp.int32),
            home_space,
            pltpu.SemaphoreType.DMA((6,)),
            pltpu.SemaphoreType.DMA(()),
            pltpu.SemaphoreType.DMA((REQUESTS,)),
        ],
        compiler_params=pltpu.CompilerParams(vmem_limit_bytes=8 * 2**20),
        name="pack",
    )(*map(in_hbm, (ctx_len, entry_lender, entry_blocks, entry_slot, queries.transpose(1, 0, 2), fresh, key_value_pool)))
    got = lax.all_to_all(send, "inst", split_axis=0, concat_axis=0, tiled=True)
    back, token = pl.pallas_call(
        lent_kernel,
        out_shape=(message, pltpu.VMEM((8, HEAD_SIZE), F32)),
        in_specs=[VMEM_SPEC, VMEM_SPEC, HBM_SPEC],
        out_specs=(VMEM_SPEC, VMEM_SPEC),
        scratch_shapes=[
            pool_half,
            pltpu.VMEM((SLOTS, HEAD_SIZE), jnp.int32),
            pltpu.SMEM((SLOTS, HEAD_SIZE), jnp.int32),
            pltpu.SMEM((INSTANCES * SLOTS + 1,), jnp.int32),
            pltpu.SemaphoreType.DMA(()),
            pltpu.SemaphoreType.DMA((POOL // POOL_PIECE,)),
        ],
        compiler_params=pltpu.CompilerParams(vmem_limit_bytes=12 * 2**20),
        name="lent",
    )(got, keys, in_hbm(key_value_pool))
    back = lax.all_to_all(back, "inst", split_axis=0, concat_axis=0, tiled=True)
    home_part, home_logsum, fetched = pl.pallas_call(
        home_kernel,
        out_shape=(
            rows,
            logsums,
            weight_space(FETCHED),
        ),
        in_specs=[HBM_SPEC] * 6 + [VMEM_SPEC] * 4,
        out_specs=(VMEM_SPEC,) * 3,
        scratch_shapes=[
            ctx_space, entry_space, entry_space,
            fresh_space,
            home_space,
            pltpu.SemaphoreType.DMA((4,)),
            pltpu.SemaphoreType.DMA((REQUESTS,)),
            pltpu.SemaphoreType.DMA((CHIPS,)),
        ],
        compiler_params=pltpu.CompilerParams(vmem_limit_bytes=8 * 2**20),
        cost_estimate=pl.CostEstimate(flops=10**8, bytes_accessed=12 * 10**6, transcendentals=0),
        name="home",
    )(
        *map(in_hbm, (ctx_len, entry_blocks, entry_slot, fresh, key_value_pool, out_weight)),
        query_rows,
        early_part,
        early_logsum,
        token,
    )
    merged, terms, own_weight = pl.pallas_call(
        merge_kernel,
        out_shape=(
            pltpu.VMEM((ROWS, HEADS * HEAD_SIZE), F32),
            pltpu.VMEM((CHIPS, ROWS, WIDTH), BF16),
            pltpu.VMEM((CHIPS, DEPTH, WIDTH), BF16),
        ),
        in_specs=[HBM_SPEC] + [VMEM_SPEC] * 4 + [HBM_SPEC],
        out_specs=(VMEM_SPEC,) * 3,
        scratch_shapes=[
            pltpu.VMEM((REQUESTS * ROWS, HEAD_SIZE), F32),
            pltpu.SMEM((INSTANCES,), jnp.int32),
            entry_space,
            weight_space(CHIPS * DEPTH - FETCHED),
            pltpu.SemaphoreType.DMA(()),
            pltpu.SemaphoreType.DMA((CHIPS,)),
            pltpu.SemaphoreType.DMA((CHIPS,)),
        ],
        compiler_params=pltpu.CompilerParams(vmem_limit_bytes=16 * 2**20),
        name="merge",
    )(in_hbm(entry_lender), back, home_part, home_logsum, fetched, in_hbm(out_weight))
    swap = [(place, place ^ 1) for place in range(TP)]
    other = lax.ppermute(terms, "tp", swap)
    mine = pl.pallas_call(
        own_kernel,
        out_shape=pltpu.VMEM((CHIPS, ROWS, WIDTH), F32),
        in_specs=[VMEM_SPEC] * 2,
        out_specs=VMEM_SPEC,
        compiler_params=pltpu.CompilerParams(vmem_limit_bytes=16 * 2**20),
        cost_estimate=pl.CostEstimate(flops=10**8, bytes_accessed=4 * 10**6, transcendentals=0),
        name="own",
    )(merged, own_weight)
    sums = pl.pallas_call(
        pair_kernel,
        out_shape=[pltpu.VMEM((ROWS, WIDTH), F32)] + [pltpu.VMEM((ROWS, WIDTH), BF16)] * 3,
        in_specs=[VMEM_SPEC] * 2,
        out_specs=[VMEM_SPEC] * CHIPS,
        compiler_params=pltpu.CompilerParams(vmem_limit_bytes=4 * 2**20),
        name="pair",
    )(mine, other)
    arrived = []
    for ahead in (3, 2, 1):
        swap = [(place, place ^ (CORES * ahead)) for place in range(TP)]
        arrived.append(lax.ppermute(sums[ahead], "tp", swap))
    attention, projected = pl.pallas_call(
        total_kernel,
        out_shape=(
            jax.ShapeDtypeStruct((STEPS, REQUESTS, HEADS * HEAD_SIZE), BF16),
            jax.ShapeDtypeStruct((ROWS, WIDTH), BF16),
        ),
        in_specs=[VMEM_SPEC] * (CHIPS + 1),
        out_specs=(VMEM_SPEC, VMEM_SPEC),
        compiler_params=pltpu.CompilerParams(vmem_limit_bytes=4 * 2**20),
        name="total",
    )(merged, sums[0], *arrived)
    return (attention.transpose(1, 0, 2), projected.reshape(STEPS, REQUESTS, -1).transpose(1, 0, 2))


def solution(mesh):
    return jax.shard_map(
        local,
        mesh=mesh,
        in_specs=(
            P("inst", None, "tp"),
            P("inst", None, None, "tp"),
            P("inst", None, None, "tp"),
            P("inst"),
            P("inst", None),
            P("inst", None),
            P("inst", None),
            P("tp", None),
        ),
        out_specs=(P("inst", None, "tp"), P("inst", None, "tp")),
        check_vma=False,
    )
```
